32 devices in a mesh: ctx: 16 (over z, x, core), dp: 2 (over y).
Axes of the slice: x: 2, y: 2, z: 4, core: 2. Of those that a mesh axis runs over, the one named last changes fastest.
Arguments:
- tokens: bfloat16 [4, 1024, 768], P('dp', 'ctx'), may hold values from -6 to 6
- cotangent: bfloat16 [4, 1024, 768], P('dp', 'ctx'), may hold values from -6 to 6
- block_order: int32 [32], replicated, may hold values from 0 to 31, each once
- input_weight: float32 [2, 768, 2304], P('dp', None, 'ctx'), may hold values from -0.3125 to 0.3125
- output_weight: float32 [2, 768, 768], P('dp', None, 'ctx'), may hold values from -0.4375 to 0.4375
- expand_weight: float32 [2, 768, 3072], P('dp', None, 'ctx'), may hold values from -0.21875 to 0.21875
- reduce_weight: float32 [2, 3072, 768], P('dp', 'ctx'), may hold values from -0.109375 to 0.109375
- vectors: float32 [2, 9216], P('dp', 'ctx'), may hold values from -0.8 to 1.6, as said below
- input_moment: float32 [2, 768, 2304], P('dp', None, 'ctx'), may hold values from -80 to 80
- output_moment: float32 [2, 768, 768], P('dp', None, 'ctx'), may hold values from -96 to 96
- expand_moment: float32 [2, 768, 3072], P('dp', None, 'ctx'), may hold values from -192 to 192
- reduce_moment: float32 [2, 3072, 768], P('dp', 'ctx'), may hold values from -192 to 192
- vector_first: float32 [2, 9216], P('dp', 'ctx'), may hold values from -112 to 112
- vector_second: float32 [2, 9216], P('dp', 'ctx'), may hold values from 53.248 to 217.088
Outputs:
- block_output: float32 [4, 1024, 768], P('dp', 'ctx')
- input_grad: float32 [4, 1024, 768], P('dp', 'ctx')
- new_input_weight: float32 [2, 768, 2304], P('dp', None, 'ctx')
- new_output_weight: float32 [2, 768, 768], P('dp', None, 'ctx')
- new_expand_weight: float32 [2, 768, 3072], P('dp', None, 'ctx')
- new_reduce_weight: float32 [2, 3072, 768], P('dp', 'ctx')
- new_input_moment: float32 [2, 768, 2304], P('dp', None, 'ctx')
- new_output_moment: float32 [2, 768, 768], P('dp', None, 'ctx')
- new_expand_moment: float32 [2, 768, 3072], P('dp', None, 'ctx')
- new_reduce_moment: float32 [2, 3072, 768], P('dp', 'ctx')
- new_vectors: float32 [2, 9216], P('dp', 'ctx')
- new_vector_first: float32 [2, 9216], P('dp', 'ctx')
- new_vector_second: float32 [2, 9216], P('dp', 'ctx')
The draws below stay inside these ranges and needn't reach their ends.
Inputs may be any that keep to these rules, and one draw needn't show every extreme that they name: Stored block j of every sequence holds the 32 positions from block_order[j] * 32 on; each of the 32 blocks once. `vectors`: in each layer entries 0 to 767 and 3840 to 4607 are norm gains, the others biases.
All inputs are finite; a program needn't handle non-finite values.
Results may differ from the reference program's by a relative error of at most 0.023.
Values may be sent and summed in bfloat16 or wider, within the bound.
No kernel may reach another device: no remote copies, remote signals or barrier semaphores. Data moves between devices by JAX's collectives and lax.ppermute only.
A program may use at most 320 MiB of HBM per device.

```python
import math
import jax
import jax.numpy as jnp
from jax import lax

D = 768
FF = 3072
HEADS = 12
HD = 64
BLK = 32
NS_STEPS = 5
STEP = 10
LAYERS = 2
NBLK = 32
SEQ_LEN = 1024
SEQS = 4
VEC = 9216


def draw_vectors(key, part):
    key = jax.random.fold_in(key, 7)
    base = jnp.clip(jax.random.normal(key, (LAYERS, VEC), jnp.float32), -4.0, 4.0)
    segment = jnp.arange(VEC, dtype=jnp.int32) // D
    gains = (segment == 0) | (segment == 5)
    return jnp.where(gains[None, :], 1.0 + 0.15 * base, 0.2 * base).astype(jnp.float32)


def shard_levels(stream_key, shape, cuts, least, high):
    level, own = 1.0, jax.random.fold_in(stream_key, 6)
    for dim, shards_of in cuts:
        steps = jnp.exp(jax.random.uniform(jax.random.fold_in(own, dim), (shards_of,), jnp.float32, least / len(cuts), high / len(cuts)))
        level = level * jnp.repeat(steps, shape[dim] // shards_of).reshape([-1 if axis == dim else 1 for axis in range(len(shape))])
    return level


def normal_values(stream_key, extent, deviation, reach, cuts=(), held_as=jnp.bfloat16):
    loudness = shard_levels(stream_key, extent, cuts, -0.22, 0.18) if cuts else 1.0
    drawn = jax.random.normal(stream_key, extent, jnp.float32) * deviation * loudness
    return jnp.minimum(jnp.maximum(drawn, -reach), reach).astype(held_as)


def setup_inputs(seed: int = 0) -> dict:
    seeds = jax.random.split(jax.random.key(seed), 15)
    tokens = normal_values(seeds[0], (SEQS, SEQ_LEN, D), 1.0, 6.0, ((0, 2), (1, 16)))
    cotangent = normal_values(seeds[1], (SEQS, SEQ_LEN, D), 1.0, 6.0, ((0, 2), (1, 16)))
    block_order = jax.random.permutation(seeds[2], NBLK).astype(jnp.int32)
    input_weight = normal_values(seeds[3], (LAYERS, D, 3 * D), (D // 2) ** -0.5, 0.3125, ((0, 2), (2, 16)), jnp.float32)
    output_weight = normal_values(seeds[4], (LAYERS, D, D), (D // 4) ** -0.5, 0.4375, ((0, 2), (2, 16)), jnp.float32)
    expand_weight = normal_values(seeds[5], (LAYERS, D, FF), D ** -0.5, 0.21875, ((0, 2), (2, 16)), jnp.float32)
    reduce_weight = normal_values(seeds[6], (LAYERS, FF, D), FF ** -0.5, 0.109375, ((0, 2), (1, 16)), jnp.float32)
    vectors = draw_vectors(jax.random.fold_in(seeds[14], 71), 0)
    input_moment = normal_values(seeds[8], (LAYERS, D, 3 * D), (0.2 * (SEQS * SEQ_LEN) ** 0.5), 80.0, ((0, 2), (2, 16)), jnp.float32)
    output_moment = normal_values(seeds[9], (LAYERS, D, D), (0.25 * (SEQS * SEQ_LEN) ** 0.5), 96.0, ((0, 2), (2, 16)), jnp.float32)
    expand_moment = normal_values(seeds[10], (LAYERS, D, FF), (0.5 * (SEQS * SEQ_LEN) ** 0.5), 192.0, ((0, 2), (2, 16)), jnp.float32)
    reduce_moment = normal_values(seeds[11], (LAYERS, FF, D), (0.5 * (SEQS * SEQ_LEN) ** 0.5), 192.0, ((0, 2), (1, 16)), jnp.float32)
    vector_first = normal_values(seeds[12], (LAYERS, VEC), (0.3 * (SEQS * SEQ_LEN) ** 0.5), 112.0, ((0, 2), (1, 16)), jnp.float32)
    vector_second = jnp.clip(jnp.exp(math.log(217.088) - 1.40534252 * jax.random.uniform(seeds[13], (LAYERS, VEC), jnp.float32) ** shard_levels(seeds[13], (LAYERS, VEC), ((0, 2), (1, 16)), -0.2, 0.2)), 53.248, 217.088)
    return {"tokens": tokens, "cotangent": cotangent, "block_order": block_order, "input_weight": input_weight, "output_weight": output_weight, "expand_weight": expand_weight, "reduce_weight": reduce_weight, "vectors": vectors, "input_moment": input_moment, "output_moment": output_moment, "expand_moment": expand_moment, "reduce_moment": reduce_moment, "vector_first": vector_first, "vector_second": vector_second}


@jax.custom_vjp
def low(v):
    return lax.optimization_barrier(v.astype(jnp.bfloat16)).astype(jnp.float32)

@jax.custom_vjp
def low_back(v):
    return v

def low_keep(v):
    return (low(v), None)

def low_pass(kept, grad):
    return (grad,)

def back_keep(v):
    return (v, None)

def back_low(kept, grad):
    return (low(grad),)
low.defvjp(low_keep, low_pass)
low_back.defvjp(back_keep, back_low)
norm_epsilon = 1e-05
neg_large = -1e+30
score_scale = 0.125
coef_first = 3.4445
coef_second = -4.775
coef_third = 2.0315
ortho_epsilon = 1e-07
muon_rate = 0.15
muon_moment = 0.95
muon_decay = 0.01
adam_rate = 0.3
beta_first = 0.9
beta_second = 0.95
adam_epsilon = 1e-08
highest = lax.Precision.HIGHEST

def mult(left, right):
    return jnp.dot(left, right, precision=highest)

def norm_apply(values_in, gain, shift):
    centred = values_in - lax.optimization_barrier(jnp.mean(values_in, axis=-1, keepdims=True))
    inv_std = lax.rsqrt(lax.optimization_barrier(jnp.mean(centred * centred, axis=-1, keepdims=True)) + norm_epsilon)
    return centred * inv_std * gain + shift

def attend_block(query_block, query_pos, key_heads, value_heads, key_pos):
    scores = jnp.einsum('qhd,khd->hqk', query_block, key_heads, precision=highest) * score_scale
    scores = low_back(scores)
    allowed = key_pos[None, :] <= query_pos[:, None]
    scores = jnp.where(allowed[None], scores, neg_large)
    top_score = lax.optimization_barrier(jnp.max(scores, axis=-1, keepdims=True))
    expo = jnp.exp(scores - top_score)
    prob = expo / lax.optimization_barrier(jnp.sum(expo, axis=-1, keepdims=True))
    return jnp.einsum('hqk,khd->qhd', low(prob), value_heads, precision=highest)

def attention(query_rows, key_rows, value_rows, positions):
    length = query_rows.shape[0]
    block = min(512, length)
    head_shape = (length, HEADS, HD)
    key_heads = key_rows.reshape(head_shape)
    value_heads = value_rows.reshape(head_shape)
    checked = jax.checkpoint(attend_block)

    def per_block(item):
        return checked(item[0], item[1], key_heads, value_heads, positions)
    query_blocks = query_rows.reshape(length // block, block, HEADS, HD)
    pos_blocks = positions.reshape(length // block, block)
    outputs = lax.map(per_block, (query_blocks, pos_blocks))
    return outputs.reshape(length, HEADS * HD)

def layer(stream, mix_in, mix_out, feed_in, feed_out, vec_row, positions):
    params = low(vec_row)
    pieces = [params[number * D:(number + 1) * D] for number in range(8)]
    bias_hidden = params[8 * D:]
    first_in = low(norm_apply(stream, pieces[0], pieces[1]))
    projected = mult(first_in, low(mix_in))
    query_rows = low(low_back(projected[:, :D] + pieces[2]))
    key_rows = low(low_back(projected[:, D:2 * D]))
    value_rows = low(low_back(projected[:, 2 * D:] + pieces[3]))
    mixed = low(low_back(attention(query_rows, key_rows, value_rows, positions)))
    middle = stream + low_back(mult(mixed, low(mix_out)) + pieces[4])
    second_in = low(norm_apply(middle, pieces[5], pieces[6]))
    hidden_pre = low_back(mult(second_in, low(feed_in)) + bias_hidden)
    active = low(jax.nn.gelu(hidden_pre, approximate=True))
    return middle + low_back(mult(active, low(feed_out)) + pieces[7])

def orthogonal(matrix):
    gram = mult(matrix, matrix.T)
    scale = 1.0 / (jnp.sqrt(jnp.trace(gram)) + ortho_epsilon)
    current = matrix * scale
    gram = gram * (scale * scale)
    for sweep in range(NS_STEPS):
        if sweep > 0:
            gram = mult(current, current.T)
        poly = coef_second * gram + coef_third * mult(gram, gram)
        current = coef_first * current + mult(poly, current)
    return current

def muon_update(weight, moment, grad, transpose, largest):
    new_moment = muon_moment * moment + grad
    results = []
    for layer_index in range(LAYERS):
        matrix = new_moment[layer_index]
        if transpose:
            matrix = matrix.T
        direction = orthogonal(matrix)
        if transpose:
            direction = direction.T
        results.append(weight[layer_index] * (1.0 - muon_rate * muon_decay) - muon_rate * 0.2 * math.sqrt(largest) * direction)
    return (jnp.stack(results), new_moment)

def reference(tokens, cotangent, block_order, input_weight, output_weight, expand_weight, reduce_weight, vectors, input_moment, output_moment, expand_moment, reduce_moment, vector_first, vector_second):
    row_index = jnp.arange(SEQ_LEN, dtype=jnp.int32)
    positions = (block_order[row_index // BLK] * BLK + row_index % BLK).astype(jnp.int32)
    params = (input_weight, output_weight, expand_weight, reduce_weight, vectors)

    def forward(stream, weights):
        for layer_index in range(LAYERS):
            stream = layer(stream, weights[0][layer_index], weights[1][layer_index], weights[2][layer_index], weights[3][layer_index], weights[4][layer_index], positions)
        return stream

    def per_sequence(totals, inputs):
        sequence, grad_seq = inputs
        result, pull = jax.vjp(forward, sequence.astype(jnp.float32), params)
        grad_in, grad_params = pull(grad_seq.astype(jnp.float32))
        totals = jax.tree.map(lambda left, right: left + right, totals, grad_params)
        return (totals, (result, grad_in))
    zeros = jax.tree.map(jnp.zeros_like, params)
    grads, (block_output, input_grad) = lax.scan(per_sequence, zeros, (tokens, cotangent))
    new_input_weight, new_input_moment = muon_update(input_weight, input_moment, grads[0], False, 3 * D)
    new_output_weight, new_output_moment = muon_update(output_weight, output_moment, grads[1], False, D)
    new_expand_weight, new_expand_moment = muon_update(expand_weight, expand_moment, grads[2], False, FF)
    new_reduce_weight, new_reduce_moment = muon_update(reduce_weight, reduce_moment, grads[3], True, FF)
    vec_grad = grads[4]
    new_vector_first = beta_first * vector_first + (1.0 - beta_first) * vec_grad
    new_vector_second = beta_second * vector_second + (1.0 - beta_second) * vec_grad * vec_grad
    corr_first = 1.0 - beta_first ** STEP
    corr_second = 1.0 - beta_second ** STEP
    new_vectors = vectors - adam_rate * (new_vector_first / corr_first) / (jnp.sqrt(new_vector_second / corr_second) + adam_epsilon)
    return (block_output, input_grad, new_input_weight, new_output_weight, new_expand_weight, new_reduce_weight, new_input_moment, new_output_moment, new_expand_moment, new_reduce_moment, new_vectors, new_vector_first, new_vector_second)
```

```python
import functools
import math

import jax
import jax.numpy as jnp
from jax import lax
from jax.experimental import pallas as pl
from jax.experimental.pallas import tpu as pltpu
from jax.sharding import PartitionSpec as P

HEADS = 12
NS_STEPS = 5
STEP = 10
PIECES = 8

norm_epsilon = 1e-05
neg_large = -1e30
score_scale = 0.125
coef_first = 3.4445
coef_second = -4.775
coef_third = 2.0315
ortho_epsilon = 1e-07
muon_rate = 0.15
muon_moment = 0.95
muon_decay = 0.01
adam_rate = 0.3
beta_first = 0.9
beta_second = 0.95
adam_epsilon = 1e-08
gelu_inner = 0.7978845608
gelu_cubic = 0.044715
shifts = (0.0, 0.0, 0.17, 1.0, 0.8)

f32 = jnp.float32
bf16 = jnp.bfloat16
vmem_limit = 56 * 1024 * 1024


def mm(left, right):
    return jnp.dot(left, right, preferred_element_type=f32)


def mm_nt(left, right):
    return lax.dot_general(left, right, (((1,), (1,)), ((), ())), preferred_element_type=f32)


def mm_tn(left, right):
    return lax.dot_general(left, right, (((0,), (0,)), ((), ())), preferred_element_type=f32)


def cost(micros):
    return pl.CostEstimate(
        flops=int(micros * 1e9), bytes_accessed=int(micros * 1e6), transcendentals=0
    )


def params(grid_dims):
    return pltpu.CompilerParams(
        dimension_semantics=("arbitrary",) * grid_dims, vmem_limit_bytes=vmem_limit
    )


def normalized(values_in):
    centred = values_in - jnp.mean(values_in, axis=-1, keepdims=True)
    inv_std = lax.rsqrt(jnp.mean(centred * centred, axis=-1, keepdims=True) + norm_epsilon)
    return centred * inv_std, inv_std


def norm_backward(grad_out, normed, inv_std, gain):
    scaled = grad_out * gain
    return inv_std * (
        scaled
        - jnp.mean(scaled, axis=-1, keepdims=True)
        - normed * jnp.mean(scaled * normed, axis=-1, keepdims=True)
    )


def pair_lanes(values_in, local, start, size):
    return jnp.concatenate(
        [values_in[:local, start : start + size], values_in[local:, start : start + size]], axis=1
    )


def join_heads(ref, local, hd):
    rows = []
    for s in range(2):
        rows.append(
            jnp.concatenate(
                [ref[h][:, s * hd : (s + 1) * hd].astype(f32) for h in range(HEADS)], axis=1
            )
        )
    return jnp.concatenate(rows, axis=0)


def qkv_kernel(x_ref, vec_ref, w_ref, a_ref, out_ref, proj_ref):
    step = pl.program_id(0)
    steps, _, chunk = proj_ref.shape
    local = out_ref.shape[1]
    hd = out_ref.shape[2] // 6
    width = x_ref.shape[1]

    @pl.when(step == 0)
    def _():
        normed, _ = normalized(x_ref[...].astype(f32))
        a_ref[...] = (normed * vec_ref[0:1, :] + vec_ref[1:2, :]).astype(bf16)

    proj_ref[step] = mm_nt(a_ref[...], w_ref[...].reshape(chunk, width))

    @pl.when(step == steps - 1)
    def _():
        proj = jnp.concatenate([proj_ref[i] for i in range(steps)], axis=1)
        bias = (vec_ref[2:3, :], jnp.zeros((1, width), f32), vec_ref[3:4, :])
        for part in range(3):
            piece = proj[:, part * width : (part + 1) * width] + bias[part]
            for h in range(HEADS):
                out_ref[h, :, part * 2 * hd : (part + 1) * 2 * hd] = pair_lanes(
                    piece, local, h * hd, hd
                ).astype(bf16)
        for h in range(HEADS, out_ref.shape[0]):
            out_ref[h] = jnp.zeros(out_ref.shape[1:], bf16)


def shard_blocks(array, start, own, steps):
    ctx, _, width = array.shape
    group = ctx // steps
    if own % 16 == 0 and start % own == 0:
        return array, pl.BlockSpec(
            (group, own, width), lambda i: (i if steps > 1 else 0, start // own, 0)
        )
    part = array[:, start : start + own].reshape(steps, group * own, width)
    return part, pl.BlockSpec((1, group * own, width), lambda i: (i if steps > 1 else 0, 0, 0))


def qkv_forward(x, vec, weights, at, own_in, local):
    rows, width = x.shape
    ctx = weights.shape[0]
    hd = width // HEADS
    steps = 4
    w_array, w_spec = shard_blocks(weights, at, own_in, steps)
    whole = lambda i: (0, 0)
    return pl.pallas_call(
        qkv_kernel,
        grid=(steps,),
        in_specs=[
            pl.BlockSpec((rows, width), whole),
            pl.BlockSpec(vec.shape, whole),
            w_spec,
        ],
        out_specs=[
            pl.BlockSpec((rows, width), whole),
            pl.BlockSpec((ctx, local, 6 * hd), lambda i: (0, 0, 0)),
        ],
        out_shape=[
            jax.ShapeDtypeStruct((rows, width), bf16),
            jax.ShapeDtypeStruct((ctx, local, 6 * hd), bf16),
        ],
        scratch_shapes=[pltpu.VMEM((steps, rows, 3 * width // steps), f32)],
        compiler_params=params(1),
        cost_estimate=cost(5),
        name="qkv_forward",
    )(x, vec, w_array)


def head_qkv_kernel(head_ref, x_ref, vec_ref, bias_ref, w_ref, a_ref, out_ref, w_all_ref, own_ref):
    shards, rows, width = x_ref.shape
    local = rows // 2
    hd = out_ref.shape[1] // 6

    @pl.when(pl.program_id(0) == 0)
    def _():
        w_all_ref[...] = w_ref[...].reshape(w_all_ref.shape)
        for part in range(3):
            first = pl.multiple_of(part * width + head_ref[0] * hd, hd)
            own_ref[part * hd : (part + 1) * hd, :] = w_all_ref[pl.ds(first, hd), :]

    normed, _ = normalized(x_ref[...].reshape(shards * rows, width).astype(f32))
    first_in = (normed * vec_ref[0:1, :] + vec_ref[1:2, :]).astype(bf16)
    a_ref[...] = first_in.reshape(shards, rows, width)
    proj = (mm_nt(first_in, own_ref[...]) + bias_ref[...]).reshape(shards, 2, local, 3 * hd)
    sides = [proj[:, s].reshape(shards * local, 3 * hd) for s in range(2)]
    for part in range(3):
        cut = slice(part * hd, (part + 1) * hd)
        out_ref[:, 2 * part * hd : 2 * (part + 1) * hd] = jnp.concatenate(
            [sides[0][:, cut], sides[1][:, cut]], axis=1
        ).astype(bf16)


def head_qkv(head, tokens_all, tokens_at, vec, bias, weights, at, own_in, rows):
    ctx, _, width = tokens_all.shape
    hd = width // HEADS
    local = rows // 2
    x_array, x_spec = shard_blocks(tokens_all, tokens_at, rows, ctx // 4)
    w_array, w_spec = shard_blocks(weights, at, own_in, 1)
    whole = lambda i: (0, 0)
    return pl.pallas_call(
        head_qkv_kernel,
        grid=(ctx // 4,),
        in_specs=[
            pl.BlockSpec(memory_space=pltpu.SMEM),
            x_spec,
            pl.BlockSpec(vec.shape, whole),
            pl.BlockSpec(bias.shape, whole),
            w_spec,
        ],
        out_specs=[
            pl.BlockSpec((4, rows, width), lambda i: (i, 0, 0)),
            pl.BlockSpec((4 * local, 6 * hd), lambda i: (i, 0)),
        ],
        out_shape=[
            jax.ShapeDtypeStruct((ctx, rows, width), bf16),
            jax.ShapeDtypeStruct((ctx * local, 6 * hd), bf16),
        ],
        scratch_shapes=[pltpu.VMEM((3 * width, width), bf16), pltpu.VMEM((3 * hd, width), bf16)],
        compiler_params=params(1),
        cost_estimate=cost(6),
        name="head_qkv",
    )(head, x_array, vec, bias, w_array)


def lane_masks(rows, lanes):
    lane = lax.broadcasted_iota(jnp.int32, (rows, lanes), 1)
    first = jnp.where(lane < lanes // 2, 1.0, 0.0)
    return first.astype(bf16), (1.0 - first).astype(bf16)


def attn_fwd_kernel(qpos_ref, kpos_ref, q_ref, k_ref, v_ref, of_ref, ob_ref, p_ref):
    allowed = kpos_ref[...] <= qpos_ref[...]
    q_masks = lane_masks(*q_ref.shape)
    v_masks = lane_masks(*v_ref.shape)
    out = jnp.zeros(of_ref.shape, f32)
    for s in range(2):
        scores = mm_nt(q_ref[...] * q_masks[s], k_ref[...]) * score_scale
        scores = jnp.where(allowed, scores, neg_large)
        expo = jnp.exp(scores - jnp.max(scores, axis=-1, keepdims=True))
        prob = (expo * (1.0 / jnp.sum(expo, axis=-1, keepdims=True))).astype(bf16)
        p_ref[s] = prob
        out = out + mm(prob, v_ref[...] * v_masks[s])
    of_ref[...] = out
    ob_ref[...] = out.astype(bf16)


def attn_forward(qkv, qpos, kpos):
    length, lanes = qkv.shape
    pair = lanes // 3
    tile = min(256, length)
    return pl.pallas_call(
        attn_fwd_kernel,
        grid=(length // tile,),
        in_specs=[
            pl.BlockSpec((tile, 1), lambda i: (i, 0)),
            pl.BlockSpec((1, length), lambda i: (0, 0)),
            pl.BlockSpec((tile, pair), lambda i: (i, 0)),
            pl.BlockSpec((length, pair), lambda i: (0, 1)),
            pl.BlockSpec((length, pair), lambda i: (0, 2)),
        ],
        out_specs=[
            pl.BlockSpec((tile, pair), lambda i: (i, 0)),
            pl.BlockSpec((tile, pair), lambda i: (i, 0)),
            pl.BlockSpec((2, tile, length), lambda i: (0, i, 0)),
        ],
        out_shape=[
            jax.ShapeDtypeStruct((length, pair), f32),
            jax.ShapeDtypeStruct((length, pair), bf16),
            jax.ShapeDtypeStruct((2, length, length), bf16),
        ],
        compiler_params=params(1),
        cost_estimate=cost(8),
        name="attn_forward",
    )(qpos, kpos, qkv, qkv, qkv)


def attn_bwd_kernel(q_ref, go_ref, of_ref, p_ref, k_ref, v_ref, out_ref, dk_ref, dv_ref):
    step = pl.program_id(0)
    tile, pair = q_ref.shape
    masks = lane_masks(tile, pair)
    k_masks = lane_masks(*k_ref.shape)

    @pl.when(step == 0)
    def _():
        dk_ref[...] = jnp.zeros_like(dk_ref)
        dv_ref[...] = jnp.zeros_like(dv_ref)

    dq = jnp.zeros((tile, pair), f32)
    for s in range(2):
        go = go_ref[...] * masks[s]
        row_dot = jnp.sum(go.astype(f32) * of_ref[...], axis=-1, keepdims=True)
        prob = p_ref[s]
        grad_prob = mm_nt(go, v_ref[...])
        ds = (prob.astype(f32) * (grad_prob - row_dot)).astype(bf16)
        dv_ref[...] += mm_tn(go, prob)
        dk_ref[...] += mm_tn(q_ref[...] * masks[s], ds)
        dq = dq + mm(ds, k_ref[...] * k_masks[s])
    out_ref[pl.ds(pl.multiple_of(step * tile, tile), tile), 0:pair] = (dq * score_scale).astype(bf16)

    @pl.when(step == pl.num_programs(0) - 1)
    def _():
        out_ref[:, pair : 2 * pair] = (dk_ref[...].T * score_scale).astype(bf16)
        out_ref[:, 2 * pair :] = dv_ref[...].T.astype(bf16)


def attn_backward(qkv, go, out_full, prob):
    length, lanes = qkv.shape
    pair = lanes // 3
    tile = min(256, length)
    return pl.pallas_call(
        attn_bwd_kernel,
        grid=(length // tile,),
        in_specs=[
            pl.BlockSpec((tile, pair), lambda i: (i, 0)),
            pl.BlockSpec((tile, pair), lambda i: (i, 0)),
            pl.BlockSpec((tile, pair), lambda i: (i, 0)),
            pl.BlockSpec((2, tile, length), lambda i: (0, i, 0)),
            pl.BlockSpec((length, pair), lambda i: (0, 1)),
            pl.BlockSpec((length, pair), lambda i: (0, 2)),
        ],
        out_specs=pl.BlockSpec((length, lanes), lambda i: (0, 0)),
        out_shape=jax.ShapeDtypeStruct((length, lanes), bf16),
        scratch_shapes=[pltpu.VMEM((pair, length), f32), pltpu.VMEM((pair, length), f32)],
        compiler_params=params(1),
        cost_estimate=cost(8),
        name="attn_backward",
    )(qkv, go, out_full, prob, qkv, qkv)


def mlp_fwd_kernel(o_ref, x_ref, vec_ref, mix_ref, fc_ref, red_ref, mid_ref, c_ref, h_ref, out_ref):
    step = pl.program_id(0)
    rows, width = x_ref.shape

    @pl.when(step == 0)
    def _():
        mixed = join_heads(o_ref, rows // 2, o_ref.shape[2] // 2).astype(bf16)
        mix_w = mix_ref[...].reshape(width, width)
        middle = x_ref[...].astype(f32) + (mm_nt(mixed, mix_w) + vec_ref[4:5, :])
        mid_ref[...] = middle
        normed, _ = normalized(middle)
        c_ref[...] = (normed * vec_ref[5:6, :] + vec_ref[6:7, :]).astype(bf16)
        out_ref[...] = middle + vec_ref[7:8, :]

    hidden = mm_nt(c_ref[...], fc_ref[...].reshape(width, width))
    hidden = hidden + vec_ref[pl.ds(PIECES + step, 1), :]
    h_ref[...] = hidden
    inner = jnp.tanh(gelu_inner * (hidden + gelu_cubic * hidden * hidden * hidden))
    active = (0.5 * hidden * (1.0 + inner)).astype(bf16)
    out_ref[...] += mm(active, red_ref[...].reshape(width, width))


def mlp_forward(o_pack, x, vec, weights, at, own_ff, own_mix):
    rows, width = x.shape
    hidden = weights.shape[0] * own_ff
    steps = hidden // width
    fc_array, fc_spec = shard_blocks(weights, at["fc"], own_ff, steps)
    red_array, red_spec = shard_blocks(weights, at["red"], own_ff, steps)
    mix_array, mix_spec = shard_blocks(weights, at["mix"], own_mix, 1)
    whole = lambda i: (0, 0)
    return pl.pallas_call(
        mlp_fwd_kernel,
        grid=(steps,),
        in_specs=[
            pl.BlockSpec(o_pack.shape, lambda i: (0, 0, 0)),
            pl.BlockSpec((rows, width), whole),
            pl.BlockSpec(vec.shape, whole),
            mix_spec,
            fc_spec,
            red_spec,
        ],
        out_specs=[
            pl.BlockSpec((rows, width), whole),
            pl.BlockSpec((rows, width), whole),
            pl.BlockSpec((rows, width), lambda i: (0, i)),
            pl.BlockSpec((rows, width), whole),
        ],
        out_shape=[
            jax.ShapeDtypeStruct((rows, width), f32),
            jax.ShapeDtypeStruct((rows, width), bf16),
            jax.ShapeDtypeStruct((rows, hidden), f32),
            jax.ShapeDtypeStruct((rows, width), f32),
        ],
        compiler_params=params(1),
        cost_estimate=cost(8),
        name="mlp_forward",
    )(o_pack, x, vec, mix_array, fc_array, red_array)


def gelu_slope(hidden):
    square = hidden * hidden
    inner = jnp.tanh(gelu_inner * (hidden + gelu_cubic * hidden * square))
    slope = 0.5 * (1.0 + inner) + (0.5 * gelu_inner) * hidden * (1.0 - inner * inner) * (
        1.0 + (3.0 * gelu_cubic) * square
    )
    return inner, slope


def mlp_bwd_kernel(
    gr_ref, mid_ref, h_ref, vec_ref, mix_ref, fc_ref, red_ref,
    gz_ref, gmid_ref, gy_ref, go_ref, vg_ref, gc_ref,
):
    step = pl.program_id(0)
    rows, width = gr_ref.shape

    @pl.when(step == 0)
    def _():
        gz_ref[...] = gr_ref[...].astype(bf16)
        gc_ref[...] = jnp.zeros_like(gc_ref)

    _, slope = gelu_slope(h_ref[...])
    grad_hidden = (mm_nt(gz_ref[...], red_ref[...].reshape(width, width)) * slope).astype(bf16)
    vg_ref[pl.ds(4 + step, 1), :] = jnp.sum(grad_hidden.astype(f32), axis=0, keepdims=True)
    gc_ref[...] += mm(grad_hidden, fc_ref[...].reshape(width, width))

    @pl.when(step == pl.num_programs(0) - 1)
    def _():
        grad = gr_ref[...].astype(f32)
        normed, inv_std = normalized(mid_ref[...])
        grad_second = gc_ref[...]
        grad_mid = grad + norm_backward(grad_second, normed, inv_std, vec_ref[5:6, :])
        gmid_ref[...] = grad_mid
        gy = grad_mid.astype(bf16)
        gy_ref[...] = gy
        vg_ref[0:1, :] = jnp.sum(gy.astype(f32), axis=0, keepdims=True)
        vg_ref[1:2, :] = jnp.sum(grad_second * normed, axis=0, keepdims=True)
        vg_ref[2:3, :] = jnp.sum(grad_second, axis=0, keepdims=True)
        vg_ref[3:4, :] = jnp.sum(gz_ref[...].astype(f32), axis=0, keepdims=True)
        grad_attn = mm(gy, mix_ref[...].reshape(width, width))
        hd = go_ref.shape[2] // 2
        for h in range(HEADS):
            go_ref[h] = pair_lanes(grad_attn, rows // 2, h * hd, hd).astype(bf16)
        for h in range(HEADS, go_ref.shape[0]):
            go_ref[h] = jnp.zeros(go_ref.shape[1:], bf16)


def mlp_backward(gr, mid, hidden, vec, weights, at, own_ff, own_mix):
    rows, width = mid.shape
    ctx = weights.shape[0]
    steps = hidden.shape[1] // width
    hd = width // HEADS
    fc_array, fc_spec = shard_blocks(weights, at["fc"], own_ff, steps)
    red_array, red_spec = shard_blocks(weights, at["red"], own_ff, steps)
    mix_array, mix_spec = shard_blocks(weights, at["mix"], own_mix, 1)
    whole = lambda i: (0, 0)
    return pl.pallas_call(
        mlp_bwd_kernel,
        grid=(steps,),
        in_specs=[
            pl.BlockSpec((rows, width), whole),
            pl.BlockSpec((rows, width), whole),
            pl.BlockSpec((rows, width), lambda i: (0, i)),
            pl.BlockSpec(vec.shape, whole),
            mix_spec,
            fc_spec,
            red_spec,
        ],
        out_specs=[
            pl.BlockSpec((rows, width), whole),
            pl.BlockSpec((rows, width), whole),
            pl.BlockSpec((rows, width), whole),
            pl.BlockSpec((ctx, rows // 2, 2 * hd), lambda i: (0, 0, 0)),
            pl.BlockSpec((PIECES, width), whole),
        ],
        out_shape=[
            jax.ShapeDtypeStruct((rows, width), bf16),
            jax.ShapeDtypeStruct((rows, width), f32),
            jax.ShapeDtypeStruct((rows, width), bf16),
            jax.ShapeDtypeStruct((ctx, rows // 2, 2 * hd), bf16),
            jax.ShapeDtypeStruct((PIECES, width), f32),
        ],
        scratch_shapes=[pltpu.VMEM((rows, width), f32)],
        compiler_params=params(1),
        cost_estimate=cost(8),
        name="mlp_backward",
    )(gr, mid, hidden, vec, mix_array, fc_array, red_array)


def qkv_bwd_kernel(d_ref, x_ref, gmid_ref, vec_ref, w_ref, gin_ref, vg_ref, d_all_ref, ga_ref):
    step = pl.program_id(0)
    steps, rows, chunk = d_all_ref.shape
    width = x_ref.shape[1]

    @pl.when(step == 0)
    def _():
        hd = d_ref.shape[2] // 6
        parts = []
        for part in range(3):
            for s in range(2):
                start = (2 * part + s) * hd
                parts.append(
                    jnp.concatenate(
                        [d_ref[h, :, start : start + hd].astype(f32) for h in range(HEADS)], axis=1
                    )
                )
        joined = jnp.concatenate(
            [jnp.concatenate([parts[2 * part], parts[2 * part + 1]], axis=0) for part in range(3)],
            axis=1,
        )
        vg_ref[...] = jnp.zeros_like(vg_ref)
        vg_ref[2:3, :] = jnp.sum(joined[:, :width], axis=0, keepdims=True)
        vg_ref[3:4, :] = jnp.sum(joined[:, 2 * width :], axis=0, keepdims=True)
        for i in range(steps):
            d_all_ref[i] = joined[:, i * chunk : (i + 1) * chunk].astype(bf16)
        ga_ref[...] = jnp.zeros_like(ga_ref)

    ga_ref[...] += mm(d_all_ref[step], w_ref[...].reshape(chunk, width))

    @pl.when(step == steps - 1)
    def _():
        normed, inv_std = normalized(x_ref[...].astype(f32))
        grad_first = ga_ref[...]
        gin_ref[...] = gmid_ref[...] + norm_backward(grad_first, normed, inv_std, vec_ref[0:1, :])
        vg_ref[0:1, :] = jnp.sum(grad_first * normed, axis=0, keepdims=True)
        vg_ref[1:2, :] = jnp.sum(grad_first, axis=0, keepdims=True)


def qkv_backward(dqkv, x, gmid, vec, weights, at, own_in):
    rows, width = x.shape
    steps = 4
    w_array, w_spec = shard_blocks(weights, at, own_in, steps)
    whole = lambda i: (0, 0)
    return pl.pallas_call(
        qkv_bwd_kernel,
        grid=(steps,),
        in_specs=[
            pl.BlockSpec(dqkv.shape, lambda i: (0, 0, 0)),
            pl.BlockSpec((rows, width), whole),
            pl.BlockSpec((rows, width), whole),
            pl.BlockSpec(vec.shape, whole),
            w_spec,
        ],
        out_specs=[
            pl.BlockSpec((rows, width), whole),
            pl.BlockSpec((PIECES, width), whole),
        ],
        out_shape=[
            jax.ShapeDtypeStruct((rows, width), f32),
            jax.ShapeDtypeStruct((PIECES, width), f32),
        ],
        scratch_shapes=[
            pltpu.VMEM((steps, rows, 3 * width // steps), bf16),
            pltpu.VMEM((rows, width), f32),
        ],
        compiler_params=params(1),
        cost_estimate=cost(5),
        name="qkv_backward",
    )(dqkv, x, gmid, vec, w_array)


def hidden_grads_kernel(c_ref, gz_ref, fc_ref, red_ref, bias_ref, gfc_ref, gred_ref):
    own, width = gfc_ref.shape
    second = c_ref[...].reshape(-1, width)
    branch = gz_ref[...].reshape(-1, width)
    hidden = mm_nt(fc_ref[...], second) + bias_ref[...]
    inner, slope = gelu_slope(hidden)
    active = (0.5 * hidden * (1.0 + inner)).astype(bf16)
    grad_hidden = (mm_nt(red_ref[...], branch) * slope).astype(bf16)

    @pl.when(pl.program_id(0) == 0)
    def _():
        gfc_ref[...] = jnp.zeros_like(gfc_ref)
        gred_ref[...] = jnp.zeros_like(gred_ref)

    gfc_ref[...] += mm(grad_hidden, second)
    gred_ref[...] += mm(active, branch)


def hidden_grads(c_all, c_at, gz_all, gz_at, fc_own, red_own, bias, rows):
    ctx, _, width = c_all.shape
    own_ff = fc_own.shape[0]
    steps = ctx // 4
    c_array, c_spec = shard_blocks(c_all, c_at, rows, steps)
    gz_array, gz_spec = shard_blocks(gz_all, gz_at, rows, steps)
    whole = lambda i: (0, 0)
    return pl.pallas_call(
        hidden_grads_kernel,
        grid=(steps,),
        in_specs=[
            c_spec,
            gz_spec,
            pl.BlockSpec((own_ff, width), whole),
            pl.BlockSpec((own_ff, width), whole),
            pl.BlockSpec((own_ff, 1), whole),
        ],
        out_specs=[pl.BlockSpec((own_ff, width), whole)] * 2,
        out_shape=[jax.ShapeDtypeStruct((own_ff, width), f32)] * 2,
        compiler_params=params(1),
        cost_estimate=cost(6),
        name="hidden_grads",
    )(c_array, gz_array, fc_own, red_own, bias)


def hidden_ready_kernel(c_ref, fc_ref, bias_ref, u_ref, slope_ref):
    width = fc_ref.shape[1]
    hidden = mm_nt(fc_ref[...], c_ref[...].reshape(-1, width)) + bias_ref[...]
    inner, slope = gelu_slope(hidden)
    u_ref[...] = (0.5 * hidden * (1.0 + inner)).astype(bf16)
    slope_ref[...] = slope


def rows_by_z(c_all, c_at, rows):
    ctx, _, width = c_all.shape
    assert c_at % rows == 0
    view = c_all.reshape(ctx // 16, 4, 4, *c_all.shape[1:])
    return view, pl.BlockSpec(
        (1, 4, 1, rows, width),
        lambda i: (i // 4, 0, (i % 2) * 2 + (i // 2) % 2, c_at // rows, 0),
    )


def hidden_ready(c_all, c_at, fc_own, bias, rows):
    ctx, _, width = c_all.shape
    own_ff = fc_own.shape[0]
    c_array, c_spec = rows_by_z(c_all, c_at, rows)
    whole = lambda i: (0, 0)
    return pl.pallas_call(
        hidden_ready_kernel,
        grid=(ctx // 4,),
        in_specs=[
            c_spec,
            pl.BlockSpec((own_ff, width), whole),
            pl.BlockSpec((own_ff, 1), whole),
        ],
        out_specs=[pl.BlockSpec((own_ff, 4 * rows), lambda i: (0, i))] * 2,
        out_shape=[
            jax.ShapeDtypeStruct((own_ff, ctx * rows), bf16),
            jax.ShapeDtypeStruct((own_ff, ctx * rows), f32),
        ],
        compiler_params=params(1),
        cost_estimate=cost(5),
        name="hidden_ready",
    )(c_array, fc_own, bias)


def hidden_last_kernel(c_ref, gz_ref, u_ref, slope_ref, red_ref, gfc_ref, gred_ref):
    width = red_ref.shape[1]
    second = c_ref[...].reshape(-1, width)
    branch = gz_ref[...].reshape(-1, width)
    grad_hidden = (mm_nt(red_ref[...], branch) * slope_ref[...]).astype(bf16)

    @pl.when(pl.program_id(0) == 0)
    def _():
        gfc_ref[...] = jnp.zeros_like(gfc_ref)
        gred_ref[...] = jnp.zeros_like(gred_ref)

    gred_ref[...] += mm(u_ref[...], branch)
    gfc_ref[...] += mm(grad_hidden, second)


def hidden_last(c_all, c_at, gz_all, active, slope, red_own, rows):
    steps, _, width = gz_all.shape
    own_ff = red_own.shape[0]
    c_array, c_spec = rows_by_z(c_all, c_at, rows)
    whole = lambda i: (0, 0)
    return pl.pallas_call(
        hidden_last_kernel,
        grid=(steps,),
        in_specs=[
            c_spec,
            pl.BlockSpec((1, 4 * rows, width), lambda i: (i, 0, 0)),
            pl.BlockSpec((own_ff, 4 * rows), lambda i: (0, i)),
            pl.BlockSpec((own_ff, 4 * rows), lambda i: (0, i)),
            pl.BlockSpec((own_ff, width), whole),
        ],
        out_specs=[pl.BlockSpec((own_ff, width), whole)] * 2,
        out_shape=[jax.ShapeDtypeStruct((own_ff, width), f32)] * 2,
        compiler_params=params(1),
        cost_estimate=cost(5),
        name="hidden_last",
    )(c_array, gz_all, active, slope, red_own)


def head_grads_kernel(pack_ref, rows_ref, out_ref):
    length, lanes = pack_ref.shape
    _, rows, width = rows_ref.shape
    local = rows // 2
    hd = width // HEADS
    for s in range(2):
        piece = rows_ref[:, s * local : (s + 1) * local, :].reshape(length, width)
        result = mm_tn(pack_ref[...], piece)
        for part in range(out_ref.shape[0] // hd):
            start = (2 * part + s) * hd
            if s == 0:
                out_ref[part * hd : (part + 1) * hd, :] = result[start : start + hd]
            else:
                out_ref[part * hd : (part + 1) * hd, :] += result[start : start + hd]


def head_grads(pack, rows_all, at, rows):
    length, lanes = pack.shape
    ctx, _, width = rows_all.shape
    rows_array, rows_spec = shard_blocks(rows_all, at, rows, 1)
    return pl.pallas_call(
        head_grads_kernel,
        grid=(1,),
        in_specs=[
            pl.BlockSpec((length, lanes), lambda i: (0, 0)),
            rows_spec,
        ],
        out_specs=pl.BlockSpec((lanes // 2, width), lambda i: (0, 0)),
        out_shape=jax.ShapeDtypeStruct((lanes // 2, width), f32),
        compiler_params=params(1),
        cost_estimate=cost(4),
        name="head_grads",
    )(pack, rows_array)


def copy_all(moves, sems):
    copies = [pltpu.make_async_copy(src, dst, sems.at[i]) for i, (src, dst) in enumerate(moves)]
    for copy in copies:
        copy.start()
    for copy in copies:
        copy.wait()


def ns_kernel(own, parts_count, role_ref, *refs):
    parts, (sums_ref, out_ref) = refs[:parts_count], refs[parts_count : parts_count + 2]
    y_ref, full_ref, low_ref, gram_ref, poly_ref, sems = refs[parts_count + 2 :]
    length, side = y_ref.shape
    own_in, own_ff, own_mix = own
    tile = 256
    role = role_ref[0]
    is_in, is_mix = role == 0, role == 3
    is_long = (role == 1) | (role == 2)
    kinds = ((is_long, length, own_ff), (is_in, 3 * side, own_in), (is_mix, side, own_mix))
    chunks = jnp.where(is_mix, 1, jnp.where(is_in, 3, length // side))

    @pl.when(is_long)
    def _():
        moves, start = [], 0
        for part in parts:
            moves.append((part, y_ref.at[start : start + part.shape[0]]))
            start += part.shape[0]
        copy_all(moves, sems)

    @pl.when(is_in)
    def _():
        copy_all([(sums_ref, y_ref.at[: 3 * side])], sems)

    @pl.when(is_mix)
    def _():
        copy_all([(sums_ref.at[:side], y_ref.at[:side])], sems)

    eye = jnp.where(
        lax.broadcasted_iota(jnp.int32, (side, side), 0)
        == lax.broadcasted_iota(jnp.int32, (side, side), 1),
        1.0,
        0.0,
    )

    def each_chunk(work):
        def one(i, carry):
            work(pl.ds(pl.multiple_of(i * side, side), side))
            return carry

        lax.fori_loop(0, chunks, one, 0)

    def gram():
        for kind, columns, _ in kinds:

            @pl.when(kind)
            def _():
                for i in range(side // tile):
                    rows = slice(i * tile, (i + 1) * tile)
                    gram_ref[rows, i * tile :] = mm_nt(
                        low_ref[rows, :columns], low_ref[i * tile :, :columns]
                    )

        for i in range(side // tile):
            for j in range(i + 1, side // tile):
                gram_ref[j * tile : (j + 1) * tile, i * tile : (i + 1) * tile] = gram_ref[
                    i * tile : (i + 1) * tile, j * tile : (j + 1) * tile
                ].T

    def load(cols):
        low_ref[:, cols] = y_ref[cols, :].T

    each_chunk(load)
    gram()
    scale = 1.0 / (jnp.sqrt(jnp.sum(gram_ref[...] * eye, keepdims=True)) + ortho_epsilon)
    gram_ref[...] = gram_ref[...] * (scale * scale)

    linear_only = coef_second * gram_ref[...]
    low_gram = gram_ref[...].astype(bf16)
    poly_ref[...] = (scale * (linear_only + coef_third * mm(low_gram, low_gram))).astype(bf16)

    def first(cols):
        matrix = low_ref[:, cols]
        fresh = (coef_first * scale) * matrix.astype(f32) + mm(poly_ref[...], matrix)
        full_ref[:, cols] = fresh
        low_ref[:, cols] = fresh.astype(bf16)

    each_chunk(first)
    gram()

    def polynomial(k):
        shift = jnp.float32(shifts[1])
        for number in range(2, NS_STEPS):
            shift = jnp.where(k == number, shifts[number], shift)
        linear = coef_second + 2.0 * coef_third * shift
        diff = gram_ref[...] - shift * eye
        low_diff = diff.astype(bf16)
        poly_ref[...] = (linear * diff + coef_third * mm(low_diff, low_diff)).astype(bf16)
        return coef_first + coef_second * shift + coef_third * shift * shift

    def sweep(k, carry):
        base = polynomial(k)

        def update(cols):
            fresh = base * full_ref[:, cols] + mm(poly_ref[...], low_ref[:, cols])
            full_ref[:, cols] = fresh
            low_ref[:, cols] = fresh.astype(bf16)

        each_chunk(update)
        gram()
        return carry

    lax.fori_loop(1, NS_STEPS - 1, sweep, 0)
    base = polynomial(NS_STEPS - 1)
    wanted = -(-4 * own_ff // tile) * tile
    fresh = base * full_ref[:, :wanted] + mm(poly_ref[...], low_ref[:, :wanted])
    gram_ref[:wanted, :] = fresh.T
    for kind, _, size in kinds:

        @pl.when(kind)
        def _():
            for k in range(4):
                piece = gram_ref[k * size : (k + 1) * size, :].astype(bf16)
                if size < own_ff:
                    piece = jnp.concatenate(
                        [piece, jnp.zeros((own_ff - size, side), bf16)], axis=0
                    )
                out_ref[k * own_ff : (k + 1) * own_ff, :] = piece


def orthogonal(role, columns, sums, own):
    width = sums.shape[1]
    parts = [part.reshape(-1, width) for column in columns for part in column]
    length = sum(part.shape[0] for part in parts)
    return pl.pallas_call(
        functools.partial(ns_kernel, own, len(parts)),
        out_shape=jax.ShapeDtypeStruct((4 * own[1], width), bf16),
        in_specs=[pl.BlockSpec(memory_space=pltpu.SMEM)]
        + [pl.BlockSpec(memory_space=pl.ANY)] * (len(parts) + 1),
        out_specs=pl.BlockSpec(memory_space=pltpu.VMEM),
        scratch_shapes=[
            pltpu.VMEM((length, width), bf16),
            pltpu.VMEM((width, length), f32),
            pltpu.VMEM((width, length), bf16),
            pltpu.VMEM((width, width), f32),
            pltpu.VMEM((width, width), bf16),
            pltpu.SemaphoreType.DMA((len(parts),)),
        ],
        compiler_params=pltpu.CompilerParams(vmem_limit_bytes=vmem_limit),
        cost_estimate=cost(46),
        name="newton_schulz",
    )(role, *parts, sums)


def column_place(mask):
    return ((mask >> 1) & 1) + 2 * (mask & 1)


def sum_heads_kernel(own_mix, old_at, role_ref, near_ref, *refs):
    parts, (acts_ref, y_out_ref, fresh_ref) = refs[:8], refs[8:11]
    held_ref, old_ref, y_ref, natural_ref, turned_ref, sems = refs[11:]
    width = held_ref.shape[3]
    own_in = fresh_ref.shape[1]
    hd = width // HEADS
    block = 16
    place = [column_place(near_ref[0] ^ n) for n in range(4)]

    def fetch(size, at, own):
        moves = [(acts_ref.at[:, at : at + own], old_ref.at[:, :own])]
        for c in range(4):
            moves.append((parts[2 * c].at[:size], held_ref.at[c, 0, :size]))
            moves.append((parts[2 * c + 1].at[:, :size], held_ref.at[c, 1:, :size]))
        copy_all(moves, sems)

    @pl.when(role_ref[0] == 0)
    def _():
        fetch(3 * hd, old_at, own_in)
        for z in range(4):
            for n in range(4):
                for start in range(0, own_in, block):
                    first = (4 * z + n) * own_in + start
                    part, rest = divmod(first, width)
                    h, off = divmod(rest, hd)
                    at = part * hd + off
                    source = held_ref[place[h & 3], h >> 2, at : at + block, :]
                    natural_ref[place[n], z, start : start + block, :] = source
                    old = old_ref[4 * z + n, start : start + block, :]
                    y_ref[pl.ds((place[n] * 4 + z) * own_in + start, block), :] = (
                        muon_moment * old.astype(f32) + source.astype(f32)
                    ).astype(bf16)
        fresh_ref[...] = natural_ref[0]
        copy_all([(y_ref, y_out_ref)], sems)

    @pl.when(role_ref[0] == 3)
    def _():
        fetch(hd, old_at + own_in, own_mix)
        for h in range(HEADS):
            turned_ref[h * hd : (h + 1) * hd, :] = held_ref[
                place[h & 3], 3 ^ (h >> 2), :hd
            ].astype(f32)
        turned_ref[...] = turned_ref[...].T
        fresh_ref[...] = jnp.zeros_like(fresh_ref)
        for z in range(4):
            for n in range(4):
                first = (4 * z + n) * own_mix
                source = turned_ref[first : first + own_mix, :]
                natural_ref[place[n], 3 ^ z, :own_mix] = source.astype(bf16)
                old = old_ref[4 * z + n, :own_mix]
                y_ref[pl.ds((place[n] * 4 + (3 ^ z)) * own_mix, own_mix), :] = (
                    muon_moment * old.astype(f32) + source
                ).astype(bf16)
        fresh_ref[:, :own_mix] = natural_ref[0, :, :own_mix]
        copy_all([(y_ref.at[:width], y_out_ref.at[:width])], sems)

    @pl.when((role_ref[0] == 1) | (role_ref[0] == 2))
    def _():
        fresh_ref[...] = jnp.zeros_like(fresh_ref)


def sum_heads(role, near, columns, acts, old_at, own_in, own_mix):
    ctx, _, width = acts.shape
    parts = [part for column in columns for part in column]
    size = parts[0].shape[0]
    smem = pl.BlockSpec(memory_space=pltpu.SMEM)
    hbm = pl.BlockSpec(memory_space=pl.ANY)
    return pl.pallas_call(
        functools.partial(sum_heads_kernel, own_mix, old_at),
        out_shape=[
            jax.ShapeDtypeStruct((ctx * own_in, width), bf16),
            jax.ShapeDtypeStruct((4, own_in, width), bf16),
        ],
        in_specs=[smem, smem] + [hbm] * 9,
        out_specs=[hbm, pl.BlockSpec(memory_space=pltpu.VMEM)],
        scratch_shapes=[
            pltpu.VMEM((4, 4, size, width), bf16),
            pltpu.VMEM((ctx, own_in, width), bf16),
            pltpu.VMEM((ctx * own_in, width), bf16),
            pltpu.VMEM((4, 4, own_in, width), bf16),
            pltpu.VMEM((width, width), f32),
            pltpu.SemaphoreType.DMA((9,)),
        ],
        compiler_params=pltpu.CompilerParams(vmem_limit_bytes=vmem_limit),
        cost_estimate=cost(4),
        name="sum_heads",
    )(role, near, *parts, acts)


def exchange(packed):
    return lax.all_to_all(packed, "ctx", split_axis=0, concat_axis=0, tiled=True)


def gather(array):
    return lax.all_gather(array, "ctx", axis=0, tiled=False)


def flip(array, mask, ctx):
    return lax.ppermute(array, "ctx", [(j, j ^ mask) for j in range(ctx)])


def spread_z(array, z_here, ctx):
    held = [array] + [flip(array, 4 * k, ctx) for k in (1, 2, 3)]
    odd, high = (z_here & 1) == 1, z_here >= 2
    first = [jnp.where(odd, held[k ^ 1], held[k]) for k in range(4)]
    return jnp.stack([jnp.where(high, first[k ^ 2], first[k]) for k in range(4)])


def both_sides(held, other, mask, ctx_index):
    upper = (ctx_index & mask) != 0
    return jnp.stack([jnp.where(upper, other, held), jnp.where(upper, held, other)])


def gather_start(piece_for, z_here, ctx):
    own = piece_for(z_here)
    far = [flip(piece_for(z_here ^ k), 4 * k, ctx) for k in (1, 2, 3)]
    return own, far, [flip(own, mask, ctx) for mask in (2, 1)]


def gather_finish(started, ctx):
    own, far, own_sides = started
    far = jnp.stack(far)
    far_sides = [flip(far, mask, ctx) for mask in (2, 1)]
    across = tuple(flip(part, 1, ctx) for part in (own_sides[0], far_sides[0]))
    columns = [(own, far), (own_sides[0], far_sides[0]), (own_sides[1], far_sides[1]), across]
    for mask in [1 << n for n in range(4, ctx.bit_length() - 1)]:
        columns = columns + [tuple(flip(part, mask, ctx) for part in column) for column in columns]
    return columns


def column_at(mask):
    high = mask >> 4
    return ((mask >> 1) & 1) + 2 * (mask & 1) + 4 * high


def body(
    ctx,
    tokens,
    cotangent,
    block_order,
    input_weight,
    output_weight,
    expand_weight,
    reduce_weight,
    vectors,
    input_moment,
    output_moment,
    expand_moment,
    reduce_moment,
    vector_first,
    vector_second,
):
    seqs, local, width = tokens.shape
    rows = seqs * local
    length = ctx * local
    hd = width // HEADS
    layers = 2
    own_in = input_weight.shape[2]
    own_mix = output_weight.shape[2]
    own_ff = expand_weight.shape[2]
    own_vec = vectors.shape[1]
    dp_index = lax.axis_index("dp")
    ctx_index = lax.axis_index("ctx")
    owner_first = dp_index == 0

    ring_rows = 688

    def sections(parts):
        at, pieces, used = {}, [], 0
        for name, array in parts:
            size = array.shape[0]
            aligned = size % 16 == 0 and not name.startswith("old")
            start = -(-used // size) * size if aligned else used
            pieces.append(jnp.pad(array, ((start - used, 0), (0, 0))))
            at[name], used = start, start + size
        goal = -(-used // 16) * 16
        if ctx == 16 and goal > 512:
            goal = max(goal, ring_rows)
        pieces.append(jnp.zeros((goal - used, width), bf16))
        return jnp.concatenate(pieces, axis=0), at

    x_own = tokens.reshape(rows, width)
    cot = cotangent.reshape(rows, width)
    vec_row = jnp.pad(vectors.astype(bf16), ((0, 15), (0, width - own_vec)))
    pack = jnp.concatenate(
        [
            expand_weight[0].T.astype(bf16),
            reduce_weight[0].astype(bf16),
            output_weight[0].T.astype(bf16),
            input_weight[0].T.astype(bf16),
            vec_row,
        ],
        axis=0,
    )
    pack_other = lax.ppermute(pack, "dp", [(0, 1), (1, 0)])
    cuts = (own_ff, 2 * own_ff, 2 * own_ff + own_mix, 2 * own_ff + own_mix + own_in)
    own_parts = []
    for l in range(layers):
        mine = jnp.where(owner_first, (pack, pack_other)[l], (pack_other, pack)[l])
        own_parts.append(jnp.split(mine, cuts))
    pack_first, at_first = sections(
        [
            ("fc", own_parts[0][0]),
            ("red", own_parts[0][1]),
            ("tokens", x_own),
            ("vec", jnp.concatenate([own_parts[l][4][:8] for l in range(layers)], axis=0)),
            ("mix", own_parts[0][2]),
            ("in", own_parts[0][3]),
            ("next", own_parts[1][3]),
        ]
    )
    pack_second, at_second = sections(
        [
            ("fc", own_parts[1][0]),
            ("red", own_parts[1][1]),
            ("cot", cot),
            ("mix", own_parts[1][2]),
        ]
    )
    all_first, all_second = gather(pack_first), gather(pack_second)
    weights = (all_first, all_second)
    places = (at_first, at_second)
    in_at = (at_first["in"], at_first["next"])
    vecs = [
        all_first[:, at_first["vec"] + 8 * l, :own_vec].reshape(-1, width).astype(f32)
        for l in range(layers)
    ]

    block_len = length // block_order.shape[0]
    positions = (
        block_order[:, None] * block_len + jnp.arange(block_len, dtype=jnp.int32)[None, :]
    ).reshape(length)
    qpos = positions[:, None]
    kpos = positions[None, :]

    head = jnp.minimum(ctx_index, HEADS - 1)
    head_bias = jnp.concatenate(
        [
            lax.dynamic_slice_in_dim(vecs[0][2], head * hd, hd),
            jnp.zeros((hd,), f32),
            lax.dynamic_slice_in_dim(vecs[0][3], head * hd, hd),
        ]
    )
    stream = x_own
    saved = []
    for l in range(layers):
        if l == 0:
            a, qkv = head_qkv(
                head[None], all_first, at_first["tokens"], vecs[0], head_bias[None],
                all_first, at_first["in"], own_in, rows,
            )
        else:
            a, qkv_pack = qkv_forward(stream, vecs[l], all_first, in_at[l], own_in, local)
            qkv = exchange(qkv_pack).reshape(length, 6 * hd)
        out_full, out_low, prob = attn_forward(qkv, qpos, kpos)
        o_pack = exchange(out_low.reshape(ctx, local, 2 * hd))
        mid, c, hidden, fresh = mlp_forward(
            o_pack, stream, vecs[l], weights[l], places[l], own_ff, own_mix
        )
        saved.append((stream, a, qkv, out_full, out_low, prob, mid, c, hidden))
        stream = fresh
    block_output = stream.reshape(seqs, local, width)

    bias = [
        lax.dynamic_slice_in_dim(vecs[l][PIECES:].reshape(-1), ctx_index * own_ff, own_ff)[:, None]
        for l in range(layers)
    ]

    role = (ctx_index // 4) % 4

    grad = cot
    kept = [None, None]
    vec_grads = [None, None]
    for l in (1, 0):
        x, a, qkv, out_full, out_low, prob, mid, c, hidden = saved[l]
        gz, gmid, gy, go_pack, vg_late = mlp_backward(
            grad, mid, hidden, vecs[l], weights[l], places[l], own_ff, own_mix
        )
        if l == 1:
            pack_acts, at_acts = sections(
                [
                    ("c", saved[0][7]),
                    ("next_a", saved[1][1]),
                    ("next_c", saved[1][7]),
                    ("next_gy", gy),
                    ("old_in", input_moment[0].T.astype(bf16)),
                    ("old_mix", output_moment[0].T.astype(bf16)),
                ]
            )
            acts = gather(pack_acts)
        if l == 0:
            gz_held = spread_z(gz, role, ctx)
        go = exchange(go_pack).reshape(length, 2 * hd)
        dqkv = attn_backward(qkv, go, out_full, prob)
        if l == 0:
            dqkv, gz_held = lax.optimization_barrier((dqkv, gz_held))
            gz_other = flip(gz_held, 2, ctx)
        dqkv_own = exchange(dqkv.reshape(ctx, local, 6 * hd))
        if l == 0:
            g_head = [
                head_grads(dqkv, saved[0][1], 0, rows),
                head_grads(kept[1][2], acts, at_acts["next_a"], rows),
                head_grads(saved[1][4], acts, at_acts["next_gy"], rows),
            ]
            g_hidden_second = hidden_grads(
                acts, at_acts["next_c"], all_second, at_second["cot"],
                *own_parts[1][:2], bias[1], rows,
            )
            ready = hidden_ready(acts, at_acts["c"], own_parts[0][0], bias[0], rows)
            dqkv_own, g_head, ready, g_hidden_second, gz_other = lax.optimization_barrier(
                (dqkv_own, g_head, ready, g_hidden_second, gz_other)
            )
            gz_held = both_sides(gz_held, gz_other, 2, ctx_index)
            for mask in [1] + [1 << n for n in range(4, ctx.bit_length() - 1)]:
                gz_held = both_sides(gz_held, flip(gz_held, mask, ctx), mask, ctx_index)
            gz_all = gz_held.reshape(ctx // 4, 4 * rows, width)
        gin, vg_early = qkv_backward(dqkv_own, x, gmid, vecs[l], all_first, in_at[l], own_in)
        vec_grads[l] = jnp.concatenate([vg_early[:4], vg_late], axis=0)
        kept[l] = (gz, gy, dqkv)
        grad = gin
    input_grad = grad.reshape(seqs, local, width)

    gy_all = gather(kept[0][1])

    def owned(first, second):
        given = jnp.where(owner_first, second, first).astype(bf16)
        taken = lax.ppermute(given, "dp", [(0, 1), (1, 0)]).astype(f32)
        return jnp.where(owner_first, first, second) + taken

    g_in_head = owned(g_head[0], g_head[1]).astype(bf16)
    hidden_second = jnp.concatenate(g_hidden_second, axis=0)
    old_hidden = jnp.concatenate([expand_moment[0].T, reduce_moment[0]], axis=0)
    vec_terms = jnp.stack(vec_grads).reshape(layers, ctx, own_vec).swapaxes(0, 1)
    gz_all, input_grad, hidden_second, old_hidden, g_in_head, vec_terms, ready, g_head = (
        lax.optimization_barrier(
            (gz_all, input_grad, hidden_second, old_hidden, g_in_head, vec_terms, ready, g_head)
        )
    )
    hidden_first = jnp.concatenate(
        hidden_last(acts, at_acts["c"], gz_all, *ready, own_parts[0][1], rows), axis=0
    )
    vec_terms, hidden_first = lax.optimization_barrier((vec_terms, hidden_first))
    vec_sums = jnp.sum(exchange(vec_terms), axis=0)
    moved = muon_moment * old_hidden + owned(hidden_first, hidden_second)
    m_fc = moved[:own_ff].T
    m_red = moved[own_ff:]

    big = max(own_ff, 3 * hd)

    def padded(piece):
        return jnp.pad(piece.astype(bf16), ((0, big - piece.shape[0]), (0, 0)))

    g_mix_first = head_grads(saved[0][4], gy_all, 0, rows)
    g_mix_head = owned(g_mix_first, g_head[2])
    pieces = (g_in_head, padded(moved[:own_ff]), padded(m_red), padded(g_mix_head))

    def piece_for(z):
        low = jnp.where(z == 0, pieces[0], pieces[1])
        return jnp.where(z < 2, low, jnp.where(z == 2, pieces[2], pieces[3]))

    started, vec_sums = lax.optimization_barrier((gather_start(piece_for, role, ctx), vec_sums))
    columns = gather_finish(started, ctx)

    groups = ctx // 4
    near = ctx_index % 4
    masks = [m for m in range(ctx) if m & 12 == 0]
    order = sorted(masks, key=column_at)

    def absolute(array, size):
        mine = (ctx_index // 16) * 4 + near
        spots = jnp.array([column_at(((n >> 2) << 4) | (n & 3)) for n in range(groups)])
        listed = jnp.stack(
            [
                lax.dynamic_index_in_dim(array, spots[n ^ mine], 0, keepdims=False)[:, :size]
                for n in range(groups)
            ]
        )
        listed = listed.reshape(ctx // 16, 4, 4, size, width).swapaxes(1, 2)
        return listed.reshape(ctx, size, width)

    def relative(array):
        size = array.shape[1]
        split = array.reshape(ctx // 16, 4, 4, size, width).swapaxes(1, 2)
        split = split.reshape(groups, 4, size, width)
        mine = (ctx_index // 16) * 4 + near
        spread = jnp.stack(
            [
                lax.dynamic_index_in_dim(
                    split, mine ^ (((m >> 4) << 2) | (m & 3)), 0, keepdims=False
                )
                for m in order
            ]
        )
        return spread

    old_at = at_acts["old_in"]
    if ctx == 16 and own_in % 16 == 0 and own_mix % 16 == 0:
        sums, fresh = sum_heads(role[None], near[None], columns, acts, old_at, own_in, own_mix)
    else:
        old = acts[:, old_at : old_at + own_in + own_mix].astype(f32)

        def joined(parts):
            return jnp.stack([jnp.concatenate([own[None], far]) for own, far in parts])

        new_in = absolute(joined(columns), 3 * hd)[:HEADS].reshape(HEADS, 3, hd, width)
        new_in = new_in.swapaxes(0, 1).reshape(ctx, own_in, width)
        sum_in = relative((muon_moment * old[:, :own_in] + new_in.astype(f32)).astype(bf16))
        new_mix = absolute(joined(columns)[:, ::-1], hd)[:HEADS].reshape(width, width)
        new_mix = new_mix.T.reshape(ctx, own_mix, width)
        sum_mix = relative((muon_moment * old[:, own_in:] + new_mix.astype(f32)).astype(bf16))
        sum_mix = jnp.pad(sum_mix[:, ::-1].reshape(width, width), ((0, 2 * width), (0, 0)))
        sums = jnp.where(role == 3, sum_mix, sum_in.reshape(3 * width, width))
        new_mix = jnp.pad(relative(new_mix)[0, ::-1], ((0, 0), (0, own_in - own_mix), (0, 0)))
        fresh = jnp.where(role == 3, new_mix, relative(new_in)[0])

    taken = [fresh[0]]
    for k in (1, 2, 3):
        pairs = [(j, j ^ (4 * k)) for j in range(ctx) if (j // 4) % 4 in (0, 3)]
        taken.append(lax.ppermute(fresh[k], "ctx", pairs))
    direction = orthogonal(
        role[None],
        [(own[:own_ff], far[:, :own_ff]) for own, far in columns],
        sums,
        (own_in, own_ff, own_mix),
    )
    direction, taken, vec_sums = lax.optimization_barrier((direction, taken, vec_sums))
    vec_given = jnp.where(owner_first, vec_sums[1], vec_sums[0])
    vec_kept = jnp.where(owner_first, vec_sums[0], vec_sums[1])
    vec_grad = (vec_kept + lax.ppermute(vec_given, "dp", [(0, 1), (1, 0)]))[None]
    direction = direction.reshape(4, own_ff, width)
    by_distance = [direction[0]] + [flip(direction[k], 4 * k, ctx) for k in (1, 2, 3)]

    def from_role(by_distance, wanted):
        result = by_distance[wanted]
        for k in range(4):
            if k != wanted:
                result = jnp.where(role == wanted ^ k, by_distance[k], result)
        return result

    m_in = muon_moment * input_moment[0] + from_role(taken, 0).astype(f32).T
    m_mix = muon_moment * output_moment[0] + from_role(taken, 3)[:own_mix].astype(f32).T

    got = [from_role(by_distance, wanted) for wanted in range(4)]
    steps = (
        got[0][:own_in].astype(f32).T,
        got[3][:own_mix].astype(f32).T,
        got[1].astype(f32).T,
        got[2].astype(f32),
    )
    hidden_units = ctx * own_ff
    largest = (3 * width, width, hidden_units, hidden_units)
    old_weights = (input_weight, output_weight, expand_weight, reduce_weight)
    new_weights = [
        old_weights[kind] * (1.0 - muon_rate * muon_decay)
        - muon_rate * 0.2 * math.sqrt(largest[kind]) * steps[kind][None]
        for kind in range(4)
    ]

    new_vector_first = beta_first * vector_first + (1.0 - beta_first) * vec_grad
    new_vector_second = beta_second * vector_second + (1.0 - beta_second) * vec_grad * vec_grad
    corr_first = 1.0 - beta_first**STEP
    corr_second = 1.0 - beta_second**STEP
    new_vectors = vectors - adam_rate * (new_vector_first / corr_first) / (
        jnp.sqrt(new_vector_second / corr_second) + adam_epsilon
    )
    return (
        block_output,
        input_grad,
        new_weights[0],
        new_weights[1],
        new_weights[2],
        new_weights[3],
        m_in[None],
        m_mix[None],
        m_fc[None],
        m_red[None],
        new_vectors,
        new_vector_first,
        new_vector_second,
    )


def solution(mesh):
    return jax.shard_map(
        functools.partial(body, mesh.shape["ctx"]),
        mesh=mesh,
        in_specs=(
            P("dp", "ctx", None),
            P("dp", "ctx", None),
            P(),
            P("dp", None, "ctx"),
            P("dp", None, "ctx"),
            P("dp", None, "ctx"),
            P("dp", "ctx", None),
            P("dp", "ctx"),
            P("dp", None, "ctx"),
            P("dp", None, "ctx"),
            P("dp", None, "ctx"),
            P("dp", "ctx", None),
            P("dp", "ctx"),
            P("dp", "ctx"),
        ),
        out_specs=(
            P("dp", "ctx", None),
            P("dp", "ctx", None),
            P("dp", None, "ctx"),
            P("dp", None, "ctx"),
            P("dp", None, "ctx"),
            P("dp", "ctx", None),
            P("dp", None, "ctx"),
            P("dp", None, "ctx"),
            P("dp", None, "ctx"),
            P("dp", "ctx", None),
            P("dp", "ctx"),
            P("dp", "ctx"),
            P("dp", "ctx"),
        ),
        check_vma=False,
    )
```

```python
import functools
import math

import jax
import jax.numpy as jnp
from jax import lax
from jax.experimental import pallas as pl
from jax.experimental.pallas import tpu as pltpu
from jax.sharding import PartitionSpec as P

HEADS = 12
NS_STEPS = 5
STEP = 10
PIECES = 8

norm_epsilon = 1e-05
neg_large = -1e30
score_scale = 0.125
coef_first = 3.4445
coef_second = -4.775
coef_third = 2.0315
ortho_epsilon = 1e-07
muon_rate = 0.15
muon_moment = 0.95
muon_decay = 0.01
adam_rate = 0.3
beta_first = 0.9
beta_second = 0.95
adam_epsilon = 1e-08
gelu_inner = 0.7978845608
gelu_cubic = 0.044715
shifts = (0.0, 0.0, 0.17, 1.0, 0.8)

f32 = jnp.float32
bf16 = jnp.bfloat16
vmem_limit = 56 * 1024 * 1024


def mm(left, right):
    return jnp.dot(left, right, preferred_element_type=f32)


def mm_nt(left, right):
    return lax.dot_general(left, right, (((1,), (1,)), ((), ())), preferred_element_type=f32)


def mm_tn(left, right):
    return lax.dot_general(left, right, (((0,), (0,)), ((), ())), preferred_element_type=f32)


def cost(micros):
    return pl.CostEstimate(
        flops=int(micros * 1e9), bytes_accessed=int(micros * 1e6), transcendentals=0
    )


def params(grid_dims):
    return pltpu.CompilerParams(
        dimension_semantics=("arbitrary",) * grid_dims, vmem_limit_bytes=vmem_limit
    )


def normalized(values_in):
    centred = values_in - jnp.mean(values_in, axis=-1, keepdims=True)
    inv_std = lax.rsqrt(jnp.mean(centred * centred, axis=-1, keepdims=True) + norm_epsilon)
    return centred * inv_std, inv_std


def norm_backward(grad_out, normed, inv_std, gain):
    scaled = grad_out * gain
    return inv_std * (
        scaled
        - jnp.mean(scaled, axis=-1, keepdims=True)
        - normed * jnp.mean(scaled * normed, axis=-1, keepdims=True)
    )


def pair_lanes(values_in, local, start, size):
    return jnp.concatenate(
        [values_in[:local, start : start + size], values_in[local:, start : start + size]], axis=1
    )


def join_heads(ref, local, hd):
    rows = []
    for s in range(2):
        rows.append(
            jnp.concatenate(
                [ref[h][:, s * hd : (s + 1) * hd].astype(f32) for h in range(HEADS)], axis=1
            )
        )
    return jnp.concatenate(rows, axis=0)


def qkv_kernel(x_ref, vec_ref, w_ref, a_ref, out_ref, proj_ref):
    step = pl.program_id(0)
    steps, _, chunk = proj_ref.shape
    local = out_ref.shape[1]
    hd = out_ref.shape[2] // 6
    width = x_ref.shape[1]

    @pl.when(step == 0)
    def _():
        normed, _ = normalized(x_ref[...].astype(f32))
        a_ref[...] = (normed * vec_ref[0:1, :] + vec_ref[1:2, :]).astype(bf16)

    proj_ref[step] = mm_nt(a_ref[...], w_ref[...].reshape(chunk, width))

    @pl.when(step == steps - 1)
    def _():
        proj = jnp.concatenate([proj_ref[i] for i in range(steps)], axis=1)
        bias = (vec_ref[2:3, :], jnp.zeros((1, width), f32), vec_ref[3:4, :])
        for part in range(3):
            piece = proj[:, part * width : (part + 1) * width] + bias[part]
            for h in range(HEADS):
                out_ref[h, :, part * 2 * hd : (part + 1) * 2 * hd] = pair_lanes(
                    piece, local, h * hd, hd
                ).astype(bf16)
        for h in range(HEADS, out_ref.shape[0]):
            out_ref[h] = jnp.zeros(out_ref.shape[1:], bf16)


def shard_blocks(array, start, own, steps):
    ctx, _, width = array.shape
    group = ctx // steps
    if own % 16 == 0 and start % own == 0:
        return array, pl.BlockSpec(
            (group, own, width), lambda i: (i if steps > 1 else 0, start // own, 0)
        )
    part = array[:, start : start + own].reshape(steps, group * own, width)
    return part, pl.BlockSpec((1, group * own, width), lambda i: (i if steps > 1 else 0, 0, 0))


def qkv_forward(x, vec, weights, at, own_in, local):
    rows, width = x.shape
    ctx = weights.shape[0]
    hd = width // HEADS
    steps = 4
    w_array, w_spec = shard_blocks(weights, at, own_in, steps)
    whole = lambda i: (0, 0)
    return pl.pallas_call(
        qkv_kernel,
        grid=(steps,),
        in_specs=[
            pl.BlockSpec((rows, width), whole),
            pl.BlockSpec(vec.shape, whole),
            w_spec,
        ],
        out_specs=[
            pl.BlockSpec((rows, width), whole),
            pl.BlockSpec((ctx, local, 6 * hd), lambda i: (0, 0, 0)),
        ],
        out_shape=[
            jax.ShapeDtypeStruct((rows, width), bf16),
            jax.ShapeDtypeStruct((ctx, local, 6 * hd), bf16),
        ],
        scratch_shapes=[pltpu.VMEM((steps, rows, 3 * width // steps), f32)],
        compiler_params=params(1),
        cost_estimate=cost(5),
        name="qkv_forward",
    )(x, vec, w_array)


def head_qkv_kernel(head_ref, x_ref, vec_ref, bias_ref, w_ref, a_ref, out_ref, w_all_ref, own_ref):
    shards, rows, width = x_ref.shape
    local = rows // 2
    hd = out_ref.shape[1] // 6

    @pl.when(pl.program_id(0) == 0)
    def _():
        w_all_ref[...] = w_ref[...].reshape(w_all_ref.shape)
        for part in range(3):
            first = pl.multiple_of(part * width + head_ref[0] * hd, hd)
            own_ref[part * hd : (part + 1) * hd, :] = w_all_ref[pl.ds(first, hd), :]

    normed, _ = normalized(x_ref[...].reshape(shards * rows, width).astype(f32))
    first_in = (normed * vec_ref[0:1, :] + vec_ref[1:2, :]).astype(bf16)
    a_ref[...] = first_in.reshape(shards, rows, width)
    proj = (mm_nt(first_in, own_ref[...]) + bias_ref[...]).reshape(shards, 2, local, 3 * hd)
    sides = [proj[:, s].reshape(shards * local, 3 * hd) for s in range(2)]
    for part in range(3):
        cut = slice(part * hd, (part + 1) * hd)
        out_ref[:, 2 * part * hd : 2 * (part + 1) * hd] = jnp.concatenate(
            [sides[0][:, cut], sides[1][:, cut]], axis=1
        ).astype(bf16)


def head_qkv(head, tokens_all, tokens_at, vec, bias, weights, at, own_in, rows):
    ctx, _, width = tokens_all.shape
    hd = width // HEADS
    local = rows // 2
    x_array, x_spec = shard_blocks(tokens_all, tokens_at, rows, ctx // 4)
    w_array, w_spec = shard_blocks(weights, at, own_in, 1)
    whole = lambda i: (0, 0)
    return pl.pallas_call(
        head_qkv_kernel,
        grid=(ctx // 4,),
        in_specs=[
            pl.BlockSpec(memory_space=pltpu.SMEM),
            x_spec,
            pl.BlockSpec(vec.shape, whole),
            pl.BlockSpec(bias.shape, whole),
            w_spec,
        ],
        out_specs=[
            pl.BlockSpec((4, rows, width), lambda i: (i, 0, 0)),
            pl.BlockSpec((4 * local, 6 * hd), lambda i: (i, 0)),
        ],
        out_shape=[
            jax.ShapeDtypeStruct((ctx, rows, width), bf16),
            jax.ShapeDtypeStruct((ctx * local, 6 * hd), bf16),
        ],
        scratch_shapes=[pltpu.VMEM((3 * width, width), bf16), pltpu.VMEM((3 * hd, width), bf16)],
        compiler_params=params(1),
        cost_estimate=cost(6),
        name="head_qkv",
    )(head, x_array, vec, bias, w_array)


def lane_masks(rows, lanes):
    lane = lax.broadcasted_iota(jnp.int32, (rows, lanes), 1)
    first = jnp.where(lane < lanes // 2, 1.0, 0.0)
    return first.astype(bf16), (1.0 - first).astype(bf16)


def attn_fwd_kernel(qpos_ref, kpos_ref, q_ref, k_ref, v_ref, of_ref, ob_ref, p_ref):
    allowed = kpos_ref[...] <= qpos_ref[...]
    q_masks = lane_masks(*q_ref.shape)
    v_masks = lane_masks(*v_ref.shape)
    out = jnp.zeros(of_ref.shape, f32)
    for s in range(2):
        scores = mm_nt(q_ref[...] * q_masks[s], k_ref[...]) * score_scale
        scores = jnp.where(allowed, scores, neg_large)
        expo = jnp.exp(scores - jnp.max(scores, axis=-1, keepdims=True))
        prob = (expo * (1.0 / jnp.sum(expo, axis=-1, keepdims=True))).astype(bf16)
        p_ref[s] = prob
        out = out + mm(prob, v_ref[...] * v_masks[s])
    of_ref[...] = out
    ob_ref[...] = out.astype(bf16)


def attn_forward(qkv, qpos, kpos):
    length, lanes = qkv.shape
    pair = lanes // 3
    tile = min(256, length)
    return pl.pallas_call(
        attn_fwd_kernel,
        grid=(length // tile,),
        in_specs=[
            pl.BlockSpec((tile, 1), lambda i: (i, 0)),
            pl.BlockSpec((1, length), lambda i: (0, 0)),
            pl.BlockSpec((tile, pair), lambda i: (i, 0)),
            pl.BlockSpec((length, pair), lambda i: (0, 1)),
            pl.BlockSpec((length, pair), lambda i: (0, 2)),
        ],
        out_specs=[
            pl.BlockSpec((tile, pair), lambda i: (i, 0)),
            pl.BlockSpec((tile, pair), lambda i: (i, 0)),
            pl.BlockSpec((2, tile, length), lambda i: (0, i, 0)),
        ],
        out_shape=[
            jax.ShapeDtypeStruct((length, pair), f32),
            jax.ShapeDtypeStruct((length, pair), bf16),
            jax.ShapeDtypeStruct((2, length, length), bf16),
        ],
        compiler_params=params(1),
        cost_estimate=cost(8),
        name="attn_forward",
    )(qpos, kpos, qkv, qkv, qkv)


def attn_bwd_kernel(q_ref, go_ref, of_ref, p_ref, k_ref, v_ref, out_ref, dk_ref, dv_ref):
    step = pl.program_id(0)
    tile, pair = q_ref.shape
    masks = lane_masks(tile, pair)
    k_masks = lane_masks(*k_ref.shape)

    @pl.when(step == 0)
    def _():
        dk_ref[...] = jnp.zeros_like(dk_ref)
        dv_ref[...] = jnp.zeros_like(dv_ref)

    dq = jnp.zeros((tile, pair), f32)
    for s in range(2):
        go = go_ref[...] * masks[s]
        row_dot = jnp.sum(go.astype(f32) * of_ref[...], axis=-1, keepdims=True)
        prob = p_ref[s]
        grad_prob = mm_nt(go, v_ref[...])
        ds = (prob.astype(f32) * (grad_prob - row_dot)).astype(bf16)
        dv_ref[...] += mm_tn(go, prob)
        dk_ref[...] += mm_tn(q_ref[...] * masks[s], ds)
        dq = dq + mm(ds, k_ref[...] * k_masks[s])
    out_ref[pl.ds(pl.multiple_of(step * tile, tile), tile), 0:pair] = (dq * score_scale).astype(bf16)

    @pl.when(step == pl.num_programs(0) - 1)
    def _():
        out_ref[:, pair : 2 * pair] = (dk_ref[...].T * score_scale).astype(bf16)
        out_ref[:, 2 * pair :] = dv_ref[...].T.astype(bf16)


def attn_backward(qkv, go, out_full, prob):
    length, lanes = qkv.shape
    pair = lanes // 3
    tile = min(256, length)
    return pl.pallas_call(
        attn_bwd_kernel,
        grid=(length // tile,),
        in_specs=[
            pl.BlockSpec((tile, pair), lambda i: (i, 0)),
            pl.BlockSpec((tile, pair), lambda i: (i, 0)),
            pl.BlockSpec((tile, pair), lambda i: (i, 0)),
            pl.BlockSpec((2, tile, length), lambda i: (0, i, 0)),
            pl.BlockSpec((length, pair), lambda i: (0, 1)),
            pl.BlockSpec((length, pair), lambda i: (0, 2)),
        ],
        out_specs=pl.BlockSpec((length, lanes), lambda i: (0, 0)),
        out_shape=jax.ShapeDtypeStruct((length, lanes), bf16),
        scratch_shapes=[pltpu.VMEM((pair, length), f32), pltpu.VMEM((pair, length), f32)],
        compiler_params=params(1),
        cost_estimate=cost(8),
        name="attn_backward",
    )(qkv, go, out_full, prob, qkv, qkv)


def mlp_fwd_kernel(o_ref, x_ref, vec_ref, mix_ref, fc_ref, red_ref, mid_ref, c_ref, h_ref, out_ref):
    step = pl.program_id(0)
    rows, width = x_ref.shape

    @pl.when(step == 0)
    def _():
        mixed = join_heads(o_ref, rows // 2, o_ref.shape[2] // 2).astype(bf16)
        mix_w = mix_ref[...].reshape(width, width)
        middle = x_ref[...].astype(f32) + (mm_nt(mixed, mix_w) + vec_ref[4:5, :])
        mid_ref[...] = middle
        normed, _ = normalized(middle)
        c_ref[...] = (normed * vec_ref[5:6, :] + vec_ref[6:7, :]).astype(bf16)
        out_ref[...] = middle + vec_ref[7:8, :]

    hidden = mm_nt(c_ref[...], fc_ref[...].reshape(width, width))
    hidden = hidden + vec_ref[pl.ds(PIECES + step, 1), :]
    h_ref[...] = hidden
    inner = jnp.tanh(gelu_inner * (hidden + gelu_cubic * hidden * hidden * hidden))
    active = (0.5 * hidden * (1.0 + inner)).astype(bf16)
    out_ref[...] += mm(active, red_ref[...].reshape(width, width))


def mlp_forward(o_pack, x, vec, weights, at, own_ff, own_mix):
    rows, width = x.shape
    hidden = weights.shape[0] * own_ff
    steps = hidden // width
    fc_array, fc_spec = shard_blocks(weights, at["fc"], own_ff, steps)
    red_array, red_spec = shard_blocks(weights, at["red"], own_ff, steps)
    mix_array, mix_spec = shard_blocks(weights, at["mix"], own_mix, 1)
    whole = lambda i: (0, 0)
    return pl.pallas_call(
        mlp_fwd_kernel,
        grid=(steps,),
        in_specs=[
            pl.BlockSpec(o_pack.shape, lambda i: (0, 0, 0)),
            pl.BlockSpec((rows, width), whole),
            pl.BlockSpec(vec.shape, whole),
            mix_spec,
            fc_spec,
            red_spec,
        ],
        out_specs=[
            pl.BlockSpec((rows, width), whole),
            pl.BlockSpec((rows, width), whole),
            pl.BlockSpec((rows, width), lambda i: (0, i)),
            pl.BlockSpec((rows, width), whole),
        ],
        out_shape=[
            jax.ShapeDtypeStruct((rows, width), f32),
            jax.ShapeDtypeStruct((rows, width), bf16),
            jax.ShapeDtypeStruct((rows, hidden), f32),
            jax.ShapeDtypeStruct((rows, width), f32),
        ],
        compiler_params=params(1),
        cost_estimate=cost(8),
        name="mlp_forward",
    )(o_pack, x, vec, mix_array, fc_array, red_array)


def gelu_slope(hidden):
    square = hidden * hidden
    inner = jnp.tanh(gelu_inner * (hidden + gelu_cubic * hidden * square))
    slope = 0.5 * (1.0 + inner) + (0.5 * gelu_inner) * hidden * (1.0 - inner * inner) * (
        1.0 + (3.0 * gelu_cubic) * square
    )
    return inner, slope


def mlp_bwd_kernel(
    gr_ref, mid_ref, h_ref, vec_ref, mix_ref, fc_ref, red_ref,
    gz_ref, gmid_ref, gy_ref, go_ref, vg_ref, gc_ref,
):
    step = pl.program_id(0)
    rows, width = gr_ref.shape

    @pl.when(step == 0)
    def _():
        gz_ref[...] = gr_ref[...].astype(bf16)
        gc_ref[...] = jnp.zeros_like(gc_ref)

    _, slope = gelu_slope(h_ref[...])
    grad_hidden = (mm_nt(gz_ref[...], red_ref[...].reshape(width, width)) * slope).astype(bf16)
    vg_ref[pl.ds(4 + step, 1), :] = jnp.sum(grad_hidden.astype(f32), axis=0, keepdims=True)
    gc_ref[...] += mm(grad_hidden, fc_ref[...].reshape(width, width))

    @pl.when(step == pl.num_programs(0) - 1)
    def _():
        grad = gr_ref[...].astype(f32)
        normed, inv_std = normalized(mid_ref[...])
        grad_second = gc_ref[...]
        grad_mid = grad + norm_backward(grad_second, normed, inv_std, vec_ref[5:6, :])
        gmid_ref[...] = grad_mid
        gy = grad_mid.astype(bf16)
        gy_ref[...] = gy
        vg_ref[0:1, :] = jnp.sum(gy.astype(f32), axis=0, keepdims=True)
        vg_ref[1:2, :] = jnp.sum(grad_second * normed, axis=0, keepdims=True)
        vg_ref[2:3, :] = jnp.sum(grad_second, axis=0, keepdims=True)
        vg_ref[3:4, :] = jnp.sum(gz_ref[...].astype(f32), axis=0, keepdims=True)
        grad_attn = mm(gy, mix_ref[...].reshape(width, width))
        hd = go_ref.shape[2] // 2
        for h in range(HEADS):
            go_ref[h] = pair_lanes(grad_attn, rows // 2, h * hd, hd).astype(bf16)
        for h in range(HEADS, go_ref.shape[0]):
            go_ref[h] = jnp.zeros(go_ref.shape[1:], bf16)


def mlp_backward(gr, mid, hidden, vec, weights, at, own_ff, own_mix):
    rows, width = mid.shape
    ctx = weights.shape[0]
    steps = hidden.shape[1] // width
    hd = width // HEADS
    fc_array, fc_spec = shard_blocks(weights, at["fc"], own_ff, steps)
    red_array, red_spec = shard_blocks(weights, at["red"], own_ff, steps)
    mix_array, mix_spec = shard_blocks(weights, at["mix"], own_mix, 1)
    whole = lambda i: (0, 0)
    return pl.pallas_call(
        mlp_bwd_kernel,
        grid=(steps,),
        in_specs=[
            pl.BlockSpec((rows, width), whole),
            pl.BlockSpec((rows, width), whole),
            pl.BlockSpec((rows, width), lambda i: (0, i)),
            pl.BlockSpec(vec.shape, whole),
            mix_spec,
            fc_spec,
            red_spec,
        ],
        out_specs=[
            pl.BlockSpec((rows, width), whole),
            pl.BlockSpec((rows, width), whole),
            pl.BlockSpec((rows, width), whole),
            pl.BlockSpec((ctx, rows // 2, 2 * hd), lambda i: (0, 0, 0)),
            pl.BlockSpec((PIECES, width), whole),
        ],
        out_shape=[
            jax.ShapeDtypeStruct((rows, width), bf16),
            jax.ShapeDtypeStruct((rows, width), f32),
            jax.ShapeDtypeStruct((rows, width), bf16),
            jax.ShapeDtypeStruct((ctx, rows // 2, 2 * hd), bf16),
            jax.ShapeDtypeStruct((PIECES, width), f32),
        ],
        scratch_shapes=[pltpu.VMEM((rows, width), f32)],
        compiler_params=params(1),
        cost_estimate=cost(8),
        name="mlp_backward",
    )(gr, mid, hidden, vec, mix_array, fc_array, red_array)


def qkv_bwd_kernel(d_ref, x_ref, gmid_ref, vec_ref, w_ref, gin_ref, vg_ref, d_all_ref, ga_ref):
    step = pl.program_id(0)
    steps, rows, chunk = d_all_ref.shape
    width = x_ref.shape[1]

    @pl.when(step == 0)
    def _():
        hd = d_ref.shape[2] // 6
        parts = []
        for part in range(3):
            for s in range(2):
                start = (2 * part + s) * hd
                parts.append(
                    jnp.concatenate(
                        [d_ref[h, :, start : start + hd].astype(f32) for h in range(HEADS)], axis=1
                    )
                )
        joined = jnp.concatenate(
            [jnp.concatenate([parts[2 * part], parts[2 * part + 1]], axis=0) for part in range(3)],
            axis=1,
        )
        vg_ref[...] = jnp.zeros_like(vg_ref)
        vg_ref[2:3, :] = jnp.sum(joined[:, :width], axis=0, keepdims=True)
        vg_ref[3:4, :] = jnp.sum(joined[:, 2 * width :], axis=0, keepdims=True)
        for i in range(steps):
            d_all_ref[i] = joined[:, i * chunk : (i + 1) * chunk].astype(bf16)
        ga_ref[...] = jnp.zeros_like(ga_ref)

    ga_ref[...] += mm(d_all_ref[step], w_ref[...].reshape(chunk, width))

    @pl.when(step == steps - 1)
    def _():
        normed, inv_std = normalized(x_ref[...].astype(f32))
        grad_first = ga_ref[...]
        gin_ref[...] = gmid_ref[...] + norm_backward(grad_first, normed, inv_std, vec_ref[0:1, :])
        vg_ref[0:1, :] = jnp.sum(grad_first * normed, axis=0, keepdims=True)
        vg_ref[1:2, :] = jnp.sum(grad_first, axis=0, keepdims=True)


def qkv_backward(dqkv, x, gmid, vec, weights, at, own_in):
    rows, width = x.shape
    steps = 4
    w_array, w_spec = shard_blocks(weights, at, own_in, steps)
    whole = lambda i: (0, 0)
    return pl.pallas_call(
        qkv_bwd_kernel,
        grid=(steps,),
        in_specs=[
            pl.BlockSpec(dqkv.shape, lambda i: (0, 0, 0)),
            pl.BlockSpec((rows, width), whole),
            pl.BlockSpec((rows, width), whole),
            pl.BlockSpec(vec.shape, whole),
            w_spec,
        ],
        out_specs=[
            pl.BlockSpec((rows, width), whole),
            pl.BlockSpec((PIECES, width), whole),
        ],
        out_shape=[
            jax.ShapeDtypeStruct((rows, width), f32),
            jax.ShapeDtypeStruct((PIECES, width), f32),
        ],
        scratch_shapes=[
            pltpu.VMEM((steps, rows, 3 * width // steps), bf16),
            pltpu.VMEM((rows, width), f32),
        ],
        compiler_params=params(1),
        cost_estimate=cost(5),
        name="qkv_backward",
    )(dqkv, x, gmid, vec, w_array)


def hidden_grads_kernel(c_ref, gz_ref, fc_ref, red_ref, bias_ref, gfc_ref, gred_ref):
    own, width = gfc_ref.shape
    second = c_ref[...].reshape(-1, width)
    branch = gz_ref[...].reshape(-1, width)
    hidden = mm_nt(fc_ref[...], second) + bias_ref[...]
    inner, slope = gelu_slope(hidden)
    active = (0.5 * hidden * (1.0 + inner)).astype(bf16)
    grad_hidden = (mm_nt(red_ref[...], branch) * slope).astype(bf16)

    @pl.when(pl.program_id(0) == 0)
    def _():
        gfc_ref[...] = jnp.zeros_like(gfc_ref)
        gred_ref[...] = jnp.zeros_like(gred_ref)

    gfc_ref[...] += mm(grad_hidden, second)
    gred_ref[...] += mm(active, branch)


def hidden_grads(c_all, c_at, gz_all, gz_at, fc_own, red_own, bias, rows):
    ctx, _, width = c_all.shape
    own_ff = fc_own.shape[0]
    steps = ctx // 4
    c_array, c_spec = shard_blocks(c_all, c_at, rows, steps)
    gz_array, gz_spec = shard_blocks(gz_all, gz_at, rows, steps)
    whole = lambda i: (0, 0)
    return pl.pallas_call(
        hidden_grads_kernel,
        grid=(steps,),
        in_specs=[
            c_spec,
            gz_spec,
            pl.BlockSpec((own_ff, width), whole),
            pl.BlockSpec((own_ff, width), whole),
            pl.BlockSpec((own_ff, 1), whole),
        ],
        out_specs=[pl.BlockSpec((own_ff, width), whole)] * 2,
        out_shape=[jax.ShapeDtypeStruct((own_ff, width), f32)] * 2,
        compiler_params=params(1),
        cost_estimate=cost(1),
        name="hidden_grads",
    )(c_array, gz_array, fc_own, red_own, bias)


def hidden_ready_kernel(c_ref, fc_ref, bias_ref, u_ref, slope_ref):
    width = fc_ref.shape[1]
    hidden = mm_nt(fc_ref[...], c_ref[...].reshape(-1, width)) + bias_ref[...]
    inner, slope = gelu_slope(hidden)
    u_ref[...] = (0.5 * hidden * (1.0 + inner)).astype(bf16)
    slope_ref[...] = slope


def rows_by_z(c_all, c_at, rows):
    ctx, _, width = c_all.shape
    assert c_at % rows == 0
    view = c_all.reshape(ctx // 16, 4, 4, *c_all.shape[1:])
    return view, pl.BlockSpec(
        (1, 4, 1, rows, width),
        lambda i: (i // 4, 0, (i % 2) * 2 + (i // 2) % 2, c_at // rows, 0),
    )


def hidden_ready(c_all, c_at, fc_own, bias, rows):
    ctx, _, width = c_all.shape
    own_ff = fc_own.shape[0]
    c_array, c_spec = rows_by_z(c_all, c_at, rows)
    whole = lambda i: (0, 0)
    return pl.pallas_call(
        hidden_ready_kernel,
        grid=(ctx // 4,),
        in_specs=[
            c_spec,
            pl.BlockSpec((own_ff, width), whole),
            pl.BlockSpec((own_ff, 1), whole),
        ],
        out_specs=[pl.BlockSpec((own_ff, 4 * rows), lambda i: (0, i))] * 2,
        out_shape=[
            jax.ShapeDtypeStruct((own_ff, ctx * rows), bf16),
            jax.ShapeDtypeStruct((own_ff, ctx * rows), f32),
        ],
        compiler_params=params(1),
        cost_estimate=cost(1),
        name="hidden_ready",
    )(c_array, fc_own, bias)


def hidden_last_kernel(c_ref, gz_ref, u_ref, slope_ref, red_ref, gfc_ref, gred_ref):
    width = red_ref.shape[1]
    second = c_ref[...].reshape(-1, width)
    branch = gz_ref[...].reshape(-1, width)
    grad_hidden = (mm_nt(red_ref[...], branch) * slope_ref[...]).astype(bf16)

    @pl.when(pl.program_id(0) == 0)
    def _():
        gfc_ref[...] = jnp.zeros_like(gfc_ref)
        gred_ref[...] = jnp.zeros_like(gred_ref)

    gred_ref[...] += mm(u_ref[...], branch)
    gfc_ref[...] += mm(grad_hidden, second)


def hidden_last(c_all, c_at, gz_all, active, slope, red_own, rows):
    steps, _, width = gz_all.shape
    own_ff = red_own.shape[0]
    c_array, c_spec = rows_by_z(c_all, c_at, rows)
    whole = lambda i: (0, 0)
    return pl.pallas_call(
        hidden_last_kernel,
        grid=(steps,),
        in_specs=[
            c_spec,
            pl.BlockSpec((1, 4 * rows, width), lambda i: (i, 0, 0)),
            pl.BlockSpec((own_ff, 4 * rows), lambda i: (0, i)),
            pl.BlockSpec((own_ff, 4 * rows), lambda i: (0, i)),
            pl.BlockSpec((own_ff, width), whole),
        ],
        out_specs=[pl.BlockSpec((own_ff, width), whole)] * 2,
        out_shape=[jax.ShapeDtypeStruct((own_ff, width), f32)] * 2,
        compiler_params=params(1),
        cost_estimate=cost(1),
        name="hidden_last",
    )(c_array, gz_all, active, slope, red_own)


def head_grads_kernel(pack_ref, rows_ref, out_ref):
    length, lanes = pack_ref.shape
    _, rows, width = rows_ref.shape
    local = rows // 2
    hd = width // HEADS
    for s in range(2):
        piece = rows_ref[:, s * local : (s + 1) * local, :].reshape(length, width)
        result = mm_tn(pack_ref[...], piece)
        for part in range(out_ref.shape[0] // hd):
            start = (2 * part + s) * hd
            if s == 0:
                out_ref[part * hd : (part + 1) * hd, :] = result[start : start + hd]
            else:
                out_ref[part * hd : (part + 1) * hd, :] += result[start : start + hd]


def head_grads(pack, rows_all, at, rows):
    length, lanes = pack.shape
    ctx, _, width = rows_all.shape
    rows_array, rows_spec = shard_blocks(rows_all, at, rows, 1)
    return pl.pallas_call(
        head_grads_kernel,
        grid=(1,),
        in_specs=[
            pl.BlockSpec((length, lanes), lambda i: (0, 0)),
            rows_spec,
        ],
        out_specs=pl.BlockSpec((lanes // 2, width), lambda i: (0, 0)),
        out_shape=jax.ShapeDtypeStruct((lanes // 2, width), f32),
        compiler_params=params(1),
        cost_estimate=cost(1),
        name="head_grads",
    )(pack, rows_array)


def copy_all(moves, sems):
    copies = [pltpu.make_async_copy(src, dst, sems.at[i]) for i, (src, dst) in enumerate(moves)]
    for copy in copies:
        copy.start()
    for copy in copies:
        copy.wait()


def ns_kernel(own, parts_count, role_ref, *refs):
    parts, (sums_ref, out_ref) = refs[:parts_count], refs[parts_count : parts_count + 2]
    y_ref, full_ref, low_ref, gram_ref, poly_ref, sems = refs[parts_count + 2 :]
    length, side = y_ref.shape
    own_in, own_ff, own_mix = own
    tile = 256
    role = role_ref[0]
    is_in, is_mix = role == 0, role == 3
    is_long = (role == 1) | (role == 2)
    kinds = ((is_long, length, own_ff), (is_in, 3 * side, own_in), (is_mix, side, own_mix))
    chunks = jnp.where(is_mix, 1, jnp.where(is_in, 3, length // side))

    @pl.when(is_long)
    def _():
        moves, start = [], 0
        for part in parts:
            moves.append((part, y_ref.at[start : start + part.shape[0]]))
            start += part.shape[0]
        copy_all(moves, sems)

    @pl.when(is_in)
    def _():
        copy_all([(sums_ref, y_ref.at[: 3 * side])], sems)

    @pl.when(is_mix)
    def _():
        copy_all([(sums_ref.at[:side], y_ref.at[:side])], sems)

    eye = jnp.where(
        lax.broadcasted_iota(jnp.int32, (side, side), 0)
        == lax.broadcasted_iota(jnp.int32, (side, side), 1),
        1.0,
        0.0,
    )

    def each_chunk(work):
        def one(i, carry):
            work(pl.ds(pl.multiple_of(i * side, side), side))
            return carry

        lax.fori_loop(0, chunks, one, 0)

    def gram():
        for kind, columns, _ in kinds:

            @pl.when(kind)
            def _():
                for i in range(side // tile):
                    rows = slice(i * tile, (i + 1) * tile)
                    gram_ref[rows, i * tile :] = mm_nt(
                        low_ref[rows, :columns], low_ref[i * tile :, :columns]
                    )

        for i in range(side // tile):
            for j in range(i + 1, side // tile):
                gram_ref[j * tile : (j + 1) * tile, i * tile : (i + 1) * tile] = gram_ref[
                    i * tile : (i + 1) * tile, j * tile : (j + 1) * tile
                ].T

    def load(cols):
        low_ref[:, cols] = y_ref[cols, :].T

    each_chunk(load)
    gram()
    scale = 1.0 / (jnp.sqrt(jnp.sum(gram_ref[...] * eye, keepdims=True)) + ortho_epsilon)
    gram_ref[...] = gram_ref[...] * (scale * scale)

    linear_only = coef_second * gram_ref[...]
    low_gram = gram_ref[...].astype(bf16)
    poly_ref[...] = (scale * (linear_only + coef_third * mm(low_gram, low_gram))).astype(bf16)

    def first(cols):
        matrix = low_ref[:, cols]
        fresh = (coef_first * scale) * matrix.astype(f32) + mm(poly_ref[...], matrix)
        full_ref[:, cols] = fresh
        low_ref[:, cols] = fresh.astype(bf16)

    each_chunk(first)
    gram()

    def polynomial(k):
        shift = jnp.float32(shifts[1])
        for number in range(2, NS_STEPS):
            shift = jnp.where(k == number, shifts[number], shift)
        linear = coef_second + 2.0 * coef_third * shift
        diff = gram_ref[...] - shift * eye
        low_diff = diff.astype(bf16)
        poly_ref[...] = (linear * diff + coef_third * mm(low_diff, low_diff)).astype(bf16)
        return coef_first + coef_second * shift + coef_third * shift * shift

    def sweep(k, carry):
        base = polynomial(k)

        def update(cols):
            fresh = base * full_ref[:, cols] + mm(poly_ref[...], low_ref[:, cols])
            full_ref[:, cols] = fresh
            low_ref[:, cols] = fresh.astype(bf16)

        each_chunk(update)
        gram()
        return carry

    lax.fori_loop(1, NS_STEPS - 1, sweep, 0)
    base = polynomial(NS_STEPS - 1)
    wanted = -(-4 * own_ff // tile) * tile
    fresh = base * full_ref[:, :wanted] + mm(poly_ref[...], low_ref[:, :wanted])
    gram_ref[:wanted, :] = fresh.T
    for kind, _, size in kinds:

        @pl.when(kind)
        def _():
            for k in range(4):
                piece = gram_ref[k * size : (k + 1) * size, :].astype(bf16)
                if size < own_ff:
                    piece = jnp.concatenate(
                        [piece, jnp.zeros((own_ff - size, side), bf16)], axis=0
                    )
                out_ref[k * own_ff : (k + 1) * own_ff, :] = piece


def orthogonal(role, columns, sums, own):
    width = sums.shape[1]
    parts = [part.reshape(-1, width) for column in columns for part in column]
    length = sum(part.shape[0] for part in parts)
    return pl.pallas_call(
        functools.partial(ns_kernel, own, len(parts)),
        out_shape=jax.ShapeDtypeStruct((4 * own[1], width), bf16),
        in_specs=[pl.BlockSpec(memory_space=pltpu.SMEM)]
        + [pl.BlockSpec(memory_space=pl.ANY)] * (len(parts) + 1),
        out_specs=pl.BlockSpec(memory_space=pltpu.VMEM),
        scratch_shapes=[
            pltpu.VMEM((length, width), bf16),
            pltpu.VMEM((width, length), f32),
            pltpu.VMEM((width, length), bf16),
            pltpu.VMEM((width, width), f32),
            pltpu.VMEM((width, width), bf16),
            pltpu.SemaphoreType.DMA((len(parts),)),
        ],
        compiler_params=pltpu.CompilerParams(vmem_limit_bytes=vmem_limit),
        cost_estimate=cost(46),
        name="newton_schulz",
    )(role, *parts, sums)


def column_place(mask):
    return ((mask >> 1) & 1) + 2 * (mask & 1)


def sum_heads_kernel(own_mix, old_at, role_ref, near_ref, *refs):
    parts, (acts_ref, y_out_ref, fresh_ref) = refs[:8], refs[8:11]
    held_ref, old_ref, y_ref, natural_ref, turned_ref, sems = refs[11:]
    width = held_ref.shape[3]
    own_in = fresh_ref.shape[1]
    hd = width // HEADS
    block = 16
    place = [column_place(near_ref[0] ^ n) for n in range(4)]

    def fetch(size, at, own):
        moves = [(acts_ref.at[:, at : at + own], old_ref.at[:, :own])]
        for c in range(4):
            moves.append((parts[2 * c].at[:size], held_ref.at[c, 0, :size]))
            moves.append((parts[2 * c + 1].at[:, :size], held_ref.at[c, 1:, :size]))
        copy_all(moves, sems)

    @pl.when(role_ref[0] == 0)
    def _():
        fetch(3 * hd, old_at, own_in)
        for z in range(4):
            for n in range(4):
                for start in range(0, own_in, block):
                    first = (4 * z + n) * own_in + start
                    part, rest = divmod(first, width)
                    h, off = divmod(rest, hd)
                    at = part * hd + off
                    source = held_ref[place[h & 3], h >> 2, at : at + block, :]
                    natural_ref[place[n], z, start : start + block, :] = source
                    old = old_ref[4 * z + n, start : start + block, :]
                    y_ref[pl.ds((place[n] * 4 + z) * own_in + start, block), :] = (
                        muon_moment * old.astype(f32) + source.astype(f32)
                    ).astype(bf16)
        fresh_ref[...] = natural_ref[0]
        copy_all([(y_ref, y_out_ref)], sems)

    @pl.when(role_ref[0] == 3)
    def _():
        fetch(hd, old_at + own_in, own_mix)
        for h in range(HEADS):
            turned_ref[h * hd : (h + 1) * hd, :] = held_ref[
                place[h & 3], 3 ^ (h >> 2), :hd
            ].astype(f32)
        turned_ref[...] = turned_ref[...].T
        fresh_ref[...] = jnp.zeros_like(fresh_ref)
        for z in range(4):
            for n in range(4):
                first = (4 * z + n) * own_mix
                source = turned_ref[first : first + own_mix, :]
                natural_ref[place[n], 3 ^ z, :own_mix] = source.astype(bf16)
                old = old_ref[4 * z + n, :own_mix]
                y_ref[pl.ds((place[n] * 4 + (3 ^ z)) * own_mix, own_mix), :] = (
                    muon_moment * old.astype(f32) + source
                ).astype(bf16)
        fresh_ref[:, :own_mix] = natural_ref[0, :, :own_mix]
        copy_all([(y_ref.at[:width], y_out_ref.at[:width])], sems)

    @pl.when((role_ref[0] == 1) | (role_ref[0] == 2))
    def _():
        fresh_ref[...] = jnp.zeros_like(fresh_ref)


def sum_heads(role, near, columns, acts, old_at, own_in, own_mix):
    ctx, _, width = acts.shape
    parts = [part for column in columns for part in column]
    size = parts[0].shape[0]
    smem = pl.BlockSpec(memory_space=pltpu.SMEM)
    hbm = pl.BlockSpec(memory_space=pl.ANY)
    return pl.pallas_call(
        functools.partial(sum_heads_kernel, own_mix, old_at),
        out_shape=[
            jax.ShapeDtypeStruct((ctx * own_in, width), bf16),
            jax.ShapeDtypeStruct((4, own_in, width), bf16),
        ],
        in_specs=[smem, smem] + [hbm] * 9,
        out_specs=[hbm, pl.BlockSpec(memory_space=pltpu.VMEM)],
        scratch_shapes=[
            pltpu.VMEM((4, 4, size, width), bf16),
            pltpu.VMEM((ctx, own_in, width), bf16),
            pltpu.VMEM((ctx * own_in, width), bf16),
            pltpu.VMEM((4, 4, own_in, width), bf16),
            pltpu.VMEM((width, width), f32),
            pltpu.SemaphoreType.DMA((9,)),
        ],
        compiler_params=pltpu.CompilerParams(vmem_limit_bytes=vmem_limit),
        cost_estimate=cost(4),
        name="sum_heads",
    )(role, near, *parts, acts)


def exchange(packed):
    return lax.all_to_all(packed, "ctx", split_axis=0, concat_axis=0, tiled=True)


def gather(array):
    return lax.all_gather(array, "ctx", axis=0, tiled=False)


def flip(array, mask, ctx):
    return lax.ppermute(array, "ctx", [(j, j ^ mask) for j in range(ctx)])


def spread_z(array, z_here, ctx):
    held = [array] + [flip(array, 4 * k, ctx) for k in (1, 2, 3)]
    odd, high = (z_here & 1) == 1, z_here >= 2
    first = [jnp.where(odd, held[k ^ 1], held[k]) for k in range(4)]
    return jnp.stack([jnp.where(high, first[k ^ 2], first[k]) for k in range(4)])


def both_sides(held, other, mask, ctx_index):
    upper = (ctx_index & mask) != 0
    return jnp.stack([jnp.where(upper, other, held), jnp.where(upper, held, other)])


def gather_start(piece_for, z_here, ctx):
    own = piece_for(z_here)
    far = [flip(piece_for(z_here ^ k), 4 * k, ctx) for k in (1, 2, 3)]
    return own, far, [flip(own, mask, ctx) for mask in (2, 1)]


def gather_finish(started, ctx):
    own, far, own_sides = started
    far = jnp.stack(far)
    far_sides = [flip(far, mask, ctx) for mask in (2, 1)]
    across = tuple(flip(part, 1, ctx) for part in (own_sides[0], far_sides[0]))
    columns = [(own, far), (own_sides[0], far_sides[0]), (own_sides[1], far_sides[1]), across]
    for mask in [1 << n for n in range(4, ctx.bit_length() - 1)]:
        columns = columns + [tuple(flip(part, mask, ctx) for part in column) for column in columns]
    return columns


def column_at(mask):
    high = mask >> 4
    return ((mask >> 1) & 1) + 2 * (mask & 1) + 4 * high


def body(
    ctx,
    tokens,
    cotangent,
    block_order,
    input_weight,
    output_weight,
    expand_weight,
    reduce_weight,
    vectors,
    input_moment,
    output_moment,
    expand_moment,
    reduce_moment,
    vector_first,
    vector_second,
):
    seqs, local, width = tokens.shape
    rows = seqs * local
    length = ctx * local
    hd = width // HEADS
    layers = 2
    own_in = input_weight.shape[2]
    own_mix = output_weight.shape[2]
    own_ff = expand_weight.shape[2]
    own_vec = vectors.shape[1]
    dp_index = lax.axis_index("dp")
    ctx_index = lax.axis_index("ctx")
    owner_first = dp_index == 0

    ring_rows = 688

    def sections(parts):
        at, pieces, used = {}, [], 0
        for name, array in parts:
            size = array.shape[0]
            aligned = size % 16 == 0 and not name.startswith("old")
            start = -(-used // size) * size if aligned else used
            pieces.append(jnp.pad(array, ((start - used, 0), (0, 0))))
            at[name], used = start, start + size
        goal = -(-used // 16) * 16
        if ctx == 16 and goal > 512:
            goal = max(goal, ring_rows)
        pieces.append(jnp.zeros((goal - used, width), bf16))
        return jnp.concatenate(pieces, axis=0), at

    x_own = tokens.reshape(rows, width)
    cot = cotangent.reshape(rows, width)
    vec_row = jnp.pad(vectors.astype(bf16), ((0, 15), (0, width - own_vec)))
    pack = jnp.concatenate(
        [
            expand_weight[0].T.astype(bf16),
            reduce_weight[0].astype(bf16),
            output_weight[0].T.astype(bf16),
            input_weight[0].T.astype(bf16),
            vec_row,
        ],
        axis=0,
    )
    pack_other = lax.ppermute(pack, "dp", [(0, 1), (1, 0)])
    cuts = (own_ff, 2 * own_ff, 2 * own_ff + own_mix, 2 * own_ff + own_mix + own_in)
    own_parts = []
    for l in range(layers):
        mine = jnp.where(owner_first, (pack, pack_other)[l], (pack_other, pack)[l])
        own_parts.append(jnp.split(mine, cuts))
    pack_first, at_first = sections(
        [
            ("fc", own_parts[0][0]),
            ("red", own_parts[0][1]),
            ("tokens", x_own),
            ("vec", jnp.concatenate([own_parts[l][4][:8] for l in range(layers)], axis=0)),
            ("mix", own_parts[0][2]),
            ("in", own_parts[0][3]),
            ("next", own_parts[1][3]),
        ]
    )
    pack_second, at_second = sections(
        [
            ("fc", own_parts[1][0]),
            ("red", own_parts[1][1]),
            ("cot", cot),
            ("mix", own_parts[1][2]),
        ]
    )
    all_first, all_second = gather(pack_first), gather(pack_second)
    weights = (all_first, all_second)
    places = (at_first, at_second)
    in_at = (at_first["in"], at_first["next"])
    vecs = [
        all_first[:, at_first["vec"] + 8 * l, :own_vec].reshape(-1, width).astype(f32)
        for l in range(layers)
    ]

    block_len = length // block_order.shape[0]
    positions = (
        block_order[:, None] * block_len + jnp.arange(block_len, dtype=jnp.int32)[None, :]
    ).reshape(length)
    qpos = positions[:, None]
    kpos = positions[None, :]

    head = jnp.minimum(ctx_index, HEADS - 1)
    head_bias = jnp.concatenate(
        [
            lax.dynamic_slice_in_dim(vecs[0][2], head * hd, hd),
            jnp.zeros((hd,), f32),
            lax.dynamic_slice_in_dim(vecs[0][3], head * hd, hd),
        ]
    )
    stream = x_own
    saved = []
    for l in range(layers):
        if l == 0:
            a, qkv = head_qkv(
                head[None], all_first, at_first["tokens"], vecs[0], head_bias[None],
                all_first, at_first["in"], own_in, rows,
            )
        else:
            a, qkv_pack = qkv_forward(stream, vecs[l], all_first, in_at[l], own_in, local)
            qkv = exchange(qkv_pack).reshape(length, 6 * hd)
        out_full, out_low, prob = attn_forward(qkv, qpos, kpos)
        o_pack = exchange(out_low.reshape(ctx, local, 2 * hd))
        mid, c, hidden, fresh = mlp_forward(
            o_pack, stream, vecs[l], weights[l], places[l], own_ff, own_mix
        )
        saved.append((stream, a, qkv, out_full, out_low, prob, mid, c, hidden))
        stream = fresh
    block_output = stream.reshape(seqs, local, width)

    bias = [
        lax.dynamic_slice_in_dim(vecs[l][PIECES:].reshape(-1), ctx_index * own_ff, own_ff)[:, None]
        for l in range(layers)
    ]

    role = (ctx_index // 4) % 4

    grad = cot
    kept = [None, None]
    vec_grads = [None, None]
    for l in (1, 0):
        x, a, qkv, out_full, out_low, prob, mid, c, hidden = saved[l]
        gz, gmid, gy, go_pack, vg_late = mlp_backward(
            grad, mid, hidden, vecs[l], weights[l], places[l], own_ff, own_mix
        )
        if l == 1:
            pack_acts, at_acts = sections(
                [
                    ("c", saved[0][7]),
                    ("next_a", saved[1][1]),
                    ("next_c", saved[1][7]),
                    ("next_gy", gy),
                    ("old_in", input_moment[0].T.astype(bf16)),
                    ("old_mix", output_moment[0].T.astype(bf16)),
                ]
            )
            acts = gather(pack_acts)
        if l == 0:
            gz_held = spread_z(gz, role, ctx)
        go = exchange(go_pack).reshape(length, 2 * hd)
        dqkv = attn_backward(qkv, go, out_full, prob)
        if l == 0:
            dqkv, gz_held = lax.optimization_barrier((dqkv, gz_held))
            gz_other = flip(gz_held, 2, ctx)
        dqkv_own = exchange(dqkv.reshape(ctx, local, 6 * hd))
        kept[l] = (gz, gy, dqkv)
        if l == 1:
            gin, vg_early = qkv_backward(dqkv_own, x, gmid, vecs[l], all_first, in_at[l], own_in)
            vec_grads[l] = jnp.concatenate([vg_early[:4], vg_late], axis=0)
            grad = gin

    gy_all = gather(kept[0][1])
    ready = hidden_ready(acts, at_acts["c"], own_parts[0][0], bias[0], rows)
    g_in_first = head_grads(kept[0][2], saved[0][1], 0, rows)
    ready, gz_other, dqkv_own, g_in_first = lax.optimization_barrier(
        (ready, gz_other, dqkv_own, g_in_first)
    )
    gz_held = both_sides(gz_held, gz_other, 2, ctx_index)
    gz_other = flip(gz_held, 1, ctx)
    g_head = [
        g_in_first,
        head_grads(kept[1][2], acts, at_acts["next_a"], rows),
        head_grads(saved[1][4], acts, at_acts["next_gy"], rows),
    ]
    gz_other, g_head = lax.optimization_barrier((gz_other, g_head))
    gz_held = both_sides(gz_held, gz_other, 1, ctx_index)
    for bit in range(4, ctx.bit_length() - 1):
        gz_held = both_sides(gz_held, flip(gz_held, 1 << bit, ctx), 1 << bit, ctx_index)
    gz_all = gz_held.reshape(ctx // 4, 4 * rows, width)

    def owned(first, second):
        given = jnp.where(owner_first, second, first).astype(bf16)
        taken = lax.ppermute(given, "dp", [(0, 1), (1, 0)]).astype(f32)
        return jnp.where(owner_first, first, second) + taken

    g_in_head = owned(g_head[0], g_head[1]).astype(bf16)
    old_hidden = jnp.concatenate([expand_moment[0].T, reduce_moment[0]], axis=0)
    gz_all, old_hidden = lax.optimization_barrier((gz_all, old_hidden))
    hidden_first = jnp.concatenate(
        hidden_last(acts, at_acts["c"], gz_all, *ready, own_parts[0][1], rows), axis=0
    )
    hidden_first, acts = lax.optimization_barrier((hidden_first, acts))
    hidden_second = jnp.concatenate(
        hidden_grads(
            acts, at_acts["next_c"], all_second, at_second["cot"], *own_parts[1][:2], bias[1], rows
        ),
        axis=0,
    )
    gy_all, _ = lax.optimization_barrier((gy_all, hidden_second))
    moved = muon_moment * old_hidden + owned(hidden_first, hidden_second)
    moved, dqkv_own = lax.optimization_barrier((moved, dqkv_own))
    gin, vg_early = qkv_backward(dqkv_own, x, gmid, vecs[0], all_first, in_at[0], own_in)
    vec_grads[0] = jnp.concatenate([vg_early[:4], vg_late], axis=0)
    input_grad = gin.reshape(seqs, local, width)
    vec_terms = jnp.stack(vec_grads).reshape(layers, ctx, own_vec).swapaxes(0, 1)
    vec_terms = jnp.pad(vec_terms, ((0, 0), (0, 8 - layers), (0, width - own_vec)))
    m_fc = moved[:own_ff].T
    m_red = moved[own_ff:]

    big = max(own_ff, 3 * hd)

    def padded(piece):
        return jnp.pad(piece.astype(bf16), ((0, big - piece.shape[0]), (0, 0)))

    g_mix_first = head_grads(saved[0][4], gy_all, 0, rows)
    g_mix_head = owned(g_mix_first, g_head[2])
    pieces = (g_in_head, padded(moved[:own_ff]), padded(m_red), padded(g_mix_head))

    def piece_for(z):
        low = jnp.where(z == 0, pieces[0], pieces[1])
        return jnp.where(z < 2, low, jnp.where(z == 2, pieces[2], pieces[3]))

    started, vec_terms = lax.optimization_barrier((gather_start(piece_for, role, ctx), vec_terms))
    vec_sums = lax.psum_scatter(vec_terms, "ctx", scatter_dimension=0)
    columns = gather_finish(started, ctx)

    groups = ctx // 4
    near = ctx_index % 4
    masks = [m for m in range(ctx) if m & 12 == 0]
    order = sorted(masks, key=column_at)

    def absolute(array, size):
        mine = (ctx_index // 16) * 4 + near
        spots = jnp.array([column_at(((n >> 2) << 4) | (n & 3)) for n in range(groups)])
        listed = jnp.stack(
            [
                lax.dynamic_index_in_dim(array, spots[n ^ mine], 0, keepdims=False)[:, :size]
                for n in range(groups)
            ]
        )
        listed = listed.reshape(ctx // 16, 4, 4, size, width).swapaxes(1, 2)
        return listed.reshape(ctx, size, width)

    def relative(array):
        size = array.shape[1]
        split = array.reshape(ctx // 16, 4, 4, size, width).swapaxes(1, 2)
        split = split.reshape(groups, 4, size, width)
        mine = (ctx_index // 16) * 4 + near
        spread = jnp.stack(
            [
                lax.dynamic_index_in_dim(
                    split, mine ^ (((m >> 4) << 2) | (m & 3)), 0, keepdims=False
                )
                for m in order
            ]
        )
        return spread

    old_at = at_acts["old_in"]
    if ctx == 16 and own_in % 16 == 0 and own_mix % 16 == 0:
        sums, fresh = sum_heads(role[None], near[None], columns, acts, old_at, own_in, own_mix)
    else:
        old = acts[:, old_at : old_at + own_in + own_mix].astype(f32)

        def joined(parts):
            return jnp.stack([jnp.concatenate([own[None], far]) for own, far in parts])

        new_in = absolute(joined(columns), 3 * hd)[:HEADS].reshape(HEADS, 3, hd, width)
        new_in = new_in.swapaxes(0, 1).reshape(ctx, own_in, width)
        sum_in = relative((muon_moment * old[:, :own_in] + new_in.astype(f32)).astype(bf16))
        new_mix = absolute(joined(columns)[:, ::-1], hd)[:HEADS].reshape(width, width)
        new_mix = new_mix.T.reshape(ctx, own_mix, width)
        sum_mix = relative((muon_moment * old[:, own_in:] + new_mix.astype(f32)).astype(bf16))
        sum_mix = jnp.pad(sum_mix[:, ::-1].reshape(width, width), ((0, 2 * width), (0, 0)))
        sums = jnp.where(role == 3, sum_mix, sum_in.reshape(3 * width, width))
        new_mix = jnp.pad(relative(new_mix)[0, ::-1], ((0, 0), (0, own_in - own_mix), (0, 0)))
        fresh = jnp.where(role == 3, new_mix, relative(new_in)[0])

    taken = [fresh[0]]
    for k in (1, 2, 3):
        pairs = [(j, j ^ (4 * k)) for j in range(ctx) if (j // 4) % 4 in (0, 3)]
        taken.append(lax.ppermute(fresh[k], "ctx", pairs))
    direction = orthogonal(
        role[None],
        [(own[:own_ff], far[:, :own_ff]) for own, far in columns],
        sums,
        (own_in, own_ff, own_mix),
    )
    direction, taken, vec_sums = lax.optimization_barrier((direction, taken, vec_sums))
    vec_sums = vec_sums[:layers, :own_vec]
    vec_given = jnp.where(owner_first, vec_sums[1], vec_sums[0])
    vec_kept = jnp.where(owner_first, vec_sums[0], vec_sums[1])
    vec_grad = (vec_kept + lax.ppermute(vec_given, "dp", [(0, 1), (1, 0)]))[None]
    direction = direction.reshape(4, own_ff, width)
    by_distance = [direction[0]] + [flip(direction[k], 4 * k, ctx) for k in (1, 2, 3)]

    def from_role(by_distance, wanted):
        result = by_distance[wanted]
        for k in range(4):
            if k != wanted:
                result = jnp.where(role == wanted ^ k, by_distance[k], result)
        return result

    m_in = muon_moment * input_moment[0] + from_role(taken, 0).astype(f32).T
    m_mix = muon_moment * output_moment[0] + from_role(taken, 3)[:own_mix].astype(f32).T

    got = [from_role(by_distance, wanted) for wanted in range(4)]
    steps = (
        got[0][:own_in].astype(f32).T,
        got[3][:own_mix].astype(f32).T,
        got[1].astype(f32).T,
        got[2].astype(f32),
    )
    hidden_units = ctx * own_ff
    largest = (3 * width, width, hidden_units, hidden_units)
    old_weights = (input_weight, output_weight, expand_weight, reduce_weight)
    new_weights = [
        old_weights[kind] * (1.0 - muon_rate * muon_decay)
        - muon_rate * 0.2 * math.sqrt(largest[kind]) * steps[kind][None]
        for kind in range(4)
    ]

    new_vector_first = beta_first * vector_first + (1.0 - beta_first) * vec_grad
    new_vector_second = beta_second * vector_second + (1.0 - beta_second) * vec_grad * vec_grad
    corr_first = 1.0 - beta_first**STEP
    corr_second = 1.0 - beta_second**STEP
    new_vectors = vectors - adam_rate * (new_vector_first / corr_first) / (
        jnp.sqrt(new_vector_second / corr_second) + adam_epsilon
    )
    return (
        block_output,
        input_grad,
        new_weights[0],
        new_weights[1],
        new_weights[2],
        new_weights[3],
        m_in[None],
        m_mix[None],
        m_fc[None],
        m_red[None],
        new_vectors,
        new_vector_first,
        new_vector_second,
    )


def solution(mesh):
    return jax.shard_map(
        functools.partial(body, mesh.shape["ctx"]),
        mesh=mesh,
        in_specs=(
            P("dp", "ctx", None),
            P("dp", "ctx", None),
            P(),
            P("dp", None, "ctx"),
            P("dp", None, "ctx"),
            P("dp", None, "ctx"),
            P("dp", "ctx", None),
            P("dp", "ctx"),
            P("dp", None, "ctx"),
            P("dp", None, "ctx"),
            P("dp", None, "ctx"),
            P("dp", "ctx", None),
            P("dp", "ctx"),
            P("dp", "ctx"),
        ),
        out_specs=(
            P("dp", "ctx", None),
            P("dp", "ctx", None),
            P("dp", None, "ctx"),
            P("dp", None, "ctx"),
            P("dp", None, "ctx"),
            P("dp", "ctx", None),
            P("dp", None, "ctx"),
            P("dp", None, "ctx"),
            P("dp", None, "ctx"),
            P("dp", "ctx", None),
            P("dp", "ctx"),
            P("dp", "ctx"),
            P("dp", "ctx"),
        ),
        check_vma=False,
    )
```

```python
import functools
import math

import jax
import jax.numpy as jnp
from jax import lax
from jax.experimental import pallas as pl
from jax.experimental.pallas import tpu as pltpu
from jax.sharding import PartitionSpec as P

HEADS = 12
NS_STEPS = 5
STEP = 10
PIECES = 8

norm_epsilon = 1e-05
neg_large = -1e30
score_scale = 0.125
coef_first = 3.4445
coef_second = -4.775
coef_third = 2.0315
ortho_epsilon = 1e-07
muon_rate = 0.15
muon_moment = 0.95
muon_decay = 0.01
adam_rate = 0.3
beta_first = 0.9
beta_second = 0.95
adam_epsilon = 1e-08
gelu_inner = 0.7978845608
gelu_cubic = 0.044715
shifts = (0.0, 0.0, 0.17, 1.0, 0.8)

f32 = jnp.float32
bf16 = jnp.bfloat16
vmem_limit = 56 * 1024 * 1024


def mm(left, right):
    return jnp.dot(left, right, preferred_element_type=f32)


def mm_nt(left, right):
    return lax.dot_general(left, right, (((1,), (1,)), ((), ())), preferred_element_type=f32)


def mm_tn(left, right):
    return lax.dot_general(left, right, (((0,), (0,)), ((), ())), preferred_element_type=f32)


def cost(micros):
    return pl.CostEstimate(
        flops=int(micros * 1e9), bytes_accessed=int(micros * 1e6), transcendentals=0
    )


def params(grid_dims):
    return pltpu.CompilerParams(
        dimension_semantics=("arbitrary",) * grid_dims, vmem_limit_bytes=vmem_limit
    )


def normalized(values_in):
    centred = values_in - jnp.mean(values_in, axis=-1, keepdims=True)
    inv_std = lax.rsqrt(jnp.mean(centred * centred, axis=-1, keepdims=True) + norm_epsilon)
    return centred * inv_std, inv_std


def norm_backward(grad_out, normed, inv_std, gain):
    scaled = grad_out * gain
    return inv_std * (
        scaled
        - jnp.mean(scaled, axis=-1, keepdims=True)
        - normed * jnp.mean(scaled * normed, axis=-1, keepdims=True)
    )


def pair_lanes(values_in, local, start, size):
    return jnp.concatenate(
        [values_in[:local, start : start + size], values_in[local:, start : start + size]], axis=1
    )


def join_heads(ref, local, hd):
    rows = []
    for s in range(2):
        rows.append(
            jnp.concatenate(
                [ref[h][:, s * hd : (s + 1) * hd].astype(f32) for h in range(HEADS)], axis=1
            )
        )
    return jnp.concatenate(rows, axis=0)


def qkv_kernel(x_ref, vec_ref, w_ref, a_ref, out_ref, proj_ref):
    step = pl.program_id(0)
    steps, _, chunk = proj_ref.shape
    local = out_ref.shape[1]
    hd = out_ref.shape[2] // 6
    width = x_ref.shape[1]

    @pl.when(step == 0)
    def _():
        normed, _ = normalized(x_ref[...].astype(f32))
        a_ref[...] = (normed * vec_ref[0:1, :] + vec_ref[1:2, :]).astype(bf16)

    proj_ref[step] = mm_nt(a_ref[...], w_ref[...].reshape(chunk, width))

    @pl.when(step == steps - 1)
    def _():
        proj = jnp.concatenate([proj_ref[i] for i in range(steps)], axis=1)
        bias = (vec_ref[2:3, :], jnp.zeros((1, width), f32), vec_ref[3:4, :])
        for part in range(3):
            piece = proj[:, part * width : (part + 1) * width] + bias[part]
            for h in range(HEADS):
                out_ref[h, :, part * 2 * hd : (part + 1) * 2 * hd] = pair_lanes(
                    piece, local, h * hd, hd
                ).astype(bf16)
        for h in range(HEADS, out_ref.shape[0]):
            out_ref[h] = jnp.zeros(out_ref.shape[1:], bf16)


def shard_blocks(array, start, own, steps):
    ctx, _, width = array.shape
    group = ctx // steps
    if own % 16 == 0 and start % own == 0:
        return array, pl.BlockSpec(
            (group, own, width), lambda i: (i if steps > 1 else 0, start // own, 0)
        )
    part = array[:, start : start + own].reshape(steps, group * own, width)
    return part, pl.BlockSpec((1, group * own, width), lambda i: (i if steps > 1 else 0, 0, 0))


def qkv_forward(x, vec, weights, at, own_in, local):
    rows, width = x.shape
    ctx = weights.shape[0]
    hd = width // HEADS
    steps = 4
    w_array, w_spec = shard_blocks(weights, at, own_in, steps)
    whole = lambda i: (0, 0)
    return pl.pallas_call(
        qkv_kernel,
        grid=(steps,),
        in_specs=[
            pl.BlockSpec((rows, width), whole),
            pl.BlockSpec(vec.shape, whole),
            w_spec,
        ],
        out_specs=[
            pl.BlockSpec((rows, width), whole),
            pl.BlockSpec((ctx, local, 6 * hd), lambda i: (0, 0, 0)),
        ],
        out_shape=[
            jax.ShapeDtypeStruct((rows, width), bf16),
            jax.ShapeDtypeStruct((ctx, local, 6 * hd), bf16),
        ],
        scratch_shapes=[pltpu.VMEM((steps, rows, 3 * width // steps), f32)],
        compiler_params=params(1),
        cost_estimate=cost(5),
        name="qkv_forward",
    )(x, vec, w_array)


def head_qkv_kernel(head_ref, x_ref, vec_ref, bias_ref, w_ref, a_ref, out_ref, w_all_ref, own_ref):
    shards, rows, width = x_ref.shape
    local = rows // 2
    hd = out_ref.shape[1] // 6

    @pl.when(pl.program_id(0) == 0)
    def _():
        w_all_ref[...] = w_ref[...].reshape(w_all_ref.shape)
        for part in range(3):
            first = pl.multiple_of(part * width + head_ref[0] * hd, hd)
            own_ref[part * hd : (part + 1) * hd, :] = w_all_ref[pl.ds(first, hd), :]

    normed, _ = normalized(x_ref[...].reshape(shards * rows, width).astype(f32))
    first_in = (normed * vec_ref[0:1, :] + vec_ref[1:2, :]).astype(bf16)
    a_ref[...] = first_in.reshape(shards, rows, width)
    proj = (mm_nt(first_in, own_ref[...]) + bias_ref[...]).reshape(shards, 2, local, 3 * hd)
    sides = [proj[:, s].reshape(shards * local, 3 * hd) for s in range(2)]
    for part in range(3):
        cut = slice(part * hd, (part + 1) * hd)
        out_ref[:, 2 * part * hd : 2 * (part + 1) * hd] = jnp.concatenate(
            [sides[0][:, cut], sides[1][:, cut]], axis=1
        ).astype(bf16)


def head_qkv(head, tokens_all, tokens_at, vec, bias, weights, at, own_in, rows):
    ctx, _, width = tokens_all.shape
    hd = width // HEADS
    local = rows // 2
    x_array, x_spec = shard_blocks(tokens_all, tokens_at, rows, ctx // 4)
    w_array, w_spec = shard_blocks(weights, at, own_in, 1)
    whole = lambda i: (0, 0)
    return pl.pallas_call(
        head_qkv_kernel,
        grid=(ctx // 4,),
        in_specs=[
            pl.BlockSpec(memory_space=pltpu.SMEM),
            x_spec,
            pl.BlockSpec(vec.shape, whole),
            pl.BlockSpec(bias.shape, whole),
            w_spec,
        ],
        out_specs=[
            pl.BlockSpec((4, rows, width), lambda i: (i, 0, 0)),
            pl.BlockSpec((4 * local, 6 * hd), lambda i: (i, 0)),
        ],
        out_shape=[
            jax.ShapeDtypeStruct((ctx, rows, width), bf16),
            jax.ShapeDtypeStruct((ctx * local, 6 * hd), bf16),
        ],
        scratch_shapes=[pltpu.VMEM((3 * width, width), bf16), pltpu.VMEM((3 * hd, width), bf16)],
        compiler_params=params(1),
        cost_estimate=cost(6),
        name="head_qkv",
    )(head, x_array, vec, bias, w_array)


def lane_masks(rows, lanes):
    lane = lax.broadcasted_iota(jnp.int32, (rows, lanes), 1)
    first = jnp.where(lane < lanes // 2, 1.0, 0.0)
    return first.astype(bf16), (1.0 - first).astype(bf16)


def attn_fwd_kernel(qpos_ref, kpos_ref, q_ref, k_ref, v_ref, of_ref, ob_ref, p_ref):
    allowed = kpos_ref[...] <= qpos_ref[...]
    q_masks = lane_masks(*q_ref.shape)
    v_masks = lane_masks(*v_ref.shape)
    out = jnp.zeros(of_ref.shape, f32)
    for s in range(2):
        scores = mm_nt(q_ref[...] * q_masks[s], k_ref[...]) * score_scale
        scores = jnp.where(allowed, scores, neg_large)
        expo = jnp.exp(scores - jnp.max(scores, axis=-1, keepdims=True))
        prob = (expo * (1.0 / jnp.sum(expo, axis=-1, keepdims=True))).astype(bf16)
        p_ref[s] = prob
        out = out + mm(prob, v_ref[...] * v_masks[s])
    of_ref[...] = out
    ob_ref[...] = out.astype(bf16)


def attn_forward(qkv, qpos, kpos):
    length, lanes = qkv.shape
    pair = lanes // 3
    tile = min(256, length)
    return pl.pallas_call(
        attn_fwd_kernel,
        grid=(length // tile,),
        in_specs=[
            pl.BlockSpec((tile, 1), lambda i: (i, 0)),
            pl.BlockSpec((1, length), lambda i: (0, 0)),
            pl.BlockSpec((tile, pair), lambda i: (i, 0)),
            pl.BlockSpec((length, pair), lambda i: (0, 1)),
            pl.BlockSpec((length, pair), lambda i: (0, 2)),
        ],
        out_specs=[
            pl.BlockSpec((tile, pair), lambda i: (i, 0)),
            pl.BlockSpec((tile, pair), lambda i: (i, 0)),
            pl.BlockSpec((2, tile, length), lambda i: (0, i, 0)),
        ],
        out_shape=[
            jax.ShapeDtypeStruct((length, pair), f32),
            jax.ShapeDtypeStruct((length, pair), bf16),
            jax.ShapeDtypeStruct((2, length, length), bf16),
        ],
        compiler_params=params(1),
        cost_estimate=cost(8),
        name="attn_forward",
    )(qpos, kpos, qkv, qkv, qkv)


def attn_bwd_kernel(q_ref, go_ref, of_ref, p_ref, k_ref, v_ref, out_ref, dk_ref, dv_ref):
    step = pl.program_id(0)
    tile, pair = q_ref.shape
    masks = lane_masks(tile, pair)
    k_masks = lane_masks(*k_ref.shape)

    @pl.when(step == 0)
    def _():
        dk_ref[...] = jnp.zeros_like(dk_ref)
        dv_ref[...] = jnp.zeros_like(dv_ref)

    dq = jnp.zeros((tile, pair), f32)
    for s in range(2):
        go = go_ref[...] * masks[s]
        row_dot = jnp.sum(go.astype(f32) * of_ref[...], axis=-1, keepdims=True)
        prob = p_ref[s]
        grad_prob = mm_nt(go, v_ref[...])
        ds = (prob.astype(f32) * (grad_prob - row_dot)).astype(bf16)
        dv_ref[...] += mm_tn(go, prob)
        dk_ref[...] += mm_tn(q_ref[...] * masks[s], ds)
        dq = dq + mm(ds, k_ref[...] * k_masks[s])
    out_ref[pl.ds(pl.multiple_of(step * tile, tile), tile), 0:pair] = (dq * score_scale).astype(bf16)

    @pl.when(step == pl.num_programs(0) - 1)
    def _():
        out_ref[:, pair : 2 * pair] = (dk_ref[...].T * score_scale).astype(bf16)
        out_ref[:, 2 * pair :] = dv_ref[...].T.astype(bf16)


def attn_backward(qkv, go, out_full, prob):
    length, lanes = qkv.shape
    pair = lanes // 3
    tile = min(256, length)
    return pl.pallas_call(
        attn_bwd_kernel,
        grid=(length // tile,),
        in_specs=[
            pl.BlockSpec((tile, pair), lambda i: (i, 0)),
            pl.BlockSpec((tile, pair), lambda i: (i, 0)),
            pl.BlockSpec((tile, pair), lambda i: (i, 0)),
            pl.BlockSpec((2, tile, length), lambda i: (0, i, 0)),
            pl.BlockSpec((length, pair), lambda i: (0, 1)),
            pl.BlockSpec((length, pair), lambda i: (0, 2)),
        ],
        out_specs=pl.BlockSpec((length, lanes), lambda i: (0, 0)),
        out_shape=jax.ShapeDtypeStruct((length, lanes), bf16),
        scratch_shapes=[pltpu.VMEM((pair, length), f32), pltpu.VMEM((pair, length), f32)],
        compiler_params=params(1),
        cost_estimate=cost(8),
        name="attn_backward",
    )(qkv, go, out_full, prob, qkv, qkv)


def mlp_fwd_kernel(o_ref, x_ref, vec_ref, mix_ref, fc_ref, red_ref, mid_ref, c_ref, h_ref, out_ref):
    step = pl.program_id(0)
    rows, width = x_ref.shape

    @pl.when(step == 0)
    def _():
        mixed = join_heads(o_ref, rows // 2, o_ref.shape[2] // 2).astype(bf16)
        mix_w = mix_ref[...].reshape(width, width)
        middle = x_ref[...].astype(f32) + (mm_nt(mixed, mix_w) + vec_ref[4:5, :])
        mid_ref[...] = middle
        normed, _ = normalized(middle)
        c_ref[...] = (normed * vec_ref[5:6, :] + vec_ref[6:7, :]).astype(bf16)
        out_ref[...] = middle + vec_ref[7:8, :]

    hidden = mm_nt(c_ref[...], fc_ref[...].reshape(width, width))
    hidden = hidden + vec_ref[pl.ds(PIECES + step, 1), :]
    h_ref[...] = hidden
    inner = jnp.tanh(gelu_inner * (hidden + gelu_cubic * hidden * hidden * hidden))
    active = (0.5 * hidden * (1.0 + inner)).astype(bf16)
    out_ref[...] += mm(active, red_ref[...].reshape(width, width))


def mlp_forward(o_pack, x, vec, weights, at, own_ff, own_mix):
    rows, width = x.shape
    hidden = weights.shape[0] * own_ff
    steps = hidden // width
    fc_array, fc_spec = shard_blocks(weights, at["fc"], own_ff, steps)
    red_array, red_spec = shard_blocks(weights, at["red"], own_ff, steps)
    mix_array, mix_spec = shard_blocks(weights, at["mix"], own_mix, 1)
    whole = lambda i: (0, 0)
    return pl.pallas_call(
        mlp_fwd_kernel,
        grid=(steps,),
        in_specs=[
            pl.BlockSpec(o_pack.shape, lambda i: (0, 0, 0)),
            pl.BlockSpec((rows, width), whole),
            pl.BlockSpec(vec.shape, whole),
            mix_spec,
            fc_spec,
            red_spec,
        ],
        out_specs=[
            pl.BlockSpec((rows, width), whole),
            pl.BlockSpec((rows, width), whole),
            pl.BlockSpec((rows, width), lambda i: (0, i)),
            pl.BlockSpec((rows, width), whole),
        ],
        out_shape=[
            jax.ShapeDtypeStruct((rows, width), f32),
            jax.ShapeDtypeStruct((rows, width), bf16),
            jax.ShapeDtypeStruct((rows, hidden), f32),
            jax.ShapeDtypeStruct((rows, width), f32),
        ],
        compiler_params=params(1),
        cost_estimate=cost(8),
        name="mlp_forward",
    )(o_pack, x, vec, mix_array, fc_array, red_array)


def gelu_slope(hidden):
    square = hidden * hidden
    inner = jnp.tanh(gelu_inner * (hidden + gelu_cubic * hidden * square))
    slope = 0.5 * (1.0 + inner) + (0.5 * gelu_inner) * hidden * (1.0 - inner * inner) * (
        1.0 + (3.0 * gelu_cubic) * square
    )
    return inner, slope


def mlp_bwd_kernel(
    gr_ref, mid_ref, h_ref, vec_ref, mix_ref, fc_ref, red_ref,
    gz_ref, gmid_ref, gy_ref, go_ref, vg_ref, gc_ref,
):
    step = pl.program_id(0)
    rows, width = gr_ref.shape

    @pl.when(step == 0)
    def _():
        gz_ref[...] = gr_ref[...].astype(bf16)
        gc_ref[...] = jnp.zeros_like(gc_ref)

    _, slope = gelu_slope(h_ref[...])
    grad_hidden = (mm_nt(gz_ref[...], red_ref[...].reshape(width, width)) * slope).astype(bf16)
    vg_ref[pl.ds(4 + step, 1), :] = jnp.sum(grad_hidden.astype(f32), axis=0, keepdims=True)
    gc_ref[...] += mm(grad_hidden, fc_ref[...].reshape(width, width))

    @pl.when(step == pl.num_programs(0) - 1)
    def _():
        grad = gr_ref[...].astype(f32)
        normed, inv_std = normalized(mid_ref[...])
        grad_second = gc_ref[...]
        grad_mid = grad + norm_backward(grad_second, normed, inv_std, vec_ref[5:6, :])
        gmid_ref[...] = grad_mid
        gy = grad_mid.astype(bf16)
        gy_ref[...] = gy
        vg_ref[0:1, :] = jnp.sum(gy.astype(f32), axis=0, keepdims=True)
        vg_ref[1:2, :] = jnp.sum(grad_second * normed, axis=0, keepdims=True)
        vg_ref[2:3, :] = jnp.sum(grad_second, axis=0, keepdims=True)
        vg_ref[3:4, :] = jnp.sum(gz_ref[...].astype(f32), axis=0, keepdims=True)
        grad_attn = mm(gy, mix_ref[...].reshape(width, width))
        hd = go_ref.shape[2] // 2
        for h in range(HEADS):
            go_ref[h] = pair_lanes(grad_attn, rows // 2, h * hd, hd).astype(bf16)
        for h in range(HEADS, go_ref.shape[0]):
            go_ref[h] = jnp.zeros(go_ref.shape[1:], bf16)


def mlp_backward(gr, mid, hidden, vec, weights, at, own_ff, own_mix):
    rows, width = mid.shape
    ctx = weights.shape[0]
    steps = hidden.shape[1] // width
    hd = width // HEADS
    fc_array, fc_spec = shard_blocks(weights, at["fc"], own_ff, steps)
    red_array, red_spec = shard_blocks(weights, at["red"], own_ff, steps)
    mix_array, mix_spec = shard_blocks(weights, at["mix"], own_mix, 1)
    whole = lambda i: (0, 0)
    return pl.pallas_call(
        mlp_bwd_kernel,
        grid=(steps,),
        in_specs=[
            pl.BlockSpec((rows, width), whole),
            pl.BlockSpec((rows, width), whole),
            pl.BlockSpec((rows, width), lambda i: (0, i)),
            pl.BlockSpec(vec.shape, whole),
            mix_spec,
            fc_spec,
            red_spec,
        ],
        out_specs=[
            pl.BlockSpec((rows, width), whole),
            pl.BlockSpec((rows, width), whole),
            pl.BlockSpec((rows, width), whole),
            pl.BlockSpec((ctx, rows // 2, 2 * hd), lambda i: (0, 0, 0)),
            pl.BlockSpec((PIECES, width), whole),
        ],
        out_shape=[
            jax.ShapeDtypeStruct((rows, width), bf16),
            jax.ShapeDtypeStruct((rows, width), f32),
            jax.ShapeDtypeStruct((rows, width), bf16),
            jax.ShapeDtypeStruct((ctx, rows // 2, 2 * hd), bf16),
            jax.ShapeDtypeStruct((PIECES, width), f32),
        ],
        scratch_shapes=[pltpu.VMEM((rows, width), f32)],
        compiler_params=params(1),
        cost_estimate=cost(8),
        name="mlp_backward",
    )(gr, mid, hidden, vec, mix_array, fc_array, red_array)


def qkv_bwd_kernel(d_ref, x_ref, gmid_ref, vec_ref, w_ref, gin_ref, vg_ref, d_all_ref, ga_ref):
    step = pl.program_id(0)
    steps, rows, chunk = d_all_ref.shape
    width = x_ref.shape[1]

    @pl.when(step == 0)
    def _():
        hd = d_ref.shape[2] // 6
        parts = []
        for part in range(3):
            for s in range(2):
                start = (2 * part + s) * hd
                parts.append(
                    jnp.concatenate(
                        [d_ref[h, :, start : start + hd].astype(f32) for h in range(HEADS)], axis=1
                    )
                )
        joined = jnp.concatenate(
            [jnp.concatenate([parts[2 * part], parts[2 * part + 1]], axis=0) for part in range(3)],
            axis=1,
        )
        vg_ref[...] = jnp.zeros_like(vg_ref)
        vg_ref[2:3, :] = jnp.sum(joined[:, :width], axis=0, keepdims=True)
        vg_ref[3:4, :] = jnp.sum(joined[:, 2 * width :], axis=0, keepdims=True)
        for i in range(steps):
            d_all_ref[i] = joined[:, i * chunk : (i + 1) * chunk].astype(bf16)
        ga_ref[...] = jnp.zeros_like(ga_ref)

    ga_ref[...] += mm(d_all_ref[step], w_ref[...].reshape(chunk, width))

    @pl.when(step == steps - 1)
    def _():
        normed, inv_std = normalized(x_ref[...].astype(f32))
        grad_first = ga_ref[...]
        gin_ref[...] = gmid_ref[...] + norm_backward(grad_first, normed, inv_std, vec_ref[0:1, :])
        vg_ref[0:1, :] = jnp.sum(grad_first * normed, axis=0, keepdims=True)
        vg_ref[1:2, :] = jnp.sum(grad_first, axis=0, keepdims=True)


def qkv_backward(dqkv, x, gmid, vec, weights, at, own_in):
    rows, width = x.shape
    steps = 4
    w_array, w_spec = shard_blocks(weights, at, own_in, steps)
    whole = lambda i: (0, 0)
    return pl.pallas_call(
        qkv_bwd_kernel,
        grid=(steps,),
        in_specs=[
            pl.BlockSpec(dqkv.shape, lambda i: (0, 0, 0)),
            pl.BlockSpec((rows, width), whole),
            pl.BlockSpec((rows, width), whole),
            pl.BlockSpec(vec.shape, whole),
            w_spec,
        ],
        out_specs=[
            pl.BlockSpec((rows, width), whole),
            pl.BlockSpec((PIECES, width), whole),
        ],
        out_shape=[
            jax.ShapeDtypeStruct((rows, width), f32),
            jax.ShapeDtypeStruct((PIECES, width), f32),
        ],
        scratch_shapes=[
            pltpu.VMEM((steps, rows, 3 * width // steps), bf16),
            pltpu.VMEM((rows, width), f32),
        ],
        compiler_params=params(1),
        cost_estimate=cost(5),
        name="qkv_backward",
    )(dqkv, x, gmid, vec, w_array)


def hidden_grads_kernel(c_ref, gz_ref, fc_ref, red_ref, bias_ref, gfc_ref, gred_ref):
    own, width = gfc_ref.shape
    second = c_ref[...].reshape(-1, width)
    branch = gz_ref[...].reshape(-1, width)
    hidden = mm_nt(fc_ref[...], second) + bias_ref[...]
    inner, slope = gelu_slope(hidden)
    active = (0.5 * hidden * (1.0 + inner)).astype(bf16)
    grad_hidden = (mm_nt(red_ref[...], branch) * slope).astype(bf16)

    @pl.when(pl.program_id(0) == 0)
    def _():
        gfc_ref[...] = jnp.zeros_like(gfc_ref)
        gred_ref[...] = jnp.zeros_like(gred_ref)

    gfc_ref[...] += mm(grad_hidden, second)
    gred_ref[...] += mm(active, branch)


def hidden_grads(c_all, c_at, gz_all, gz_at, fc_own, red_own, bias, rows):
    ctx, _, width = c_all.shape
    own_ff = fc_own.shape[0]
    steps = ctx // 4
    c_array, c_spec = shard_blocks(c_all, c_at, rows, steps)
    gz_array, gz_spec = shard_blocks(gz_all, gz_at, rows, steps)
    whole = lambda i: (0, 0)
    return pl.pallas_call(
        hidden_grads_kernel,
        grid=(steps,),
        in_specs=[
            c_spec,
            gz_spec,
            pl.BlockSpec((own_ff, width), whole),
            pl.BlockSpec((own_ff, width), whole),
            pl.BlockSpec((own_ff, 1), whole),
        ],
        out_specs=[pl.BlockSpec((own_ff, width), whole)] * 2,
        out_shape=[jax.ShapeDtypeStruct((own_ff, width), f32)] * 2,
        compiler_params=params(1),
        cost_estimate=cost(1),
        name="hidden_grads",
    )(c_array, gz_array, fc_own, red_own, bias)


def hidden_ready_kernel(c_ref, fc_ref, bias_ref, u_ref, slope_ref):
    width = fc_ref.shape[1]
    hidden = mm_nt(fc_ref[...], c_ref[...].reshape(-1, width)) + bias_ref[...]
    inner, slope = gelu_slope(hidden)
    u_ref[...] = (0.5 * hidden * (1.0 + inner)).astype(bf16)
    slope_ref[...] = slope


def rows_by_z(c_all, c_at, rows):
    ctx, _, width = c_all.shape
    assert c_at % rows == 0
    view = c_all.reshape(ctx // 16, 4, 4, *c_all.shape[1:])
    return view, pl.BlockSpec(
        (1, 4, 1, rows, width),
        lambda i: (i // 4, 0, (i % 2) * 2 + (i // 2) % 2, c_at // rows, 0),
    )


def hidden_ready(c_all, c_at, fc_own, bias, rows):
    ctx, _, width = c_all.shape
    own_ff = fc_own.shape[0]
    c_array, c_spec = rows_by_z(c_all, c_at, rows)
    whole = lambda i: (0, 0)
    return pl.pallas_call(
        hidden_ready_kernel,
        grid=(ctx // 4,),
        in_specs=[
            c_spec,
            pl.BlockSpec((own_ff, width), whole),
            pl.BlockSpec((own_ff, 1), whole),
        ],
        out_specs=[pl.BlockSpec((own_ff, 4 * rows), lambda i: (0, i))] * 2,
        out_shape=[
            jax.ShapeDtypeStruct((own_ff, ctx * rows), bf16),
            jax.ShapeDtypeStruct((own_ff, ctx * rows), f32),
        ],
        compiler_params=params(1),
        cost_estimate=cost(1),
        name="hidden_ready",
    )(c_array, fc_own, bias)


def hidden_last_kernel(own_ref, c_ref, u_ref, slope_ref, red_ref, *refs):
    gz_refs, (gfc_ref, gred_ref) = refs[:-2], refs[-2:]
    width = red_ref.shape[1]

    @pl.when(pl.program_id(0) == 0)
    def _():
        gfc_ref[...] = jnp.zeros_like(gfc_ref)
        gred_ref[...] = jnp.zeros_like(gred_ref)

    for step, gz_ref in enumerate(gz_refs):

        @pl.when(pl.program_id(0) == step)
        def _():
            branch = gz_ref[...]
            grad_hidden = (mm_nt(red_ref[...], branch) * slope_ref[...]).astype(bf16)
            gred_ref[...] += mm(u_ref[...], branch)
            gfc_ref[...] += mm(grad_hidden, c_ref[...].reshape(-1, width))


def hidden_last(c_all, c_at, columns, masks, ctx_index, active, slope, red_own, rows):
    width = red_own.shape[1]
    own_ff = red_own.shape[0]
    c_array, c_spec = rows_by_z(c_all, c_at, rows)

    def place(index):
        return (index >> 4) * 4 + (index & 1) * 2 + ((index >> 1) & 1)

    def block(step, own_ref):
        distance = 0
        for number, mask in enumerate(masks):
            distance = jnp.where(step == number, place(mask), distance)
        return own_ref[0] ^ distance

    whole = lambda i, own: (0, 0)
    return pl.pallas_call(
        hidden_last_kernel,
        grid_spec=pltpu.PrefetchScalarGridSpec(
            num_scalar_prefetch=1,
            grid=(len(columns),),
            in_specs=[
                pl.BlockSpec(
                    c_spec.block_shape, lambda i, own: c_spec.index_map(block(i, own))
                ),
                pl.BlockSpec((own_ff, 4 * rows), lambda i, own: (0, block(i, own))),
                pl.BlockSpec((own_ff, 4 * rows), lambda i, own: (0, block(i, own))),
                pl.BlockSpec((own_ff, width), whole),
            ]
            + [pl.BlockSpec((4 * rows, width), whole)] * len(columns),
            out_specs=[pl.BlockSpec((own_ff, width), whole)] * 2,
        ),
        out_shape=[jax.ShapeDtypeStruct((own_ff, width), f32)] * 2,
        compiler_params=params(1),
        cost_estimate=cost(1),
        name="hidden_last",
    )(place(ctx_index)[None], c_array, active, slope, red_own, *columns)


def head_grads_kernel(pack_ref, rows_ref, out_ref):
    length, lanes = pack_ref.shape
    _, rows, width = rows_ref.shape
    local = rows // 2
    hd = width // HEADS
    for s in range(2):
        piece = rows_ref[:, s * local : (s + 1) * local, :].reshape(length, width)
        result = mm_tn(pack_ref[...], piece)
        for part in range(out_ref.shape[0] // hd):
            start = (2 * part + s) * hd
            if s == 0:
                out_ref[part * hd : (part + 1) * hd, :] = result[start : start + hd]
            else:
                out_ref[part * hd : (part + 1) * hd, :] += result[start : start + hd]


def head_grads(pack, rows_all, at, rows):
    length, lanes = pack.shape
    ctx, _, width = rows_all.shape
    rows_array, rows_spec = shard_blocks(rows_all, at, rows, 1)
    return pl.pallas_call(
        head_grads_kernel,
        grid=(1,),
        in_specs=[
            pl.BlockSpec((length, lanes), lambda i: (0, 0)),
            rows_spec,
        ],
        out_specs=pl.BlockSpec((lanes // 2, width), lambda i: (0, 0)),
        out_shape=jax.ShapeDtypeStruct((lanes // 2, width), f32),
        compiler_params=params(1),
        cost_estimate=cost(1),
        name="head_grads",
    )(pack, rows_array)


def copy_all(moves, sems):
    copies = [pltpu.make_async_copy(src, dst, sems.at[i]) for i, (src, dst) in enumerate(moves)]
    for copy in copies:
        copy.start()
    for copy in copies:
        copy.wait()


def ns_kernel(own, parts_count, role_ref, *refs):
    parts, (sums_ref, out_ref) = refs[:parts_count], refs[parts_count : parts_count + 2]
    y_ref, full_ref, low_ref, gram_ref, poly_ref, sems = refs[parts_count + 2 :]
    length, side = y_ref.shape
    own_in, own_ff, own_mix = own
    tile = 256
    role = role_ref[0]
    is_in, is_mix = role == 0, role == 3
    is_long = (role == 1) | (role == 2)
    kinds = ((is_long, length, own_ff), (is_in, 3 * side, own_in), (is_mix, side, own_mix))
    chunks = jnp.where(is_mix, 1, jnp.where(is_in, 3, length // side))

    @pl.when(is_long)
    def _():
        moves, start = [], 0
        for part in parts:
            moves.append((part, y_ref.at[start : start + part.shape[0]]))
            start += part.shape[0]
        copy_all(moves, sems)

    @pl.when(is_in)
    def _():
        copy_all([(sums_ref, y_ref.at[: 3 * side])], sems)

    @pl.when(is_mix)
    def _():
        copy_all([(sums_ref.at[:side], y_ref.at[:side])], sems)

    eye = jnp.where(
        lax.broadcasted_iota(jnp.int32, (side, side), 0)
        == lax.broadcasted_iota(jnp.int32, (side, side), 1),
        1.0,
        0.0,
    )

    def each_chunk(work):
        def one(i, carry):
            work(pl.ds(pl.multiple_of(i * side, side), side))
            return carry

        lax.fori_loop(0, chunks, one, 0)

    def gram():
        for kind, columns, _ in kinds:

            @pl.when(kind)
            def _():
                for i in range(side // tile):
                    rows = slice(i * tile, (i + 1) * tile)
                    gram_ref[rows, i * tile :] = mm_nt(
                        low_ref[rows, :columns], low_ref[i * tile :, :columns]
                    )

        for i in range(side // tile):
            for j in range(i + 1, side // tile):
                gram_ref[j * tile : (j + 1) * tile, i * tile : (i + 1) * tile] = gram_ref[
                    i * tile : (i + 1) * tile, j * tile : (j + 1) * tile
                ].T

    def load(cols):
        low_ref[:, cols] = y_ref[cols, :].T

    each_chunk(load)
    gram()
    scale = 1.0 / (jnp.sqrt(jnp.sum(gram_ref[...] * eye, keepdims=True)) + ortho_epsilon)
    gram_ref[...] = gram_ref[...] * (scale * scale)

    linear_only = coef_second * gram_ref[...]
    low_gram = gram_ref[...].astype(bf16)
    poly_ref[...] = (scale * (linear_only + coef_third * mm(low_gram, low_gram))).astype(bf16)

    def first(cols):
        matrix = low_ref[:, cols]
        fresh = (coef_first * scale) * matrix.astype(f32) + mm(poly_ref[...], matrix)
        full_ref[:, cols] = fresh
        low_ref[:, cols] = fresh.astype(bf16)

    each_chunk(first)
    gram()

    def polynomial(k):
        shift = jnp.float32(shifts[1])
        for number in range(2, NS_STEPS):
            shift = jnp.where(k == number, shifts[number], shift)
        linear = coef_second + 2.0 * coef_third * shift
        diff = gram_ref[...] - shift * eye
        low_diff = diff.astype(bf16)
        poly_ref[...] = (linear * diff + coef_third * mm(low_diff, low_diff)).astype(bf16)
        return coef_first + coef_second * shift + coef_third * shift * shift

    def sweep(k, carry):
        base = polynomial(k)

        def update(cols):
            fresh = base * full_ref[:, cols] + mm(poly_ref[...], low_ref[:, cols])
            full_ref[:, cols] = fresh
            low_ref[:, cols] = fresh.astype(bf16)

        each_chunk(update)
        gram()
        return carry

    lax.fori_loop(1, NS_STEPS - 1, sweep, 0)
    base = polynomial(NS_STEPS - 1)
    wanted = -(-4 * own_ff // tile) * tile
    fresh = base * full_ref[:, :wanted] + mm(poly_ref[...], low_ref[:, :wanted])
    gram_ref[:wanted, :] = fresh.T
    for kind, _, size in kinds:

        @pl.when(kind)
        def _():
            for k in range(4):
                piece = gram_ref[k * size : (k + 1) * size, :].astype(bf16)
                if size < own_ff:
                    piece = jnp.concatenate(
                        [piece, jnp.zeros((own_ff - size, side), bf16)], axis=0
                    )
                out_ref[k * own_ff : (k + 1) * own_ff, :] = piece


def orthogonal(role, columns, sums, own):
    width = sums.shape[1]
    parts = [part.reshape(-1, width) for column in columns for part in column]
    length = sum(part.shape[0] for part in parts)
    return pl.pallas_call(
        functools.partial(ns_kernel, own, len(parts)),
        out_shape=jax.ShapeDtypeStruct((4 * own[1], width), bf16),
        in_specs=[pl.BlockSpec(memory_space=pltpu.SMEM)]
        + [pl.BlockSpec(memory_space=pl.ANY)] * (len(parts) + 1),
        out_specs=pl.BlockSpec(memory_space=pltpu.VMEM),
        scratch_shapes=[
            pltpu.VMEM((length, width), bf16),
            pltpu.VMEM((width, length), f32),
            pltpu.VMEM((width, length), bf16),
            pltpu.VMEM((width, width), f32),
            pltpu.VMEM((width, width), bf16),
            pltpu.SemaphoreType.DMA((len(parts),)),
        ],
        compiler_params=pltpu.CompilerParams(vmem_limit_bytes=vmem_limit),
        cost_estimate=cost(46),
        name="newton_schulz",
    )(role, *parts, sums)


def column_place(mask):
    return ((mask >> 1) & 1) + 2 * (mask & 1)


def sum_heads_kernel(own_mix, old_at, role_ref, near_ref, *refs):
    parts, (acts_ref, y_out_ref, fresh_ref) = refs[:8], refs[8:11]
    held_ref, old_ref, y_ref, natural_ref, turned_ref, sems = refs[11:]
    width = held_ref.shape[3]
    own_in = fresh_ref.shape[1]
    hd = width // HEADS
    block = 16
    place = [column_place(near_ref[0] ^ n) for n in range(4)]

    def fetch(size, at, own):
        moves = [(acts_ref.at[:, at : at + own], old_ref.at[:, :own])]
        for c in range(4):
            moves.append((parts[2 * c].at[:size], held_ref.at[c, 0, :size]))
            moves.append((parts[2 * c + 1].at[:, :size], held_ref.at[c, 1:, :size]))
        copy_all(moves, sems)

    @pl.when(role_ref[0] == 0)
    def _():
        fetch(3 * hd, old_at, own_in)
        for z in range(4):
            for n in range(4):
                for start in range(0, own_in, block):
                    first = (4 * z + n) * own_in + start
                    part, rest = divmod(first, width)
                    h, off = divmod(rest, hd)
                    at = part * hd + off
                    source = held_ref[place[h & 3], h >> 2, at : at + block, :]
                    natural_ref[place[n], z, start : start + block, :] = source
                    old = old_ref[4 * z + n, start : start + block, :]
                    y_ref[pl.ds((place[n] * 4 + z) * own_in + start, block), :] = (
                        muon_moment * old.astype(f32) + source.astype(f32)
                    ).astype(bf16)
        fresh_ref[...] = natural_ref[0]
        copy_all([(y_ref, y_out_ref)], sems)

    @pl.when(role_ref[0] == 3)
    def _():
        fetch(hd, old_at + own_in, own_mix)
        for h in range(HEADS):
            turned_ref[h * hd : (h + 1) * hd, :] = held_ref[
                place[h & 3], 3 ^ (h >> 2), :hd
            ].astype(f32)
        turned_ref[...] = turned_ref[...].T
        fresh_ref[...] = jnp.zeros_like(fresh_ref)
        for z in range(4):
            for n in range(4):
                first = (4 * z + n) * own_mix
                source = turned_ref[first : first + own_mix, :]
                natural_ref[place[n], 3 ^ z, :own_mix] = source.astype(bf16)
                old = old_ref[4 * z + n, :own_mix]
                y_ref[pl.ds((place[n] * 4 + (3 ^ z)) * own_mix, own_mix), :] = (
                    muon_moment * old.astype(f32) + source
                ).astype(bf16)
        fresh_ref[:, :own_mix] = natural_ref[0, :, :own_mix]
        copy_all([(y_ref.at[:width], y_out_ref.at[:width])], sems)

    @pl.when((role_ref[0] == 1) | (role_ref[0] == 2))
    def _():
        fresh_ref[...] = jnp.zeros_like(fresh_ref)


def sum_heads(role, near, columns, acts, old_at, own_in, own_mix):
    ctx, _, width = acts.shape
    parts = [part for column in columns for part in column]
    size = parts[0].shape[0]
    smem = pl.BlockSpec(memory_space=pltpu.SMEM)
    hbm = pl.BlockSpec(memory_space=pl.ANY)
    return pl.pallas_call(
        functools.partial(sum_heads_kernel, own_mix, old_at),
        out_shape=[
            jax.ShapeDtypeStruct((ctx * own_in, width), bf16),
            jax.ShapeDtypeStruct((4, own_in, width), bf16),
        ],
        in_specs=[smem, smem] + [hbm] * 9,
        out_specs=[hbm, pl.BlockSpec(memory_space=pltpu.VMEM)],
        scratch_shapes=[
            pltpu.VMEM((4, 4, size, width), bf16),
            pltpu.VMEM((ctx, own_in, width), bf16),
            pltpu.VMEM((ctx * own_in, width), bf16),
            pltpu.VMEM((4, 4, own_in, width), bf16),
            pltpu.VMEM((width, width), f32),
            pltpu.SemaphoreType.DMA((9,)),
        ],
        compiler_params=pltpu.CompilerParams(vmem_limit_bytes=vmem_limit),
        cost_estimate=cost(4),
        name="sum_heads",
    )(role, near, *parts, acts)


def exchange(packed):
    return lax.all_to_all(packed, "ctx", split_axis=0, concat_axis=0, tiled=True)


def gather(array):
    return lax.all_gather(array, "ctx", axis=0, tiled=False)


def flip(array, mask, ctx):
    return lax.ppermute(array, "ctx", [(j, j ^ mask) for j in range(ctx)])


def spread_z(array, z_here, ctx):
    held = [array] + [flip(array, 4 * k, ctx) for k in (1, 2, 3)]
    odd, high = (z_here & 1) == 1, z_here >= 2
    first = [jnp.where(odd, held[k ^ 1], held[k]) for k in range(4)]
    return jnp.stack([jnp.where(high, first[k ^ 2], first[k]) for k in range(4)])


def gather_start(piece_for, z_here, ctx):
    own = piece_for(z_here)
    far = [flip(piece_for(z_here ^ k), 4 * k, ctx) for k in (1, 2, 3)]
    return own, far, [flip(own, mask, ctx) for mask in (2, 1)]


def gather_finish(started, ctx):
    own, far, own_sides = started
    far = jnp.stack(far)
    far_sides = [flip(far, mask, ctx) for mask in (2, 1)]
    across = tuple(flip(part, 1, ctx) for part in (own_sides[0], far_sides[0]))
    columns = [(own, far), (own_sides[0], far_sides[0]), (own_sides[1], far_sides[1]), across]
    for mask in [1 << n for n in range(4, ctx.bit_length() - 1)]:
        columns = columns + [tuple(flip(part, mask, ctx) for part in column) for column in columns]
    return columns


def column_at(mask):
    high = mask >> 4
    return ((mask >> 1) & 1) + 2 * (mask & 1) + 4 * high


def body(
    ctx,
    tokens,
    cotangent,
    block_order,
    input_weight,
    output_weight,
    expand_weight,
    reduce_weight,
    vectors,
    input_moment,
    output_moment,
    expand_moment,
    reduce_moment,
    vector_first,
    vector_second,
):
    seqs, local, width = tokens.shape
    rows = seqs * local
    length = ctx * local
    hd = width // HEADS
    layers = 2
    own_in = input_weight.shape[2]
    own_mix = output_weight.shape[2]
    own_ff = expand_weight.shape[2]
    own_vec = vectors.shape[1]
    dp_index = lax.axis_index("dp")
    ctx_index = lax.axis_index("ctx")
    owner_first = dp_index == 0

    ring_rows = 688

    def sections(parts):
        at, pieces, used = {}, [], 0
        for name, array in parts:
            size = array.shape[0]
            aligned = size % 16 == 0 and not name.startswith("old")
            start = -(-used // size) * size if aligned else used
            pieces.append(jnp.pad(array, ((start - used, 0), (0, 0))))
            at[name], used = start, start + size
        goal = -(-used // 16) * 16
        if ctx == 16 and goal > 512:
            goal = max(goal, ring_rows)
        pieces.append(jnp.zeros((goal - used, width), bf16))
        return jnp.concatenate(pieces, axis=0), at

    x_own = tokens.reshape(rows, width)
    cot = cotangent.reshape(rows, width)
    vec_row = jnp.pad(vectors.astype(bf16), ((0, 15), (0, width - own_vec)))
    pack = jnp.concatenate(
        [
            expand_weight[0].T.astype(bf16),
            reduce_weight[0].astype(bf16),
            output_weight[0].T.astype(bf16),
            input_weight[0].T.astype(bf16),
            vec_row,
        ],
        axis=0,
    )
    pack_other = lax.ppermute(pack, "dp", [(0, 1), (1, 0)])
    cuts = (own_ff, 2 * own_ff, 2 * own_ff + own_mix, 2 * own_ff + own_mix + own_in)
    own_parts = []
    for l in range(layers):
        mine = jnp.where(owner_first, (pack, pack_other)[l], (pack_other, pack)[l])
        own_parts.append(jnp.split(mine, cuts))
    pack_first, at_first = sections(
        [
            ("fc", own_parts[0][0]),
            ("red", own_parts[0][1]),
            ("tokens", x_own),
            ("vec", jnp.concatenate([own_parts[l][4][:8] for l in range(layers)], axis=0)),
            ("mix", own_parts[0][2]),
            ("in", own_parts[0][3]),
            ("next", own_parts[1][3]),
        ]
    )
    pack_second, at_second = sections(
        [
            ("fc", own_parts[1][0]),
            ("red", own_parts[1][1]),
            ("cot", cot),
            ("mix", own_parts[1][2]),
        ]
    )
    all_first, all_second = gather(pack_first), gather(pack_second)
    weights = (all_first, all_second)
    places = (at_first, at_second)
    in_at = (at_first["in"], at_first["next"])
    vecs = [
        all_first[:, at_first["vec"] + 8 * l, :own_vec].reshape(-1, width).astype(f32)
        for l in range(layers)
    ]

    block_len = length // block_order.shape[0]
    positions = (
        block_order[:, None] * block_len + jnp.arange(block_len, dtype=jnp.int32)[None, :]
    ).reshape(length)
    qpos = positions[:, None]
    kpos = positions[None, :]

    head = jnp.minimum(ctx_index, HEADS - 1)
    head_bias = jnp.concatenate(
        [
            lax.dynamic_slice_in_dim(vecs[0][2], head * hd, hd),
            jnp.zeros((hd,), f32),
            lax.dynamic_slice_in_dim(vecs[0][3], head * hd, hd),
        ]
    )
    stream = x_own
    saved = []
    for l in range(layers):
        if l == 0:
            a, qkv = head_qkv(
                head[None], all_first, at_first["tokens"], vecs[0], head_bias[None],
                all_first, at_first["in"], own_in, rows,
            )
        else:
            a, qkv_pack = qkv_forward(stream, vecs[l], all_first, in_at[l], own_in, local)
            qkv = exchange(qkv_pack).reshape(length, 6 * hd)
        out_full, out_low, prob = attn_forward(qkv, qpos, kpos)
        o_pack = exchange(out_low.reshape(ctx, local, 2 * hd))
        mid, c, hidden, fresh = mlp_forward(
            o_pack, stream, vecs[l], weights[l], places[l], own_ff, own_mix
        )
        saved.append((stream, a, qkv, out_full, out_low, prob, mid, c, hidden))
        stream = fresh
    block_output = stream.reshape(seqs, local, width)

    bias = [
        lax.dynamic_slice_in_dim(vecs[l][PIECES:].reshape(-1), ctx_index * own_ff, own_ff)[:, None]
        for l in range(layers)
    ]

    role = (ctx_index // 4) % 4

    grad = cot
    kept = [None, None]
    vec_grads = [None, None]
    for l in (1, 0):
        x, a, qkv, out_full, out_low, prob, mid, c, hidden = saved[l]
        gz, gmid, gy, go_pack, vg_late = mlp_backward(
            grad, mid, hidden, vecs[l], weights[l], places[l], own_ff, own_mix
        )
        if l == 1:
            pack_acts, at_acts = sections(
                [
                    ("c", saved[0][7]),
                    ("next_a", saved[1][1]),
                    ("next_c", saved[1][7]),
                    ("next_gy", gy),
                    ("old_in", input_moment[0].T.astype(bf16)),
                    ("old_mix", output_moment[0].T.astype(bf16)),
                ]
            )
            acts = gather(pack_acts)
        if l == 0:
            gz_held = spread_z(gz, role, ctx)
        go = exchange(go_pack).reshape(length, 2 * hd)
        dqkv = attn_backward(qkv, go, out_full, prob)
        if l == 0:
            dqkv, gz_held = lax.optimization_barrier((dqkv, gz_held))
            gz_held = gz_held.reshape(4 * rows, width)
            gz_sides = [flip(gz_held, mask, ctx) for mask in (2, 1)]
        dqkv_own = exchange(dqkv.reshape(ctx, local, 6 * hd))
        kept[l] = (gz, gy, dqkv)
        if l == 1:
            gin, vg_early = qkv_backward(dqkv_own, x, gmid, vecs[l], all_first, in_at[l], own_in)
            vec_grads[l] = jnp.concatenate([vg_early[:4], vg_late], axis=0)
            grad = gin

    gy_all = gather(kept[0][1])
    ready = hidden_ready(acts, at_acts["c"], own_parts[0][0], bias[0], rows)
    g_in_first = head_grads(kept[0][2], saved[0][1], 0, rows)
    old_hidden = jnp.concatenate([expand_moment[0].T, reduce_moment[0]], axis=0)
    ready, gz_sides, dqkv_own, g_in_first, old_hidden = lax.optimization_barrier(
        (ready, gz_sides, dqkv_own, g_in_first, old_hidden)
    )
    gz_masks = [0, 2, 1, 3]
    gz_columns = [gz_held, *gz_sides, flip(gz_sides[0], 1, ctx)]
    for mask in [1 << n for n in range(4, ctx.bit_length() - 1)]:
        gz_masks = gz_masks + [mask | other for other in gz_masks]
        gz_columns = gz_columns + [flip(column, mask, ctx) for column in gz_columns]
    g_head = [
        g_in_first,
        head_grads(kept[1][2], acts, at_acts["next_a"], rows),
        head_grads(saved[1][4], acts, at_acts["next_gy"], rows),
    ]
    gz_columns, g_head = lax.optimization_barrier((gz_columns, g_head))

    def owned(first, second):
        given = jnp.where(owner_first, second, first).astype(bf16)
        taken = lax.ppermute(given, "dp", [(0, 1), (1, 0)]).astype(f32)
        return jnp.where(owner_first, first, second) + taken

    g_in_head = owned(g_head[0], g_head[1]).astype(bf16)
    hidden_first = jnp.concatenate(
        hidden_last(
            acts, at_acts["c"], gz_columns, gz_masks, ctx_index, *ready, own_parts[0][1], rows
        ),
        axis=0,
    )
    hidden_first, acts, g_in_head = lax.optimization_barrier((hidden_first, acts, g_in_head))
    hidden_second = jnp.concatenate(
        hidden_grads(
            acts, at_acts["next_c"], all_second, at_second["cot"], *own_parts[1][:2], bias[1], rows
        ),
        axis=0,
    )
    gy_all, _ = lax.optimization_barrier((gy_all, hidden_second))
    moved = muon_moment * old_hidden + owned(hidden_first, hidden_second)
    moved, dqkv_own = lax.optimization_barrier((moved, dqkv_own))
    gin, vg_early = qkv_backward(dqkv_own, x, gmid, vecs[0], all_first, in_at[0], own_in)
    vec_grads[0] = jnp.concatenate([vg_early[:4], vg_late], axis=0)
    input_grad = gin.reshape(seqs, local, width)
    vec_terms = jnp.stack(vec_grads).reshape(layers, ctx, own_vec).swapaxes(0, 1)
    vec_terms = jnp.pad(vec_terms, ((0, 0), (0, 8 - layers), (0, width - own_vec)))
    m_fc = moved[:own_ff].T
    m_red = moved[own_ff:]

    big = max(own_ff, 3 * hd)

    def padded(piece):
        return jnp.pad(piece.astype(bf16), ((0, big - piece.shape[0]), (0, 0)))

    g_mix_first = head_grads(saved[0][4], gy_all, 0, rows)
    g_mix_head = owned(g_mix_first, g_head[2])
    pieces = (g_in_head, padded(moved[:own_ff]), padded(m_red), padded(g_mix_head))

    def piece_for(z):
        low = jnp.where(z == 0, pieces[0], pieces[1])
        return jnp.where(z < 2, low, jnp.where(z == 2, pieces[2], pieces[3]))

    started, vec_terms = lax.optimization_barrier((gather_start(piece_for, role, ctx), vec_terms))
    vec_sums = lax.psum_scatter(vec_terms, "ctx", scatter_dimension=0)
    columns = gather_finish(started, ctx)

    groups = ctx // 4
    near = ctx_index % 4
    masks = [m for m in range(ctx) if m & 12 == 0]
    order = sorted(masks, key=column_at)

    def absolute(array, size):
        mine = (ctx_index // 16) * 4 + near
        spots = jnp.array([column_at(((n >> 2) << 4) | (n & 3)) for n in range(groups)])
        listed = jnp.stack(
            [
                lax.dynamic_index_in_dim(array, spots[n ^ mine], 0, keepdims=False)[:, :size]
                for n in range(groups)
            ]
        )
        listed = listed.reshape(ctx // 16, 4, 4, size, width).swapaxes(1, 2)
        return listed.reshape(ctx, size, width)

    def relative(array):
        size = array.shape[1]
        split = array.reshape(ctx // 16, 4, 4, size, width).swapaxes(1, 2)
        split = split.reshape(groups, 4, size, width)
        mine = (ctx_index // 16) * 4 + near
        spread = jnp.stack(
            [
                lax.dynamic_index_in_dim(
                    split, mine ^ (((m >> 4) << 2) | (m & 3)), 0, keepdims=False
                )
                for m in order
            ]
        )
        return spread

    old_at = at_acts["old_in"]
    if ctx == 16 and own_in % 16 == 0 and own_mix % 16 == 0:
        sums, fresh = sum_heads(role[None], near[None], columns, acts, old_at, own_in, own_mix)
    else:
        old = acts[:, old_at : old_at + own_in + own_mix].astype(f32)

        def joined(parts):
            return jnp.stack([jnp.concatenate([own[None], far]) for own, far in parts])

        new_in = absolute(joined(columns), 3 * hd)[:HEADS].reshape(HEADS, 3, hd, width)
        new_in = new_in.swapaxes(0, 1).reshape(ctx, own_in, width)
        sum_in = relative((muon_moment * old[:, :own_in] + new_in.astype(f32)).astype(bf16))
        new_mix = absolute(joined(columns)[:, ::-1], hd)[:HEADS].reshape(width, width)
        new_mix = new_mix.T.reshape(ctx, own_mix, width)
        sum_mix = relative((muon_moment * old[:, own_in:] + new_mix.astype(f32)).astype(bf16))
        sum_mix = jnp.pad(sum_mix[:, ::-1].reshape(width, width), ((0, 2 * width), (0, 0)))
        sums = jnp.where(role == 3, sum_mix, sum_in.reshape(3 * width, width))
        new_mix = jnp.pad(relative(new_mix)[0, ::-1], ((0, 0), (0, own_in - own_mix), (0, 0)))
        fresh = jnp.where(role == 3, new_mix, relative(new_in)[0])

    taken = [fresh[0]]
    for k in (1, 2, 3):
        pairs = [(j, j ^ (4 * k)) for j in range(ctx) if (j // 4) % 4 in (0, 3)]
        taken.append(lax.ppermute(fresh[k], "ctx", pairs))
    direction = orthogonal(
        role[None],
        [(own[:own_ff], far[:, :own_ff]) for own, far in columns],
        sums,
        (own_in, own_ff, own_mix),
    )
    direction, taken, vec_sums = lax.optimization_barrier((direction, taken, vec_sums))
    vec_sums = vec_sums[:layers, :own_vec]
    vec_given = jnp.where(owner_first, vec_sums[1], vec_sums[0])
    vec_kept = jnp.where(owner_first, vec_sums[0], vec_sums[1])
    vec_grad = (vec_kept + lax.ppermute(vec_given, "dp", [(0, 1), (1, 0)]))[None]
    direction = direction.reshape(4, own_ff, width)
    by_distance = [direction[0]] + [flip(direction[k], 4 * k, ctx) for k in (1, 2, 3)]

    def from_role(by_distance, wanted):
        result = by_distance[wanted]
        for k in range(4):
            if k != wanted:
                result = jnp.where(role == wanted ^ k, by_distance[k], result)
        return result

    m_in = muon_moment * input_moment[0] + from_role(taken, 0).astype(f32).T
    m_mix = muon_moment * output_moment[0] + from_role(taken, 3)[:own_mix].astype(f32).T

    got = [from_role(by_distance, wanted) for wanted in range(4)]
    steps = (
        got[0][:own_in].astype(f32).T,
        got[3][:own_mix].astype(f32).T,
        got[1].astype(f32).T,
        got[2].astype(f32),
    )
    hidden_units = ctx * own_ff
    largest = (3 * width, width, hidden_units, hidden_units)
    old_weights = (input_weight, output_weight, expand_weight, reduce_weight)
    new_weights = [
        old_weights[kind] * (1.0 - muon_rate * muon_decay)
        - muon_rate * 0.2 * math.sqrt(largest[kind]) * steps[kind][None]
        for kind in range(4)
    ]

    new_vector_first = beta_first * vector_first + (1.0 - beta_first) * vec_grad
    new_vector_second = beta_second * vector_second + (1.0 - beta_second) * vec_grad * vec_grad
    corr_first = 1.0 - beta_first**STEP
    corr_second = 1.0 - beta_second**STEP
    new_vectors = vectors - adam_rate * (new_vector_first / corr_first) / (
        jnp.sqrt(new_vector_second / corr_second) + adam_epsilon
    )
    return (
        block_output,
        input_grad,
        new_weights[0],
        new_weights[1],
        new_weights[2],
        new_weights[3],
        m_in[None],
        m_mix[None],
        m_fc[None],
        m_red[None],
        new_vectors,
        new_vector_first,
        new_vector_second,
    )


def solution(mesh):
    return jax.shard_map(
        functools.partial(body, mesh.shape["ctx"]),
        mesh=mesh,
        in_specs=(
            P("dp", "ctx", None),
            P("dp", "ctx", None),
            P(),
            P("dp", None, "ctx"),
            P("dp", None, "ctx"),
            P("dp", None, "ctx"),
            P("dp", "ctx", None),
            P("dp", "ctx"),
            P("dp", None, "ctx"),
            P("dp", None, "ctx"),
            P("dp", None, "ctx"),
            P("dp", "ctx", None),
            P("dp", "ctx"),
            P("dp", "ctx"),
        ),
        out_specs=(
            P("dp", "ctx", None),
            P("dp", "ctx", None),
            P("dp", None, "ctx"),
            P("dp", None, "ctx"),
            P("dp", None, "ctx"),
            P("dp", "ctx", None),
            P("dp", None, "ctx"),
            P("dp", None, "ctx"),
            P("dp", None, "ctx"),
            P("dp", "ctx", None),
            P("dp", "ctx"),
            P("dp", "ctx"),
            P("dp", "ctx"),
        ),
        check_vma=False,
    )
```

```python
import functools
import math

import jax
import jax.numpy as jnp
from jax import lax
from jax.experimental import pallas as pl
from jax.experimental.pallas import tpu as pltpu
from jax.sharding import PartitionSpec as P

HEADS = 12
NS_STEPS = 5
STEP = 10
PIECES = 8

norm_epsilon = 1e-05
neg_large = -1e30
score_scale = 0.125
coef_first = 3.4445
coef_second = -4.775
coef_third = 2.0315
ortho_epsilon = 1e-07
muon_rate = 0.15
muon_moment = 0.95
muon_decay = 0.01
adam_rate = 0.3
beta_first = 0.9
beta_second = 0.95
adam_epsilon = 1e-08
gelu_inner = 0.7978845608
gelu_cubic = 0.044715
shifts = (0.0, 0.0, 0.17, 1.0, 0.8)

f32 = jnp.float32
bf16 = jnp.bfloat16
vmem_limit = 56 * 1024 * 1024


def mm(left, right):
    return jnp.dot(left, right, preferred_element_type=f32)


def mm_nt(left, right):
    return lax.dot_general(left, right, (((1,), (1,)), ((), ())), preferred_element_type=f32)


def mm_tn(left, right):
    return lax.dot_general(left, right, (((0,), (0,)), ((), ())), preferred_element_type=f32)


def cost(micros):
    return pl.CostEstimate(
        flops=int(micros * 1e9), bytes_accessed=int(micros * 1e6), transcendentals=0
    )


def params(grid_dims):
    return pltpu.CompilerParams(
        dimension_semantics=("arbitrary",) * grid_dims, vmem_limit_bytes=vmem_limit
    )


def normalized(values_in):
    centred = values_in - jnp.mean(values_in, axis=-1, keepdims=True)
    inv_std = lax.rsqrt(jnp.mean(centred * centred, axis=-1, keepdims=True) + norm_epsilon)
    return centred * inv_std, inv_std


def norm_backward(grad_out, normed, inv_std, gain):
    scaled = grad_out * gain
    return inv_std * (
        scaled
        - jnp.mean(scaled, axis=-1, keepdims=True)
        - normed * jnp.mean(scaled * normed, axis=-1, keepdims=True)
    )


def pair_lanes(values_in, local, start, size):
    return jnp.concatenate(
        [values_in[:local, start : start + size], values_in[local:, start : start + size]], axis=1
    )


def join_heads(ref, local, hd):
    rows = []
    for s in range(2):
        rows.append(
            jnp.concatenate(
                [ref[h][:, s * hd : (s + 1) * hd].astype(f32) for h in range(HEADS)], axis=1
            )
        )
    return jnp.concatenate(rows, axis=0)


def qkv_kernel(x_ref, vec_ref, w_ref, a_ref, out_ref, proj_ref):
    step = pl.program_id(0)
    steps, _, chunk = proj_ref.shape
    local = out_ref.shape[1]
    hd = out_ref.shape[2] // 6
    width = x_ref.shape[1]

    @pl.when(step == 0)
    def _():
        normed, _ = normalized(x_ref[...].astype(f32))
        a_ref[...] = (normed * vec_ref[0:1, :] + vec_ref[1:2, :]).astype(bf16)

    proj_ref[step] = mm_nt(a_ref[...], w_ref[...].reshape(chunk, width))

    @pl.when(step == steps - 1)
    def _():
        proj = jnp.concatenate([proj_ref[i] for i in range(steps)], axis=1)
        bias = (vec_ref[2:3, :], jnp.zeros((1, width), f32), vec_ref[3:4, :])
        for part in range(3):
            piece = proj[:, part * width : (part + 1) * width] + bias[part]
            for h in range(HEADS):
                out_ref[h, :, part * 2 * hd : (part + 1) * 2 * hd] = pair_lanes(
                    piece, local, h * hd, hd
                ).astype(bf16)
        for h in range(HEADS, out_ref.shape[0]):
            out_ref[h] = jnp.zeros(out_ref.shape[1:], bf16)


def shard_blocks(array, start, own, steps):
    ctx, _, width = array.shape
    group = ctx // steps
    if own % 16 == 0 and start % own == 0:
        return array, pl.BlockSpec(
            (group, own, width), lambda i: (i if steps > 1 else 0, start // own, 0)
        )
    part = array[:, start : start + own].reshape(steps, group * own, width)
    return part, pl.BlockSpec((1, group * own, width), lambda i: (i if steps > 1 else 0, 0, 0))


def qkv_forward(x, vec, weights, at, own_in, local):
    rows, width = x.shape
    ctx = weights.shape[0]
    hd = width // HEADS
    steps = 4
    w_array, w_spec = shard_blocks(weights, at, own_in, steps)
    whole = lambda i: (0, 0)
    return pl.pallas_call(
        qkv_kernel,
        grid=(steps,),
        in_specs=[
            pl.BlockSpec((rows, width), whole),
            pl.BlockSpec(vec.shape, whole),
            w_spec,
        ],
        out_specs=[
            pl.BlockSpec((rows, width), whole),
            pl.BlockSpec((ctx, local, 6 * hd), lambda i: (0, 0, 0)),
        ],
        out_shape=[
            jax.ShapeDtypeStruct((rows, width), bf16),
            jax.ShapeDtypeStruct((ctx, local, 6 * hd), bf16),
        ],
        scratch_shapes=[pltpu.VMEM((steps, rows, 3 * width // steps), f32)],
        compiler_params=params(1),
        cost_estimate=cost(5),
        name="qkv_forward",
    )(x, vec, w_array)


def head_qkv_kernel(head_ref, x_ref, vec_ref, bias_ref, w_ref, a_ref, out_ref, w_all_ref, own_ref):
    shards, rows, width = x_ref.shape
    local = rows // 2
    hd = out_ref.shape[1] // 6

    @pl.when(pl.program_id(0) == 0)
    def _():
        w_all_ref[...] = w_ref[...].reshape(w_all_ref.shape)
        for part in range(3):
            first = pl.multiple_of(part * width + head_ref[0] * hd, hd)
            own_ref[part * hd : (part + 1) * hd, :] = w_all_ref[pl.ds(first, hd), :]

    normed, _ = normalized(x_ref[...].reshape(shards * rows, width).astype(f32))
    first_in = (normed * vec_ref[0:1, :] + vec_ref[1:2, :]).astype(bf16)
    a_ref[...] = first_in.reshape(shards, rows, width)
    proj = (mm_nt(first_in, own_ref[...]) + bias_ref[...]).reshape(shards, 2, local, 3 * hd)
    sides = [proj[:, s].reshape(shards * local, 3 * hd) for s in range(2)]
    for part in range(3):
        cut = slice(part * hd, (part + 1) * hd)
        out_ref[:, 2 * part * hd : 2 * (part + 1) * hd] = jnp.concatenate(
            [sides[0][:, cut], sides[1][:, cut]], axis=1
        ).astype(bf16)


def head_qkv(head, tokens_all, tokens_at, vec, bias, weights, at, own_in, rows):
    ctx, _, width = tokens_all.shape
    hd = width // HEADS
    local = rows // 2
    x_array, x_spec = shard_blocks(tokens_all, tokens_at, rows, ctx // 4)
    w_array, w_spec = shard_blocks(weights, at, own_in, 1)
    whole = lambda i: (0, 0)
    return pl.pallas_call(
        head_qkv_kernel,
        grid=(ctx // 4,),
        in_specs=[
            pl.BlockSpec(memory_space=pltpu.SMEM),
            x_spec,
            pl.BlockSpec(vec.shape, whole),
            pl.BlockSpec(bias.shape, whole),
            w_spec,
        ],
        out_specs=[
            pl.BlockSpec((4, rows, width), lambda i: (i, 0, 0)),
            pl.BlockSpec((4 * local, 6 * hd), lambda i: (i, 0)),
        ],
        out_shape=[
            jax.ShapeDtypeStruct((ctx, rows, width), bf16),
            jax.ShapeDtypeStruct((ctx * local, 6 * hd), bf16),
        ],
        scratch_shapes=[pltpu.VMEM((3 * width, width), bf16), pltpu.VMEM((3 * hd, width), bf16)],
        compiler_params=params(1),
        cost_estimate=cost(6),
        name="head_qkv",
    )(head, x_array, vec, bias, w_array)


def lane_masks(rows, lanes):
    lane = lax.broadcasted_iota(jnp.int32, (rows, lanes), 1)
    first = jnp.where(lane < lanes // 2, 1.0, 0.0)
    return first.astype(bf16), (1.0 - first).astype(bf16)


def attn_fwd_kernel(qpos_ref, kpos_ref, q_ref, k_ref, v_ref, of_ref, ob_ref, p_ref):
    allowed = kpos_ref[...] <= qpos_ref[...]
    q_masks = lane_masks(*q_ref.shape)
    v_masks = lane_masks(*v_ref.shape)
    out = jnp.zeros(of_ref.shape, f32)
    for s in range(2):
        scores = mm_nt(q_ref[...] * q_masks[s], k_ref[...]) * score_scale
        scores = jnp.where(allowed, scores, neg_large)
        expo = jnp.exp(scores - jnp.max(scores, axis=-1, keepdims=True))
        prob = (expo * (1.0 / jnp.sum(expo, axis=-1, keepdims=True))).astype(bf16)
        p_ref[s] = prob
        out = out + mm(prob, v_ref[...] * v_masks[s])
    of_ref[...] = out
    ob_ref[...] = out.astype(bf16)


def attn_forward(qkv, qpos, kpos):
    length, lanes = qkv.shape
    pair = lanes // 3
    tile = min(256, length)
    return pl.pallas_call(
        attn_fwd_kernel,
        grid=(length // tile,),
        in_specs=[
            pl.BlockSpec((tile, 1), lambda i: (i, 0)),
            pl.BlockSpec((1, length), lambda i: (0, 0)),
            pl.BlockSpec((tile, pair), lambda i: (i, 0)),
            pl.BlockSpec((length, pair), lambda i: (0, 1)),
            pl.BlockSpec((length, pair), lambda i: (0, 2)),
        ],
        out_specs=[
            pl.BlockSpec((tile, pair), lambda i: (i, 0)),
            pl.BlockSpec((tile, pair), lambda i: (i, 0)),
            pl.BlockSpec((2, tile, length), lambda i: (0, i, 0)),
        ],
        out_shape=[
            jax.ShapeDtypeStruct((length, pair), f32),
            jax.ShapeDtypeStruct((length, pair), bf16),
            jax.ShapeDtypeStruct((2, length, length), bf16),
        ],
        compiler_params=params(1),
        cost_estimate=cost(8),
        name="attn_forward",
    )(qpos, kpos, qkv, qkv, qkv)


def attn_bwd_kernel(q_ref, go_ref, of_ref, p_ref, k_ref, v_ref, out_ref, dk_ref, dv_ref):
    step = pl.program_id(0)
    tile, pair = q_ref.shape
    masks = lane_masks(tile, pair)
    k_masks = lane_masks(*k_ref.shape)

    @pl.when(step == 0)
    def _():
        dk_ref[...] = jnp.zeros_like(dk_ref)
        dv_ref[...] = jnp.zeros_like(dv_ref)

    dq = jnp.zeros((tile, pair), f32)
    for s in range(2):
        go = go_ref[...] * masks[s]
        row_dot = jnp.sum(go.astype(f32) * of_ref[...], axis=-1, keepdims=True)
        prob = p_ref[s]
        grad_prob = mm_nt(go, v_ref[...])
        ds = (prob.astype(f32) * (grad_prob - row_dot)).astype(bf16)
        dv_ref[...] += mm_tn(go, prob)
        dk_ref[...] += mm_tn(q_ref[...] * masks[s], ds)
        dq = dq + mm(ds, k_ref[...] * k_masks[s])
    out_ref[pl.ds(pl.multiple_of(step * tile, tile), tile), 0:pair] = (dq * score_scale).astype(bf16)

    @pl.when(step == pl.num_programs(0) - 1)
    def _():
        out_ref[:, pair : 2 * pair] = (dk_ref[...].T * score_scale).astype(bf16)
        out_ref[:, 2 * pair :] = dv_ref[...].T.astype(bf16)


def attn_backward(qkv, go, out_full, prob):
    length, lanes = qkv.shape
    pair = lanes // 3
    tile = min(256, length)
    return pl.pallas_call(
        attn_bwd_kernel,
        grid=(length // tile,),
        in_specs=[
            pl.BlockSpec((tile, pair), lambda i: (i, 0)),
            pl.BlockSpec((tile, pair), lambda i: (i, 0)),
            pl.BlockSpec((tile, pair), lambda i: (i, 0)),
            pl.BlockSpec((2, tile, length), lambda i: (0, i, 0)),
            pl.BlockSpec((length, pair), lambda i: (0, 1)),
            pl.BlockSpec((length, pair), lambda i: (0, 2)),
        ],
        out_specs=pl.BlockSpec((length, lanes), lambda i: (0, 0)),
        out_shape=jax.ShapeDtypeStruct((length, lanes), bf16),
        scratch_shapes=[pltpu.VMEM((pair, length), f32), pltpu.VMEM((pair, length), f32)],
        compiler_params=params(1),
        cost_estimate=cost(8),
        name="attn_backward",
    )(qkv, go, out_full, prob, qkv, qkv)


def mlp_fwd_kernel(o_ref, x_ref, vec_ref, mix_ref, fc_ref, red_ref, mid_ref, c_ref, h_ref, out_ref):
    step = pl.program_id(0)
    rows, width = x_ref.shape

    @pl.when(step == 0)
    def _():
        mixed = join_heads(o_ref, rows // 2, o_ref.shape[2] // 2).astype(bf16)
        mix_w = mix_ref[...].reshape(width, width)
        middle = x_ref[...].astype(f32) + (mm_nt(mixed, mix_w) + vec_ref[4:5, :])
        mid_ref[...] = middle
        normed, _ = normalized(middle)
        c_ref[...] = (normed * vec_ref[5:6, :] + vec_ref[6:7, :]).astype(bf16)
        out_ref[...] = middle + vec_ref[7:8, :]

    hidden = mm_nt(c_ref[...], fc_ref[...].reshape(width, width))
    hidden = hidden + vec_ref[pl.ds(PIECES + step, 1), :]
    h_ref[...] = hidden
    inner = jnp.tanh(gelu_inner * (hidden + gelu_cubic * hidden * hidden * hidden))
    active = (0.5 * hidden * (1.0 + inner)).astype(bf16)
    out_ref[...] += mm(active, red_ref[...].reshape(width, width))


def mlp_forward(o_pack, x, vec, weights, at, own_ff, own_mix):
    rows, width = x.shape
    hidden = weights.shape[0] * own_ff
    steps = hidden // width
    fc_array, fc_spec = shard_blocks(weights, at["fc"], own_ff, steps)
    red_array, red_spec = shard_blocks(weights, at["red"], own_ff, steps)
    mix_array, mix_spec = shard_blocks(weights, at["mix"], own_mix, 1)
    whole = lambda i: (0, 0)
    return pl.pallas_call(
        mlp_fwd_kernel,
        grid=(steps,),
        in_specs=[
            pl.BlockSpec(o_pack.shape, lambda i: (0, 0, 0)),
            pl.BlockSpec((rows, width), whole),
            pl.BlockSpec(vec.shape, whole),
            mix_spec,
            fc_spec,
            red_spec,
        ],
        out_specs=[
            pl.BlockSpec((rows, width), whole),
            pl.BlockSpec((rows, width), whole),
            pl.BlockSpec((rows, width), lambda i: (0, i)),
            pl.BlockSpec((rows, width), whole),
        ],
        out_shape=[
            jax.ShapeDtypeStruct((rows, width), f32),
            jax.ShapeDtypeStruct((rows, width), bf16),
            jax.ShapeDtypeStruct((rows, hidden), f32),
            jax.ShapeDtypeStruct((rows, width), f32),
        ],
        compiler_params=params(1),
        cost_estimate=cost(8),
        name="mlp_forward",
    )(o_pack, x, vec, mix_array, fc_array, red_array)


def gelu_slope(hidden):
    square = hidden * hidden
    inner = jnp.tanh(gelu_inner * (hidden + gelu_cubic * hidden * square))
    slope = 0.5 * (1.0 + inner) + (0.5 * gelu_inner) * hidden * (1.0 - inner * inner) * (
        1.0 + (3.0 * gelu_cubic) * square
    )
    return inner, slope


def mlp_bwd_kernel(
    gr_ref, mid_ref, h_ref, vec_ref, mix_ref, fc_ref, red_ref,
    gz_ref, gmid_ref, gy_ref, go_ref, vg_ref, gc_ref,
):
    step = pl.program_id(0)
    rows, width = gr_ref.shape

    @pl.when(step == 0)
    def _():
        gz_ref[...] = gr_ref[...].astype(bf16)
        gc_ref[...] = jnp.zeros_like(gc_ref)

    _, slope = gelu_slope(h_ref[...])
    grad_hidden = (mm_nt(gz_ref[...], red_ref[...].reshape(width, width)) * slope).astype(bf16)
    vg_ref[pl.ds(4 + step, 1), :] = jnp.sum(grad_hidden.astype(f32), axis=0, keepdims=True)
    gc_ref[...] += mm(grad_hidden, fc_ref[...].reshape(width, width))

    @pl.when(step == pl.num_programs(0) - 1)
    def _():
        grad = gr_ref[...].astype(f32)
        normed, inv_std = normalized(mid_ref[...])
        grad_second = gc_ref[...]
        grad_mid = grad + norm_backward(grad_second, normed, inv_std, vec_ref[5:6, :])
        gmid_ref[...] = grad_mid
        gy = grad_mid.astype(bf16)
        gy_ref[...] = gy
        vg_ref[0:1, :] = jnp.sum(gy.astype(f32), axis=0, keepdims=True)
        vg_ref[1:2, :] = jnp.sum(grad_second * normed, axis=0, keepdims=True)
        vg_ref[2:3, :] = jnp.sum(grad_second, axis=0, keepdims=True)
        vg_ref[3:4, :] = jnp.sum(gz_ref[...].astype(f32), axis=0, keepdims=True)
        grad_attn = mm(gy, mix_ref[...].reshape(width, width))
        hd = go_ref.shape[2] // 2
        for h in range(HEADS):
            go_ref[h] = pair_lanes(grad_attn, rows // 2, h * hd, hd).astype(bf16)
        for h in range(HEADS, go_ref.shape[0]):
            go_ref[h] = jnp.zeros(go_ref.shape[1:], bf16)


def mlp_backward(gr, mid, hidden, vec, weights, at, own_ff, own_mix):
    rows, width = mid.shape
    ctx = weights.shape[0]
    steps = hidden.shape[1] // width
    hd = width // HEADS
    fc_array, fc_spec = shard_blocks(weights, at["fc"], own_ff, steps)
    red_array, red_spec = shard_blocks(weights, at["red"], own_ff, steps)
    mix_array, mix_spec = shard_blocks(weights, at["mix"], own_mix, 1)
    whole = lambda i: (0, 0)
    return pl.pallas_call(
        mlp_bwd_kernel,
        grid=(steps,),
        in_specs=[
            pl.BlockSpec((rows, width), whole),
            pl.BlockSpec((rows, width), whole),
            pl.BlockSpec((rows, width), lambda i: (0, i)),
            pl.BlockSpec(vec.shape, whole),
            mix_spec,
            fc_spec,
            red_spec,
        ],
        out_specs=[
            pl.BlockSpec((rows, width), whole),
            pl.BlockSpec((rows, width), whole),
            pl.BlockSpec((rows, width), whole),
            pl.BlockSpec((ctx, rows // 2, 2 * hd), lambda i: (0, 0, 0)),
            pl.BlockSpec((PIECES, width), whole),
        ],
        out_shape=[
            jax.ShapeDtypeStruct((rows, width), bf16),
            jax.ShapeDtypeStruct((rows, width), f32),
            jax.ShapeDtypeStruct((rows, width), bf16),
            jax.ShapeDtypeStruct((ctx, rows // 2, 2 * hd), bf16),
            jax.ShapeDtypeStruct((PIECES, width), f32),
        ],
        scratch_shapes=[pltpu.VMEM((rows, width), f32)],
        compiler_params=params(1),
        cost_estimate=cost(8),
        name="mlp_backward",
    )(gr, mid, hidden, vec, mix_array, fc_array, red_array)


def qkv_bwd_kernel(d_ref, x_ref, gmid_ref, vec_ref, w_ref, gin_ref, vg_ref, d_all_ref, ga_ref):
    step = pl.program_id(0)
    steps, rows, chunk = d_all_ref.shape
    width = x_ref.shape[1]

    @pl.when(step == 0)
    def _():
        hd = d_ref.shape[2] // 6
        parts = []
        for part in range(3):
            for s in range(2):
                start = (2 * part + s) * hd
                parts.append(
                    jnp.concatenate(
                        [d_ref[h, :, start : start + hd].astype(f32) for h in range(HEADS)], axis=1
                    )
                )
        joined = jnp.concatenate(
            [jnp.concatenate([parts[2 * part], parts[2 * part + 1]], axis=0) for part in range(3)],
            axis=1,
        )
        vg_ref[...] = jnp.zeros_like(vg_ref)
        vg_ref[2:3, :] = jnp.sum(joined[:, :width], axis=0, keepdims=True)
        vg_ref[3:4, :] = jnp.sum(joined[:, 2 * width :], axis=0, keepdims=True)
        for i in range(steps):
            d_all_ref[i] = joined[:, i * chunk : (i + 1) * chunk].astype(bf16)
        ga_ref[...] = jnp.zeros_like(ga_ref)

    ga_ref[...] += mm(d_all_ref[step], w_ref[...].reshape(chunk, width))

    @pl.when(step == steps - 1)
    def _():
        normed, inv_std = normalized(x_ref[...].astype(f32))
        grad_first = ga_ref[...]
        gin_ref[...] = gmid_ref[...] + norm_backward(grad_first, normed, inv_std, vec_ref[0:1, :])
        vg_ref[0:1, :] = jnp.sum(grad_first * normed, axis=0, keepdims=True)
        vg_ref[1:2, :] = jnp.sum(grad_first, axis=0, keepdims=True)


def qkv_backward(dqkv, x, gmid, vec, weights, at, own_in):
    rows, width = x.shape
    steps = 4
    w_array, w_spec = shard_blocks(weights, at, own_in, steps)
    whole = lambda i: (0, 0)
    return pl.pallas_call(
        qkv_bwd_kernel,
        grid=(steps,),
        in_specs=[
            pl.BlockSpec(dqkv.shape, lambda i: (0, 0, 0)),
            pl.BlockSpec((rows, width), whole),
            pl.BlockSpec((rows, width), whole),
            pl.BlockSpec(vec.shape, whole),
            w_spec,
        ],
        out_specs=[
            pl.BlockSpec((rows, width), whole),
            pl.BlockSpec((PIECES, width), whole),
        ],
        out_shape=[
            jax.ShapeDtypeStruct((rows, width), f32),
            jax.ShapeDtypeStruct((PIECES, width), f32),
        ],
        scratch_shapes=[
            pltpu.VMEM((steps, rows, 3 * width // steps), bf16),
            pltpu.VMEM((rows, width), f32),
        ],
        compiler_params=params(1),
        cost_estimate=cost(5),
        name="qkv_backward",
    )(dqkv, x, gmid, vec, w_array)


def hidden_grads_kernel(c_ref, gz_ref, fc_ref, red_ref, bias_ref, gfc_ref, gred_ref):
    own, width = gfc_ref.shape
    second = c_ref[...].reshape(-1, width)
    branch = gz_ref[...].reshape(-1, width)
    hidden = mm_nt(fc_ref[...], second) + bias_ref[...]
    inner, slope = gelu_slope(hidden)
    active = (0.5 * hidden * (1.0 + inner)).astype(bf16)
    grad_hidden = (mm_nt(red_ref[...], branch) * slope).astype(bf16)

    @pl.when(pl.program_id(0) == 0)
    def _():
        gfc_ref[...] = jnp.zeros_like(gfc_ref)
        gred_ref[...] = jnp.zeros_like(gred_ref)

    gfc_ref[...] += mm(grad_hidden, second)
    gred_ref[...] += mm(active, branch)


def hidden_grads(c_all, c_at, gz_all, gz_at, fc_own, red_own, bias, rows):
    ctx, _, width = c_all.shape
    own_ff = fc_own.shape[0]
    steps = ctx // 4
    c_array, c_spec = shard_blocks(c_all, c_at, rows, steps)
    gz_array, gz_spec = shard_blocks(gz_all, gz_at, rows, steps)
    whole = lambda i: (0, 0)
    return pl.pallas_call(
        hidden_grads_kernel,
        grid=(steps,),
        in_specs=[
            c_spec,
            gz_spec,
            pl.BlockSpec((own_ff, width), whole),
            pl.BlockSpec((own_ff, width), whole),
            pl.BlockSpec((own_ff, 1), whole),
        ],
        out_specs=[pl.BlockSpec((own_ff, width), whole)] * 2,
        out_shape=[jax.ShapeDtypeStruct((own_ff, width), f32)] * 2,
        compiler_params=params(1),
        cost_estimate=cost(1),
        name="hidden_grads",
    )(c_array, gz_array, fc_own, red_own, bias)


def hidden_ready_kernel(c_ref, fc_ref, bias_ref, u_ref, slope_ref):
    width = fc_ref.shape[1]
    hidden = mm_nt(fc_ref[...], c_ref[...].reshape(-1, width)) + bias_ref[...]
    inner, slope = gelu_slope(hidden)
    u_ref[...] = (0.5 * hidden * (1.0 + inner)).astype(bf16)
    slope_ref[...] = slope


def rows_by_z(c_all, c_at, rows):
    ctx, _, width = c_all.shape
    assert c_at % rows == 0
    view = c_all.reshape(ctx // 16, 4, 4, *c_all.shape[1:])
    return view, pl.BlockSpec(
        (1, 4, 1, rows, width),
        lambda i: (i // 4, 0, (i % 2) * 2 + (i // 2) % 2, c_at // rows, 0),
    )


def hidden_ready(c_all, c_at, fc_own, bias, rows):
    ctx, _, width = c_all.shape
    own_ff = fc_own.shape[0]
    c_array, c_spec = rows_by_z(c_all, c_at, rows)
    whole = lambda i: (0, 0)
    return pl.pallas_call(
        hidden_ready_kernel,
        grid=(ctx // 4,),
        in_specs=[
            c_spec,
            pl.BlockSpec((own_ff, width), whole),
            pl.BlockSpec((own_ff, 1), whole),
        ],
        out_specs=[pl.BlockSpec((own_ff, 4 * rows), lambda i: (0, i))] * 2,
        out_shape=[
            jax.ShapeDtypeStruct((own_ff, ctx * rows), bf16),
            jax.ShapeDtypeStruct((own_ff, ctx * rows), f32),
        ],
        compiler_params=params(1),
        cost_estimate=cost(1),
        name="hidden_ready",
    )(c_array, fc_own, bias)


def hidden_last_kernel(own_ref, c_ref, u_ref, slope_ref, red_ref, *refs):
    gz_refs, (gfc_ref, gred_ref) = refs[:-2], refs[-2:]
    width = red_ref.shape[1]

    @pl.when(pl.program_id(0) == 0)
    def _():
        gfc_ref[...] = jnp.zeros_like(gfc_ref)
        gred_ref[...] = jnp.zeros_like(gred_ref)

    for step, gz_ref in enumerate(gz_refs):

        @pl.when(pl.program_id(0) == step)
        def _():
            branch = gz_ref[...]
            grad_hidden = (mm_nt(red_ref[...], branch) * slope_ref[...]).astype(bf16)
            gred_ref[...] += mm(u_ref[...], branch)
            gfc_ref[...] += mm(grad_hidden, c_ref[...].reshape(-1, width))


def hidden_last(c_all, c_at, columns, masks, ctx_index, active, slope, red_own, rows):
    width = red_own.shape[1]
    own_ff = red_own.shape[0]
    c_array, c_spec = rows_by_z(c_all, c_at, rows)

    def place(index):
        return (index >> 4) * 4 + (index & 1) * 2 + ((index >> 1) & 1)

    def block(step, own_ref):
        distance = 0
        for number, mask in enumerate(masks):
            distance = jnp.where(step == number, place(mask), distance)
        return own_ref[0] ^ distance

    whole = lambda i, own: (0, 0)
    return pl.pallas_call(
        hidden_last_kernel,
        grid_spec=pltpu.PrefetchScalarGridSpec(
            num_scalar_prefetch=1,
            grid=(len(columns),),
            in_specs=[
                pl.BlockSpec(
                    c_spec.block_shape, lambda i, own: c_spec.index_map(block(i, own))
                ),
                pl.BlockSpec((own_ff, 4 * rows), lambda i, own: (0, block(i, own))),
                pl.BlockSpec((own_ff, 4 * rows), lambda i, own: (0, block(i, own))),
                pl.BlockSpec((own_ff, width), whole),
            ]
            + [pl.BlockSpec((4 * rows, width), whole)] * len(columns),
            out_specs=[pl.BlockSpec((own_ff, width), whole)] * 2,
        ),
        out_shape=[jax.ShapeDtypeStruct((own_ff, width), f32)] * 2,
        compiler_params=params(1),
        cost_estimate=cost(1),
        name="hidden_last",
    )(place(ctx_index)[None], c_array, active, slope, red_own, *columns)


def head_grads_kernel(pack_ref, rows_ref, out_ref):
    length, lanes = pack_ref.shape
    _, rows, width = rows_ref.shape
    local = rows // 2
    hd = width // HEADS
    for s in range(2):
        piece = rows_ref[:, s * local : (s + 1) * local, :].reshape(length, width)
        result = mm_tn(pack_ref[...], piece)
        for part in range(out_ref.shape[0] // hd):
            start = (2 * part + s) * hd
            if s == 0:
                out_ref[part * hd : (part + 1) * hd, :] = result[start : start + hd]
            else:
                out_ref[part * hd : (part + 1) * hd, :] += result[start : start + hd]


def head_grads(pack, rows_all, at, rows):
    length, lanes = pack.shape
    ctx, _, width = rows_all.shape
    rows_array, rows_spec = shard_blocks(rows_all, at, rows, 1)
    return pl.pallas_call(
        head_grads_kernel,
        grid=(1,),
        in_specs=[
            pl.BlockSpec((length, lanes), lambda i: (0, 0)),
            rows_spec,
        ],
        out_specs=pl.BlockSpec((lanes // 2, width), lambda i: (0, 0)),
        out_shape=jax.ShapeDtypeStruct((lanes // 2, width), f32),
        compiler_params=params(1),
        cost_estimate=cost(1),
        name="head_grads",
    )(pack, rows_array)


def copy_all(moves, sems):
    copies = [pltpu.make_async_copy(src, dst, sems.at[i]) for i, (src, dst) in enumerate(moves)]
    for copy in copies:
        copy.start()
    for copy in copies:
        copy.wait()


def ns_kernel(own, parts_count, role_ref, *refs):
    parts, sums_ref = refs[:parts_count], refs[parts_count]
    out_refs = refs[parts_count + 1 : parts_count + 5]
    y_ref, full_ref, low_ref, gram_ref, poly_ref, sems = refs[parts_count + 5 :]
    length, side = y_ref.shape
    own_in, own_ff, own_mix = own
    tile = 256
    role = role_ref[0]
    is_in, is_mix = role == 0, role == 3
    is_long = (role == 1) | (role == 2)
    kinds = ((is_long, length, own_ff), (is_in, 3 * side, own_in), (is_mix, side, own_mix))
    chunks = jnp.where(is_mix, 1, jnp.where(is_in, 3, length // side))

    @pl.when(is_long)
    def _():
        moves, start = [], 0
        for part in parts:
            moves.append((part, y_ref.at[start : start + part.shape[0]]))
            start += part.shape[0]
        copy_all(moves, sems)

    @pl.when(is_in)
    def _():
        copy_all([(sums_ref, y_ref.at[: 3 * side])], sems)

    @pl.when(is_mix)
    def _():
        copy_all([(sums_ref.at[:side], y_ref.at[:side])], sems)

    eye = jnp.where(
        lax.broadcasted_iota(jnp.int32, (side, side), 0)
        == lax.broadcasted_iota(jnp.int32, (side, side), 1),
        1.0,
        0.0,
    )

    def each_chunk(work):
        def one(i, carry):
            work(pl.ds(pl.multiple_of(i * side, side), side))
            return carry

        lax.fori_loop(0, chunks, one, 0)

    def gram():
        for kind, columns, _ in kinds:

            @pl.when(kind)
            def _():
                for i in range(side // tile):
                    rows = slice(i * tile, (i + 1) * tile)
                    gram_ref[rows, i * tile :] = mm_nt(
                        low_ref[rows, :columns], low_ref[i * tile :, :columns]
                    )

        for i in range(side // tile):
            for j in range(i + 1, side // tile):
                gram_ref[j * tile : (j + 1) * tile, i * tile : (i + 1) * tile] = gram_ref[
                    i * tile : (i + 1) * tile, j * tile : (j + 1) * tile
                ].T

    def load(cols):
        low_ref[:, cols] = y_ref[cols, :].T

    each_chunk(load)
    gram()
    scale = 1.0 / (jnp.sqrt(jnp.sum(gram_ref[...] * eye, keepdims=True)) + ortho_epsilon)
    gram_ref[...] = gram_ref[...] * (scale * scale)

    linear_only = coef_second * gram_ref[...]
    low_gram = gram_ref[...].astype(bf16)
    poly_ref[...] = (scale * (linear_only + coef_third * mm(low_gram, low_gram))).astype(bf16)

    def first(cols):
        matrix = low_ref[:, cols]
        fresh = (coef_first * scale) * matrix.astype(f32) + mm(poly_ref[...], matrix)
        full_ref[:, cols] = fresh
        low_ref[:, cols] = fresh.astype(bf16)

    each_chunk(first)
    gram()

    def polynomial(k):
        shift = jnp.float32(shifts[1])
        for number in range(2, NS_STEPS):
            shift = jnp.where(k == number, shifts[number], shift)
        linear = coef_second + 2.0 * coef_third * shift
        diff = gram_ref[...] - shift * eye
        low_diff = diff.astype(bf16)
        poly_ref[...] = (linear * diff + coef_third * mm(low_diff, low_diff)).astype(bf16)
        return coef_first + coef_second * shift + coef_third * shift * shift

    def sweep(k, carry):
        base = polynomial(k)

        def update(cols):
            fresh = base * full_ref[:, cols] + mm(poly_ref[...], low_ref[:, cols])
            full_ref[:, cols] = fresh
            low_ref[:, cols] = fresh.astype(bf16)

        each_chunk(update)
        gram()
        return carry

    lax.fori_loop(1, NS_STEPS - 1, sweep, 0)
    base = polynomial(NS_STEPS - 1)
    wanted = -(-4 * own_ff // tile) * tile
    fresh = base * full_ref[:, :wanted] + mm(poly_ref[...], low_ref[:, :wanted])
    gram_ref[:wanted, :] = fresh.T
    for kind, _, size in kinds:

        @pl.when(kind)
        def _():
            for k in range(4):
                piece = gram_ref[k * size : (k + 1) * size, :].astype(bf16)
                if size < own_ff:
                    piece = jnp.concatenate(
                        [piece, jnp.zeros((own_ff - size, side), bf16)], axis=0
                    )
                out_refs[k][...] = piece


def orthogonal(role, columns, sums, own):
    width = sums.shape[1]
    parts = [part.reshape(-1, width) for column in columns for part in column]
    length = sum(part.shape[0] for part in parts)
    return pl.pallas_call(
        functools.partial(ns_kernel, own, len(parts)),
        out_shape=[jax.ShapeDtypeStruct((own[1], width), bf16)] * 4,
        in_specs=[pl.BlockSpec(memory_space=pltpu.SMEM)]
        + [pl.BlockSpec(memory_space=pl.ANY)] * (len(parts) + 1),
        out_specs=[pl.BlockSpec(memory_space=pltpu.VMEM)] * 4,
        scratch_shapes=[
            pltpu.VMEM((length, width), bf16),
            pltpu.VMEM((width, length), f32),
            pltpu.VMEM((width, length), bf16),
            pltpu.VMEM((width, width), f32),
            pltpu.VMEM((width, width), bf16),
            pltpu.SemaphoreType.DMA((len(parts),)),
        ],
        compiler_params=pltpu.CompilerParams(vmem_limit_bytes=vmem_limit),
        cost_estimate=cost(46),
        name="newton_schulz",
    )(role, *parts, sums)


def column_place(mask):
    return ((mask >> 1) & 1) + 2 * (mask & 1)


def sum_heads_kernel(own_mix, old_at, role_ref, near_ref, *refs):
    parts, (acts_ref, y_out_ref), fresh_refs = refs[:8], refs[8:10], refs[10:14]
    held_ref, old_ref, y_ref, natural_ref, turned_ref, sems = refs[14:]
    width = held_ref.shape[3]
    own_in = fresh_refs[0].shape[0]
    hd = width // HEADS
    block = 16
    place = [column_place(near_ref[0] ^ n) for n in range(4)]

    def fetch(size, at, own):
        moves = [(acts_ref.at[:, at : at + own], old_ref.at[:, :own])]
        for c in range(4):
            moves.append((parts[2 * c].at[:size], held_ref.at[c, 0, :size]))
            moves.append((parts[2 * c + 1].at[:, :size], held_ref.at[c, 1:, :size]))
        copy_all(moves, sems)

    @pl.when(role_ref[0] == 0)
    def _():
        fetch(3 * hd, old_at, own_in)
        for z in range(4):
            for n in range(4):
                for start in range(0, own_in, block):
                    first = (4 * z + n) * own_in + start
                    part, rest = divmod(first, width)
                    h, off = divmod(rest, hd)
                    at = part * hd + off
                    source = held_ref[place[h & 3], h >> 2, at : at + block, :]
                    natural_ref[place[n], z, start : start + block, :] = source
                    old = old_ref[4 * z + n, start : start + block, :]
                    y_ref[pl.ds((place[n] * 4 + z) * own_in + start, block), :] = (
                        muon_moment * old.astype(f32) + source.astype(f32)
                    ).astype(bf16)
        for k in range(4):
            fresh_refs[k][...] = natural_ref[0, k]
        copy_all([(y_ref, y_out_ref)], sems)

    @pl.when(role_ref[0] == 3)
    def _():
        fetch(hd, old_at + own_in, own_mix)
        for h in range(HEADS):
            turned_ref[h * hd : (h + 1) * hd, :] = held_ref[
                place[h & 3], 3 ^ (h >> 2), :hd
            ].astype(f32)
        turned_ref[...] = turned_ref[...].T
        for z in range(4):
            for n in range(4):
                first = (4 * z + n) * own_mix
                source = turned_ref[first : first + own_mix, :]
                natural_ref[place[n], 3 ^ z, :own_mix] = source.astype(bf16)
                old = old_ref[4 * z + n, :own_mix]
                y_ref[pl.ds((place[n] * 4 + (3 ^ z)) * own_mix, own_mix), :] = (
                    muon_moment * old.astype(f32) + source
                ).astype(bf16)
        for k in range(4):
            fresh_refs[k][...] = jnp.zeros_like(fresh_refs[k])
            fresh_refs[k][:own_mix, :] = natural_ref[0, k, :own_mix]
        copy_all([(y_ref.at[:width], y_out_ref.at[:width])], sems)

    @pl.when((role_ref[0] == 1) | (role_ref[0] == 2))
    def _():
        for k in range(4):
            fresh_refs[k][...] = jnp.zeros_like(fresh_refs[k])


def sum_heads(role, near, columns, acts, old_at, own_in, own_mix):
    ctx, _, width = acts.shape
    parts = [part for column in columns for part in column]
    size = parts[0].shape[0]
    smem = pl.BlockSpec(memory_space=pltpu.SMEM)
    hbm = pl.BlockSpec(memory_space=pl.ANY)
    return pl.pallas_call(
        functools.partial(sum_heads_kernel, own_mix, old_at),
        out_shape=[
            jax.ShapeDtypeStruct((ctx * own_in, width), bf16),
        ]
        + [jax.ShapeDtypeStruct((own_in, width), bf16)] * 4,
        in_specs=[smem, smem] + [hbm] * 9,
        out_specs=[hbm] + [pl.BlockSpec(memory_space=pltpu.VMEM)] * 4,
        scratch_shapes=[
            pltpu.VMEM((4, 4, size, width), bf16),
            pltpu.VMEM((ctx, own_in, width), bf16),
            pltpu.VMEM((ctx * own_in, width), bf16),
            pltpu.VMEM((4, 4, own_in, width), bf16),
            pltpu.VMEM((width, width), f32),
            pltpu.SemaphoreType.DMA((9,)),
        ],
        compiler_params=pltpu.CompilerParams(vmem_limit_bytes=vmem_limit),
        cost_estimate=cost(4),
        name="sum_heads",
    )(role, near, *parts, acts)


def exchange(packed):
    return lax.all_to_all(packed, "ctx", split_axis=0, concat_axis=0, tiled=True)


def gather(array):
    return lax.all_gather(array, "ctx", axis=0, tiled=False)


def flip(array, mask, ctx):
    return lax.ppermute(array, "ctx", [(j, j ^ mask) for j in range(ctx)])


def spread_z(array, z_here, ctx):
    held = [array] + [flip(array, 4 * k, ctx) for k in (1, 2, 3)]
    odd, high = (z_here & 1) == 1, z_here >= 2
    first = [jnp.where(odd, held[k ^ 1], held[k]) for k in range(4)]
    return jnp.stack([jnp.where(high, first[k ^ 2], first[k]) for k in range(4)])


def gather_start(piece_for, z_here, ctx):
    own = piece_for(z_here)
    far = [flip(piece_for(z_here ^ k), 4 * k, ctx) for k in (1, 2, 3)]
    return own, far, [flip(own, mask, ctx) for mask in (2, 1)]


def gather_finish(started, ctx):
    own, far, own_sides = started
    far = jnp.stack(far)
    far_sides = [flip(far, mask, ctx) for mask in (2, 1)]
    across = tuple(flip(part, 1, ctx) for part in (own_sides[0], far_sides[0]))
    columns = [(own, far), (own_sides[0], far_sides[0]), (own_sides[1], far_sides[1]), across]
    for mask in [1 << n for n in range(4, ctx.bit_length() - 1)]:
        columns = columns + [tuple(flip(part, mask, ctx) for part in column) for column in columns]
    return columns


def column_at(mask):
    high = mask >> 4
    return ((mask >> 1) & 1) + 2 * (mask & 1) + 4 * high


def body(
    ctx,
    tokens,
    cotangent,
    block_order,
    input_weight,
    output_weight,
    expand_weight,
    reduce_weight,
    vectors,
    input_moment,
    output_moment,
    expand_moment,
    reduce_moment,
    vector_first,
    vector_second,
):
    seqs, local, width = tokens.shape
    rows = seqs * local
    length = ctx * local
    hd = width // HEADS
    layers = 2
    own_in = input_weight.shape[2]
    own_mix = output_weight.shape[2]
    own_ff = expand_weight.shape[2]
    own_vec = vectors.shape[1]
    dp_index = lax.axis_index("dp")
    ctx_index = lax.axis_index("ctx")
    owner_first = dp_index == 0

    ring_rows = 688

    def sections(parts):
        at, pieces, used = {}, [], 0
        for name, array in parts:
            size = array.shape[0]
            aligned = size % 16 == 0 and not name.startswith("old")
            start = -(-used // size) * size if aligned else used
            pieces.append(jnp.pad(array, ((start - used, 0), (0, 0))))
            at[name], used = start, start + size
        goal = -(-used // 16) * 16
        if ctx == 16 and goal > 512:
            goal = max(goal, ring_rows)
        pieces.append(jnp.zeros((goal - used, width), bf16))
        return jnp.concatenate(pieces, axis=0), at

    x_own = tokens.reshape(rows, width)
    cot = cotangent.reshape(rows, width)
    vec_row = jnp.pad(vectors.astype(bf16), ((0, 15), (0, width - own_vec)))
    pack = jnp.concatenate(
        [
            expand_weight[0].T.astype(bf16),
            reduce_weight[0].astype(bf16),
            output_weight[0].T.astype(bf16),
            input_weight[0].T.astype(bf16),
            vec_row,
        ],
        axis=0,
    )
    pack_other = lax.ppermute(pack, "dp", [(0, 1), (1, 0)])
    cuts = (own_ff, 2 * own_ff, 2 * own_ff + own_mix, 2 * own_ff + own_mix + own_in)
    own_parts = []
    for l in range(layers):
        mine = jnp.where(owner_first, (pack, pack_other)[l], (pack_other, pack)[l])
        own_parts.append(jnp.split(mine, cuts))
    pack_first, at_first = sections(
        [
            ("fc", own_parts[0][0]),
            ("red", own_parts[0][1]),
            ("tokens", x_own),
            ("vec", jnp.concatenate([own_parts[l][4][:8] for l in range(layers)], axis=0)),
            ("mix", own_parts[0][2]),
            ("in", own_parts[0][3]),
            ("next", own_parts[1][3]),
        ]
    )
    pack_second, at_second = sections(
        [
            ("fc", own_parts[1][0]),
            ("red", own_parts[1][1]),
            ("cot", cot),
            ("mix", own_parts[1][2]),
        ]
    )
    all_first, all_second = gather(pack_first), gather(pack_second)
    weights = (all_first, all_second)
    places = (at_first, at_second)
    in_at = (at_first["in"], at_first["next"])
    vecs = [
        all_first[:, at_first["vec"] + 8 * l, :own_vec].reshape(-1, width).astype(f32)
        for l in range(layers)
    ]

    block_len = length // block_order.shape[0]
    positions = (
        block_order[:, None] * block_len + jnp.arange(block_len, dtype=jnp.int32)[None, :]
    ).reshape(length)
    qpos = positions[:, None]
    kpos = positions[None, :]

    head = jnp.minimum(ctx_index, HEADS - 1)
    head_bias = jnp.concatenate(
        [
            lax.dynamic_slice_in_dim(vecs[0][2], head * hd, hd),
            jnp.zeros((hd,), f32),
            lax.dynamic_slice_in_dim(vecs[0][3], head * hd, hd),
        ]
    )
    stream = x_own
    saved = []
    for l in range(layers):
        if l == 0:
            a, qkv = head_qkv(
                head[None], all_first, at_first["tokens"], vecs[0], head_bias[None],
                all_first, at_first["in"], own_in, rows,
            )
        else:
            a, qkv_pack = qkv_forward(stream, vecs[l], all_first, in_at[l], own_in, local)
            qkv = exchange(qkv_pack).reshape(length, 6 * hd)
        out_full, out_low, prob = attn_forward(qkv, qpos, kpos)
        o_pack = exchange(out_low.reshape(ctx, local, 2 * hd))
        mid, c, hidden, fresh = mlp_forward(
            o_pack, stream, vecs[l], weights[l], places[l], own_ff, own_mix
        )
        saved.append((stream, a, qkv, out_full, out_low, prob, mid, c, hidden))
        stream = fresh
    block_output = stream.reshape(seqs, local, width)

    bias = [
        lax.dynamic_slice_in_dim(vecs[l][PIECES:].reshape(-1), ctx_index * own_ff, own_ff)[:, None]
        for l in range(layers)
    ]

    role = (ctx_index // 4) % 4

    grad = cot
    kept = [None, None]
    vec_grads = [None, None]
    for l in (1, 0):
        x, a, qkv, out_full, out_low, prob, mid, c, hidden = saved[l]
        gz, gmid, gy, go_pack, vg_late = mlp_backward(
            grad, mid, hidden, vecs[l], weights[l], places[l], own_ff, own_mix
        )
        if l == 1:
            pack_acts, at_acts = sections(
                [
                    ("c", saved[0][7]),
                    ("next_a", saved[1][1]),
                    ("next_c", saved[1][7]),
                    ("next_gy", gy),
                    ("old_in", input_moment[0].T.astype(bf16)),
                    ("old_mix", output_moment[0].T.astype(bf16)),
                ]
            )
            acts = gather(pack_acts)
        if l == 0:
            gz_held = spread_z(gz, role, ctx)
        go = exchange(go_pack).reshape(length, 2 * hd)
        dqkv = attn_backward(qkv, go, out_full, prob)
        if l == 0:
            dqkv, gz_held = lax.optimization_barrier((dqkv, gz_held))
            gz_held = gz_held.reshape(4 * rows, width)
            gz_sides = [flip(gz_held, mask, ctx) for mask in (2, 1)]
        dqkv_own = exchange(dqkv.reshape(ctx, local, 6 * hd))
        kept[l] = (gz, gy, dqkv)
        if l == 1:
            gin, vg_early = qkv_backward(dqkv_own, x, gmid, vecs[l], all_first, in_at[l], own_in)
            vec_grads[l] = jnp.concatenate([vg_early[:4], vg_late], axis=0)
            grad = gin

    gy_all = gather(kept[0][1])
    ready = hidden_ready(acts, at_acts["c"], own_parts[0][0], bias[0], rows)
    g_in_first = head_grads(kept[0][2], saved[0][1], 0, rows)
    old_hidden = jnp.concatenate([expand_moment[0].T, reduce_moment[0]], axis=0)
    ready, gz_sides, dqkv_own, g_in_first, old_hidden = lax.optimization_barrier(
        (ready, gz_sides, dqkv_own, g_in_first, old_hidden)
    )
    gz_masks = [0, 2, 1, 3]
    gz_columns = [gz_held, *gz_sides, flip(gz_sides[0], 1, ctx)]
    for mask in [1 << n for n in range(4, ctx.bit_length() - 1)]:
        gz_masks = gz_masks + [mask | other for other in gz_masks]
        gz_columns = gz_columns + [flip(column, mask, ctx) for column in gz_columns]
    g_head = [
        g_in_first,
        head_grads(kept[1][2], acts, at_acts["next_a"], rows),
        head_grads(saved[1][4], acts, at_acts["next_gy"], rows),
    ]
    gz_columns, g_head = lax.optimization_barrier((gz_columns, g_head))

    def owned(first, second, sent_as=bf16):
        given = jnp.where(owner_first, second, first).astype(sent_as)
        taken = lax.ppermute(given, "dp", [(0, 1), (1, 0)]).astype(f32)
        return jnp.where(owner_first, first, second) + taken

    g_in_head = owned(g_head[0], g_head[1]).astype(bf16)
    hidden_first = jnp.concatenate(
        hidden_last(
            acts, at_acts["c"], gz_columns, gz_masks, ctx_index, *ready, own_parts[0][1], rows
        ),
        axis=0,
    )
    hidden_first, acts, g_in_head = lax.optimization_barrier((hidden_first, acts, g_in_head))
    hidden_second = jnp.concatenate(
        hidden_grads(
            acts, at_acts["next_c"], all_second, at_second["cot"], *own_parts[1][:2], bias[1], rows
        ),
        axis=0,
    )
    gy_all, _ = lax.optimization_barrier((gy_all, hidden_second))
    moved = muon_moment * old_hidden + owned(hidden_first, hidden_second)
    moved, dqkv_own = lax.optimization_barrier((moved, dqkv_own))
    gin, vg_early = qkv_backward(dqkv_own, x, gmid, vecs[0], all_first, in_at[0], own_in)
    vec_grads[0] = jnp.concatenate([vg_early[:4], vg_late], axis=0)
    input_grad = gin.reshape(seqs, local, width)

    big = max(own_ff, 3 * hd)

    def padded(piece):
        return jnp.pad(piece.astype(bf16), ((0, big - piece.shape[0]), (0, 0)))

    g_mix_first = head_grads(saved[0][4], gy_all, 0, rows)
    g_mix_head = owned(g_mix_first, g_head[2])
    pieces = (g_in_head, padded(moved[:own_ff]), padded(moved[own_ff:]), padded(g_mix_head))

    def piece_for(z):
        low = jnp.where(z == 0, pieces[0], pieces[1])
        return jnp.where(z < 2, low, jnp.where(z == 2, pieces[2], pieces[3]))

    started, vec_grads = lax.optimization_barrier((gather_start(piece_for, role, ctx), vec_grads))
    vec_terms = owned(vec_grads[0], vec_grads[1], f32).reshape(ctx, 1, own_vec)
    vec_terms = jnp.pad(vec_terms, ((0, 0), (0, 7), (0, width - own_vec)))
    vec_sums = lax.psum_scatter(vec_terms, "ctx", scatter_dimension=0)
    columns = gather_finish(started, ctx)

    groups = ctx // 4
    near = ctx_index % 4
    masks = [m for m in range(ctx) if m & 12 == 0]
    order = sorted(masks, key=column_at)

    def absolute(array, size):
        mine = (ctx_index // 16) * 4 + near
        spots = jnp.array([column_at(((n >> 2) << 4) | (n & 3)) for n in range(groups)])
        listed = jnp.stack(
            [
                lax.dynamic_index_in_dim(array, spots[n ^ mine], 0, keepdims=False)[:, :size]
                for n in range(groups)
            ]
        )
        listed = listed.reshape(ctx // 16, 4, 4, size, width).swapaxes(1, 2)
        return listed.reshape(ctx, size, width)

    def relative(array):
        size = array.shape[1]
        split = array.reshape(ctx // 16, 4, 4, size, width).swapaxes(1, 2)
        split = split.reshape(groups, 4, size, width)
        mine = (ctx_index // 16) * 4 + near
        spread = jnp.stack(
            [
                lax.dynamic_index_in_dim(
                    split, mine ^ (((m >> 4) << 2) | (m & 3)), 0, keepdims=False
                )
                for m in order
            ]
        )
        return spread

    old_at = at_acts["old_in"]
    if ctx == 16 and own_in % 16 == 0 and own_mix % 16 == 0:
        sums, *fresh = sum_heads(role[None], near[None], columns, acts, old_at, own_in, own_mix)
    else:
        old = acts[:, old_at : old_at + own_in + own_mix].astype(f32)

        def joined(parts):
            return jnp.stack([jnp.concatenate([own[None], far]) for own, far in parts])

        new_in = absolute(joined(columns), 3 * hd)[:HEADS].reshape(HEADS, 3, hd, width)
        new_in = new_in.swapaxes(0, 1).reshape(ctx, own_in, width)
        sum_in = relative((muon_moment * old[:, :own_in] + new_in.astype(f32)).astype(bf16))
        new_mix = absolute(joined(columns)[:, ::-1], hd)[:HEADS].reshape(width, width)
        new_mix = new_mix.T.reshape(ctx, own_mix, width)
        sum_mix = relative((muon_moment * old[:, own_in:] + new_mix.astype(f32)).astype(bf16))
        sum_mix = jnp.pad(sum_mix[:, ::-1].reshape(width, width), ((0, 2 * width), (0, 0)))
        sums = jnp.where(role == 3, sum_mix, sum_in.reshape(3 * width, width))
        new_mix = jnp.pad(relative(new_mix)[0, ::-1], ((0, 0), (0, own_in - own_mix), (0, 0)))
        fresh = jnp.where(role == 3, new_mix, relative(new_in)[0])

    taken = [fresh[0]]
    for k in (1, 2, 3):
        pairs = [(j, j ^ (4 * k)) for j in range(ctx) if (j // 4) % 4 in (0, 3)]
        taken.append(lax.ppermute(fresh[k], "ctx", pairs))
    direction = orthogonal(
        role[None],
        [(own[:own_ff], far[:, :own_ff]) for own, far in columns],
        sums,
        (own_in, own_ff, own_mix),
    )
    direction, taken, moved = lax.optimization_barrier((direction, taken, moved))
    m_fc = moved[:own_ff].T
    m_red = moved[own_ff:]
    by_distance = [direction[0]] + [flip(direction[k], 4 * k, ctx) for k in (1, 2, 3)]
    by_distance[1], vec_sums = lax.optimization_barrier((by_distance[1], vec_sums))
    vec_grad = vec_sums[:1, :own_vec]

    def from_role(by_distance, wanted):
        result = by_distance[wanted]
        for k in range(4):
            if k != wanted:
                result = jnp.where(role == wanted ^ k, by_distance[k], result)
        return result

    m_in = muon_moment * input_moment[0] + from_role(taken, 0).astype(f32).T
    m_mix = muon_moment * output_moment[0] + from_role(taken, 3)[:own_mix].astype(f32).T

    got = [from_role(by_distance, wanted) for wanted in range(4)]
    steps = (
        got[0][:own_in].astype(f32).T,
        got[3][:own_mix].astype(f32).T,
        got[1].astype(f32).T,
        got[2].astype(f32),
    )
    hidden_units = ctx * own_ff
    largest = (3 * width, width, hidden_units, hidden_units)
    old_weights = (input_weight, output_weight, expand_weight, reduce_weight)
    new_weights = [
        old_weights[kind] * (1.0 - muon_rate * muon_decay)
        - muon_rate * 0.2 * math.sqrt(largest[kind]) * steps[kind][None]
        for kind in range(4)
    ]

    new_vector_first = beta_first * vector_first + (1.0 - beta_first) * vec_grad
    new_vector_second = beta_second * vector_second + (1.0 - beta_second) * vec_grad * vec_grad
    corr_first = 1.0 - beta_first**STEP
    corr_second = 1.0 - beta_second**STEP
    new_vectors = vectors - adam_rate * (new_vector_first / corr_first) / (
        jnp.sqrt(new_vector_second / corr_second) + adam_epsilon
    )
    return (
        block_output,
        input_grad,
        new_weights[0],
        new_weights[1],
        new_weights[2],
        new_weights[3],
        m_in[None],
        m_mix[None],
        m_fc[None],
        m_red[None],
        new_vectors,
        new_vector_first,
        new_vector_second,
    )


def solution(mesh):
    return jax.shard_map(
        functools.partial(body, mesh.shape["ctx"]),
        mesh=mesh,
        in_specs=(
            P("dp", "ctx", None),
            P("dp", "ctx", None),
            P(),
            P("dp", None, "ctx"),
            P("dp", None, "ctx"),
            P("dp", None, "ctx"),
            P("dp", "ctx", None),
            P("dp", "ctx"),
            P("dp", None, "ctx"),
            P("dp", None, "ctx"),
            P("dp", None, "ctx"),
            P("dp", "ctx", None),
            P("dp", "ctx"),
            P("dp", "ctx"),
        ),
        out_specs=(
            P("dp", "ctx", None),
            P("dp", "ctx", None),
            P("dp", None, "ctx"),
            P("dp", None, "ctx"),
            P("dp", None, "ctx"),
            P("dp", "ctx", None),
            P("dp", None, "ctx"),
            P("dp", None, "ctx"),
            P("dp", None, "ctx"),
            P("dp", "ctx", None),
            P("dp", "ctx"),
            P("dp", "ctx"),
            P("dp", "ctx"),
        ),
        check_vma=False,
    )
```
